512 devices in a mesh: space: 128 (over y, z, core), pipe: 4 (over x).
Axes of the slice: x: 4, y: 4, z: 16, core: 2. Of those that a mesh axis runs over, the one named last changes fastest.
Arguments:
- section_input: bfloat16 [4, 128, 96, 512], P('pipe', 'space'), may hold values from -6 to 6
- top_grad: bfloat16 [128, 96, 512], P('space'), may hold values from -6 to 6
- conv_weight: bfloat16 [4, 27, 96, 96], P('pipe'), may hold values from -0.125 to 0.125
- brick_height: int32 [128], P('space'), may hold values from 0 to 4, as said below
Outputs:
- section_grads: bfloat16 [4, 128, 96, 512], P('pipe', 'space')
- weight_grad: float32 [4, 27, 96, 96], P('pipe')
The draws below stay inside these ranges and needn't reach their ends.
Inputs may be any that keep to these rules, and one draw needn't show every extreme that they name: `brick_height`: columns next to each other along the first or along the second dimension differ in level by at most one; the lowest level is 0 and the highest is 4.
All inputs are finite; a program needn't handle non-finite values.
Results may differ from the reference program's by a relative error of at most 0.007.
Values may be sent and summed in bfloat16 or wider, within the bound.
No kernel may reach another device: no remote copies, remote signals or barrier semaphores. Data moves between devices by JAX's collectives and lax.ppermute only.
A program may use at most 64 MiB of HBM per device.

```python
import jax
import jax.numpy as jnp

C = 96
BE = 8
KERNEL = 27
GRID_W = 8
FX = 1
FY = 1
SECTIONS = 4
ROWS = 16
NXC = 16
NYC = 8
BRICKS = 128
CELLS = 512


def draw_brick_height(key, part):
    first_key, second_key = jax.random.split(jax.random.fold_in(key, 11))
    steps_x = jax.random.randint(first_key, (NXC,), -1, 2)
    steps_y = jax.random.randint(second_key, (NYC,), -1, 2)
    steps_y = steps_y.at[1:5].set(1)
    grid = jnp.cumsum(steps_x)[:, None] + jnp.cumsum(steps_y)[None, :]
    grid = grid - jnp.min(grid)
    grid = jnp.minimum(grid, 4)
    ordered = grid.reshape(ROWS, FX, GRID_W, FY).transpose(0, 2, 1, 3)
    return ordered.reshape(-1).astype(jnp.int32)


def block_levels(rng, dims, cuts, least, top_value):
    def one(position, blocks):
        heights = jax.random.uniform(jax.random.fold_in(jax.random.fold_in(rng, 6), position), (blocks,), jnp.float32, least / len(cuts), top_value / len(cuts))
        return jnp.repeat(jnp.exp(heights), dims[position] // blocks).reshape((-1,) + (1,) * (len(dims) - position - 1))

    loudness = one(*cuts[0])
    for cut in cuts[1:]:
        loudness = loudness * one(*cut)
    return loudness


def bell_draw(key, shape, scale, limit, cuts=(), kind=jnp.bfloat16):
    values = jax.random.normal(key, shape, jnp.float32) * scale
    if len(cuts) > 0:
        values = block_levels(key, shape, cuts, -0.22, 0.18) * values
    return jnp.clip(values, min=-limit, max=limit).astype(kind)


def setup_inputs(seed: int = 0) -> dict:
    arg_keys = jax.random.split(jax.random.key(seed), 5)
    return {
        "section_input": bell_draw(arg_keys[0], (SECTIONS, BRICKS, C, CELLS), 1.0, 6.0, ((0, 4), (1, 128))),
        "top_grad": bell_draw(arg_keys[1], (BRICKS, C, CELLS), 1.0, 6.0, ((0, 128),)),
        "conv_weight": bell_draw(arg_keys[2], (SECTIONS, KERNEL, C, C), (KERNEL * C) ** -0.5, 0.125, ((0, 4),)),
        "brick_height": draw_brick_height(jax.random.fold_in(arg_keys[4], 71), 0),
    }


def take_layer(block, axis, side):
    start = BE - 1 if side > 0 else 0
    return jax.lax.slice_in_dim(block, start, start + 1, axis=axis)

def pad_bricks(ext, levels, inside):
    nx, ny = (ext.shape[0] - 2, ext.shape[1] - 2)
    base = levels[1:nx + 1, 1:ny + 1]
    planes = []
    for dx in (-1, 0, 1):
        lines = []
        for dy in (-1, 0, 1):
            near = ext[1 + dx:1 + dx + nx, 1 + dy:1 + dy + ny]
            rise = levels[1 + dx:1 + dx + nx, 1 + dy:1 + dy + ny] - base
            valid = inside[1 + dx:1 + dx + nx, 1 + dy:1 + dy + ny]
            if dx != 0:
                near = take_layer(near, 3, -dx)
            if dy != 0:
                near = take_layer(near, 4, -dy)
            stacks = []
            for dz in (-1, 0, 1):
                keep = (valid & (rise == dz)).astype(near.dtype)[:, :, None, None, None, None]
                piece = near if dz == 0 else take_layer(near, 5, -dz)
                stacks.append(piece * keep)
            lines.append(jnp.concatenate(stacks, 5))
        planes.append(jnp.concatenate(lines, 4))
    whole = jnp.concatenate(planes, 3)
    return whole.reshape((nx * ny,) + whole.shape[2:])

def gather_cols(padded, group, sign):
    count, channels = (padded.shape[0], padded.shape[1])
    offset_x = group - 1
    pieces = []
    for offset_y in (-1, 0, 1):
        for offset_z in (-1, 0, 1):
            start_x = 1 + sign * offset_x
            start_y = 1 + sign * offset_y
            start_z = 1 + sign * offset_z
            piece = padded[:, :, start_x:start_x + BE, start_y:start_y + BE, start_z:start_z + BE]
            pieces.append(piece.reshape(count, channels, BE ** 3))
    return jnp.concatenate(pieces, 1)

def apply_conv(padded, weight, sign):
    total = None
    for group in range(3):
        cols = gather_cols(padded, group, sign)
        block = weight[9 * group:9 * group + 9].reshape(-1, weight.shape[2])
        part = jnp.einsum('bkp,kd->bdp', cols, block)
        total = part if total is None else total + part
    return total

def weight_terms(padded, grad_pre):
    blocks = []
    for group in range(3):
        cols = gather_cols(padded, group, 1)
        blocks.append(jnp.einsum('bkp,bdp->kd', cols, grad_pre))
    channels = grad_pre.shape[1]
    return jnp.concatenate(blocks, 0).reshape(27, channels, channels)

def to_grid(values):
    rest = values.shape[1:]
    grid = values.reshape((ROWS, GRID_W, FX, FY) + rest)
    order = (0, 2, 1, 3) + tuple(range(4, grid.ndim))
    return grid.transpose(order).reshape((NXC, NYC) + rest)

def from_grid(values):
    rest = values.shape[2:]
    grid = values.reshape((ROWS, FX, GRID_W, FY) + rest)
    order = (0, 2, 1, 3) + tuple(range(4, grid.ndim))
    return grid.transpose(order).reshape((BRICKS,) + rest)

def reference(section_input, top_grad, conv_weight, brick_height):
    sections = section_input.shape[0]
    levels = jnp.pad(to_grid(brick_height), 1)
    inside = jnp.pad(jnp.ones((NXC, NYC), dtype=bool), 1)
    shape = (NXC, NYC, C, BE, BE, BE)
    widths = ((1, 1), (1, 1), (0, 0), (0, 0), (0, 0), (0, 0))
    incoming = to_grid(top_grad).reshape(NXC * NYC, C, CELLS)
    grads = []
    wgrads = []
    for section in range(sections - 1, -1, -1):
        source = to_grid(section_input[section]).reshape(shape)
        padded_x = pad_bricks(jnp.pad(source, widths), levels, inside).astype(jnp.float32)
        weight = conv_weight[section].astype(jnp.float32)
        pre = apply_conv(padded_x, weight, 1)
        sigma = jax.nn.sigmoid(pre)
        slope = sigma * (1.0 + pre * (1.0 - sigma))
        grad_pre = (incoming.astype(jnp.float32) * slope).astype(jnp.bfloat16)
        padded_g = pad_bricks(jnp.pad(grad_pre.reshape(shape), widths), levels, inside).astype(jnp.float32)
        result = (incoming.astype(jnp.float32) + apply_conv(padded_g, jnp.swapaxes(weight, 1, 2), -1)).astype(jnp.bfloat16)
        terms = weight_terms(padded_x, grad_pre.astype(jnp.float32))
        wgrad = terms / jnp.sqrt(jnp.mean(terms * terms) + 1e-06)
        grads.insert(0, from_grid(result.reshape(NXC, NYC, C, CELLS)))
        wgrads.insert(0, wgrad)
        incoming = result
    return (jnp.stack(grads), jnp.stack(wgrads))
```

```python
import functools

import jax
import jax.numpy as jnp
from jax import lax
from jax.experimental import pallas as pl
from jax.experimental.pallas import tpu as pltpu
from jax.sharding import PartitionSpec as P

C = 96
CELLS = 512
COLS = 8
ROWS = 16
SECTIONS = 4
TAPS = 27
DEEP = TAPS * C
WIDE = 128
CODE = 8
CHUNK = 336
VMEM_BYTES = 56 * 1024 * 1024
F32 = jnp.float32
BF16 = jnp.bfloat16


def call(kernel, outs, scratch=()):
    return pl.pallas_call(
        kernel,
        out_shape=[jax.ShapeDtypeStruct(shape, dtype) for shape, dtype in outs],
        scratch_shapes=[pltpu.VMEM(shape, dtype) for shape, dtype in scratch],
        compiler_params=pltpu.CompilerParams(vmem_limit_bytes=VMEM_BYTES),
    )


def lane(row, count=1):
    start = row * WIDE
    if not isinstance(start, int):
        start = pl.multiple_of(start, WIDE)
    return pl.ds(start, count * WIDE)


def turn(value, by):
    by = by % value.shape[1]
    return pltpu.roll(value, by, 1) if by else value


def shifted_rows(base_ref, row, tile):
    level = lax.broadcasted_iota(jnp.int32, (C, WIDE), 1) % 8
    for oy in (-1, 0, 1):
        for oz in (-1, 0, 1):
            if oz == 0:
                moved = turn(tile, -8 * oy)
            elif oz > 0:
                moved = jnp.where(level < 7, turn(tile, -8 * oy - 1), turn(tile, -8 * oy + 7))
            else:
                moved = jnp.where(level > 0, turn(tile, -8 * oy + 1), turn(tile, -8 * oy - 7))
            base_ref[3 * (oy + 1) + oz + 1, :, lane(row)] = moved


def make_cols(cols_ref, base_ref, mask_ref, base_row, mask_row, at=0):
    for ox in (-1, 0, 1):
        for j in range(9):
            tap = 9 * (ox + 1) + j
            tile = base_ref[j, :, lane(base_row + ox, 2)].reshape(C // 16, 16, 2 * WIDE)
            kept = tile * mask_ref[tap, :, lane(mask_row, 2)][None]
            cols_ref[C * tap : C * tap + C, lane(at, 2)] = kept.reshape(C, 2 * WIDE)


def product(weight, cols):
    return lax.dot_general(
        weight, cols, (((1,), (0,)), ((), ())), preferred_element_type=F32
    )


def weight_kernel(w_ref, fwd_ref, bwd_ref):
    for q in range(TAPS):
        fwd_ref[:, C * q : C * q + C] = w_ref[q].T
        bwd_ref[:, C * q : C * q + C] = w_ref[TAPS - 1 - q]


def pack_kernel(own_ref, left_ref, right_ref, own_out, up_out, down_out):
    rows = []
    for i in range(8):
        at = 64 * i
        rows.append(
            jnp.concatenate(
                [
                    left_ref[:, at + 32 : at + 64],
                    own_ref[:, at : at + 64],
                    right_ref[:, at : at + 32],
                ],
                1,
            )
        )
        own_out[:, lane(i)] = rows[i]
    codes = jnp.concatenate([rows[0][2 * C :]] * (C // 16), 0)
    for out, first in ((up_out, 3), (down_out, 0)):
        for n in range(5):
            out[:, lane(n)] = rows[first + n][:C]
        for n in range(4):
            row = first + n + (1 if first else 0)
            out[:, lane(5 + n)] = rows[row][C : 2 * C]
        out[:, lane(9)] = codes


def first_kernel(
    own_ref, before_ref, after_ref, fwd_ref, bwd_ref, active_ref,
    result_ref, slope_ref, mask_ref, x_ref, grad_ref, out_ref,
    base_ref, cols_ref, code_ref, top_ref, pre_ref,
):
    active = active_ref[0:1, 0:1]
    own_code = own_ref[2 * C : 2 * C + 8, :WIDE].astype(F32)
    before_code = before_ref[0:8, lane(9)].astype(F32)
    after_code = after_ref[0:8, lane(9)].astype(F32)
    for row in range(18):
        code = before_code if row < 5 else own_code if row < 13 else after_code
        code_ref[:, lane(row)] = code
    for row in range(18):
        if row < 5:
            tile = before_ref[:, lane(row)]
        elif row < 13:
            tile = own_ref[:C, lane(row - 5)]
        else:
            tile = after_ref[:, lane(row - 13)]
        if 4 <= row < 14:
            x_ref[:, lane(row - 4)] = tile
        shifted_rows(base_ref, row, tile)
    for row in range(1, 17):
        if row < 5:
            tile = before_ref[:, lane(4 + row)]
        elif row < 13:
            tile = own_ref[C : 2 * C, lane(row - 5)]
        else:
            tile = after_ref[:, lane(5 + row - 13)]
        top_ref[:, lane(row - 1)] = tile.astype(F32) * active

    level = lax.broadcasted_iota(jnp.int32, (8, WIDE), 1) % 8
    rise_of = {
        -1: jnp.where(level == 0, -1.0, 0.0),
        0: jnp.zeros((8, WIDE), F32),
        1: jnp.where(level == 7, 1.0, 0.0),
    }

    def masks(row, carry):
        here = code_ref[:, lane(row + 1)]
        for ox in (-1, 0, 1):
            near = code_ref[:, lane(row + 1 + ox)]
            for oy in (-1, 0, 1):
                rise = turn(near, -8 * oy) - here
                for oz in (-1, 0, 1):
                    keep = jnp.where(rise == rise_of[oz], 1.0, 0.0)
                    tap = 9 * (ox + 1) + 3 * (oy + 1) + oz + 1
                    mask_ref[tap, :, lane(row)] = jnp.concatenate([keep, keep], 0).astype(BF16)
        return carry

    lax.fori_loop(0, 16, masks, 0)

    def forward(pair, carry):
        make_cols(cols_ref, base_ref, mask_ref, 2 * pair + 1, 2 * pair)
        pre_ref[:, lane(2 * pair, 2)] = product(fwd_ref[...], cols_ref[...])
        return carry

    lax.fori_loop(0, 8, forward, 0)
    for row in range(16):
        pre = pre_ref[:, lane(row)]
        sigma = 1.0 / (1.0 + jnp.exp(-pre))
        slope = sigma * (1.0 + pre * (1.0 - sigma))
        grad = (top_ref[:, lane(row)] * slope).astype(BF16)
        if 1 <= row < 15:
            slope_ref[:, lane(row - 1)] = slope
        if 4 <= row < 12:
            grad_ref[:, lane(row - 4)] = grad
        shifted_rows(base_ref, row, grad)

    def backward(pair, carry):
        make_cols(cols_ref, base_ref, mask_ref, 2 * pair + 1, 2 * pair + 1)
        total = top_ref[:, lane(2 * pair + 1, 2)] + product(bwd_ref[...], cols_ref[...])
        result_ref[:, lane(2 * pair, 2)] = total.astype(BF16)
        return carry

    lax.fori_loop(0, 7, backward, 0)
    for row in range(8):
        out_ref[:, lane(row)] = result_ref[:, lane(row + 3)]


def step_rows(incoming_ref, slope_ref, mask_ref, bwd_ref, base_ref, cols_ref, store, count, first):
    for row in range(count):
        grad = (
            incoming_ref[:, lane(row)].astype(F32) * slope_ref[:, lane(row + first - 2)]
        ).astype(BF16)
        shifted_rows(base_ref, row, grad)

    def backward(pair, carry):
        make_cols(cols_ref, base_ref, mask_ref, 2 * pair + 1, 2 * pair + first)
        total = incoming_ref[:, lane(2 * pair + 1, 2)].astype(F32) + product(
            bwd_ref[...], cols_ref[...]
        )
        store(pair, total.astype(BF16))
        return carry

    lax.fori_loop(0, (count - 2) // 2, backward, 0)


def middle_kernel(
    count, first, incoming_ref, slope_ref, mask_ref, bwd_ref, grad_in, out_in,
    result_ref, grad_ref, out_ref, base_ref, cols_ref,
):
    def store(pair, value):
        result_ref[:, lane(2 * pair, 2)] = value

    step_rows(
        incoming_ref, slope_ref, mask_ref, bwd_ref, base_ref, cols_ref, store, count, first
    )
    for row in range(8):
        grad_ref[:, lane(row)] = grad_in[:, lane(row)] + base_ref[4, :, lane(row + 5 - first)]
        out_ref[:, lane(row)] = out_in[:, lane(row)] + result_ref[:, lane(row + 4 - first)]


def late_kernel(
    count, first, incoming_ref, slope_ref, mask_ref, bwd_ref, grad_in, out_in,
    centre_ref, left_ref, right_ref, grad_ref, out_ref, base_ref, cols_ref, result_ref,
):
    middle_kernel(
        count, first, incoming_ref, slope_ref, mask_ref, bwd_ref, grad_in, out_in,
        result_ref, grad_ref, out_ref, base_ref, cols_ref,
    )
    rows = [result_ref[:, lane(row)] for row in range(count - 2)]
    for row in range(0, count - 2, 2):
        centre_ref[:, lane(row // 2)] = jnp.concatenate(
            [rows[row][:, 32:96], rows[row + 1][:, 32:96]], 1
        )
    spare = jnp.zeros((C, WIDE - 8 * (count - 2)), BF16)
    left_ref[...] = jnp.concatenate([row[:, 32:40] for row in rows] + [spare], 1)
    right_ref[...] = jnp.concatenate([row[:, 88:96] for row in rows] + [spare], 1)


def last_kernel(
    centre_ref, from_left, from_right, slope_ref, mask_ref, bwd_ref, x_ref, grad_in, out_in,
    out_ref, terms_ref, base_ref, cols_ref, incoming_ref, sums_ref, all_ref,
):
    pad = jnp.zeros((C, 24), BF16)
    for row in range(10):
        at = 64 * row
        incoming_ref[:, lane(row)] = jnp.concatenate(
            [
                pad,
                from_left[:, 8 * row : 8 * row + 8],
                centre_ref[:, at : at + 64],
                from_right[:, 8 * row : 8 * row + 8],
                pad,
            ],
            1,
        )

    def store(pair, value):
        sums_ref[:, lane(2 * pair, 2)] = out_in[:, lane(2 * pair, 2)] + value

    step_rows(incoming_ref, slope_ref, mask_ref, bwd_ref, base_ref, cols_ref, store, 10, 4)
    for pair in range(4):
        first, second = sums_ref[:, lane(2 * pair)], sums_ref[:, lane(2 * pair + 1)]
        out_ref[:, lane(pair)] = jnp.concatenate([first[:, 32:96], second[:, 32:96]], 1)

    where = lax.broadcasted_iota(jnp.int32, (C, WIDE), 1)
    inside = (where >= 32) & (where < 96)
    grads = []
    for row in range(8):
        grad = grad_in[:, lane(row)] + base_ref[4, :, lane(row + 1)]
        grads.append(jnp.where(inside, grad, jnp.zeros_like(grad)))
    grads = jnp.concatenate(grads, 1)
    for row in range(10):
        shifted_rows(base_ref, row, x_ref[:, lane(row)])

    def gather(pair, carry):
        make_cols(all_ref, base_ref, mask_ref, 2 * pair + 1, 2 * pair + 4, 2 * pair)
        return carry

    lax.fori_loop(0, 4, gather, 0)
    for tap in range(TAPS):
        part = lax.dot_general(
            all_ref[C * tap : C * tap + C, :], grads, (((1,), (1,)), ((), ())),
            preferred_element_type=F32,
        )
        terms_ref[C * tap : C * tap + C, :] = part.astype(BF16)
    terms_ref[DEEP:, :] = jnp.zeros((COLS * CHUNK - DEEP, C), BF16)


def groups(devices):
    rows = devices // (2 * ROWS)
    near = [[y * 32 + z * 2 + c for y in range(rows) for c in range(2)] for z in range(ROWS)]
    far = [[y * 32 + z * 2 + c for z in range(ROWS)] for y in range(rows) for c in range(2)]
    return near, far


def body(section_input, top_grad, conv_weight, brick_height):
    devices = lax.axis_size("space")
    section = lax.axis_index("pipe")
    both = ("space", "pipe")

    def between(by_row, by_col, sections):
        pairs = []
        for x in range(ROWS):
            for y in range(COLS):
                if 0 <= x + by_row < ROWS and 0 <= y + by_col < COLS:
                    source = x * COLS + y
                    target = (x + by_row) * COLS + y + by_col
                    for a, b in sections:
                        pairs.append((source * SECTIONS + a, target * SECTIONS + b))
        return pairs

    same = [(s, s) for s in range(SECTIONS)]
    code = jnp.broadcast_to((brick_height + CODE).astype(BF16)[:, None], (16, CELLS))
    own = jnp.concatenate([section_input.reshape(C, CELLS), top_grad.reshape(C, CELLS), code], 0)
    fwd, bwd = call(weight_kernel, [((C, DEEP), BF16)] * 2)(conv_weight[0])
    left = lax.ppermute(own, both, between(0, 1, same))
    right = lax.ppermute(own, both, between(0, -1, same))
    own, up, down = call(
        pack_kernel,
        [((2 * C + 16, 8 * WIDE), BF16), ((C, 10 * WIDE), BF16), ((C, 10 * WIDE), BF16)],
    )(own, left, right)
    before = lax.ppermute(up, both, between(1, 0, same))
    after = lax.ppermute(down, both, between(-1, 0, same))
    active = jnp.where(section == SECTIONS - 1, 1.0, 0.0) * jnp.ones((8, WIDE), F32)

    core = ((C, 8 * WIDE), BF16)
    cols = ((DEEP, 2 * WIDE), BF16)
    result, slope, mask, x_rows, grad, out = call(
        first_kernel,
        [((C, 14 * WIDE), BF16), ((C, 14 * WIDE), F32), ((TAPS, 16, 16 * WIDE), BF16),
         ((C, 10 * WIDE), BF16), core, core],
        [((9, C, 18 * WIDE), BF16), cols, ((8, 18 * WIDE), F32), ((C, 16 * WIDE), F32),
         ((C, 16 * WIDE), F32)],
    )(own, before, after, fwd, bwd, active)
    incoming = lax.ppermute(result, both, between(0, 0, [(3, 2)]))
    result, grad, out = call(
        functools.partial(middle_kernel, 14, 2),
        [((C, 12 * WIDE), BF16), core, core],
        [((9, C, 14 * WIDE), BF16), cols],
    )(incoming, slope, mask, bwd, grad, out)
    incoming = lax.ppermute(result, both, between(0, 0, [(2, 1)]))
    centre, left, right, grad, out = call(
        functools.partial(late_kernel, 12, 3),
        [((C, 5 * WIDE), BF16), ((C, WIDE), BF16), ((C, WIDE), BF16), core, core],
        [((9, C, 12 * WIDE), BF16), cols, ((C, 10 * WIDE), BF16)],
    )(incoming, slope, mask, bwd, grad, out)
    centre = lax.ppermute(centre, both, between(0, 0, [(1, 0)]))
    from_left = lax.ppermute(right, both, between(0, 1, [(1, 0)]))
    from_right = lax.ppermute(left, both, between(0, -1, [(1, 0)]))
    out, terms = call(
        last_kernel,
        [((C, CELLS), BF16), ((COLS * CHUNK, C), BF16)],
        [((9, C, 10 * WIDE), BF16), cols, ((C, 10 * WIDE), BF16), core, ((DEEP, 8 * WIDE), BF16)],
    )(centre, from_left, from_right, slope, mask, bwd, x_rows, grad, out)

    near, far = groups(devices)
    parts = lax.all_to_all(
        terms.reshape(COLS, CHUNK, C), "space", 0, 0, axis_index_groups=near
    )
    part = jnp.sum(parts.astype(F32), 0)
    pieces = lax.all_to_all(
        part.reshape(ROWS, CHUNK // ROWS, C), "space", 0, 0, axis_index_groups=far
    )
    piece = jnp.sum(pieces, 0)
    part = lax.all_gather(piece, "space", axis_index_groups=far).reshape(CHUNK, C)
    whole = lax.all_gather(part.astype(BF16), "space", axis_index_groups=near)
    total = whole.reshape(COLS * CHUNK, C)[:DEEP].astype(F32)
    scale = lax.rsqrt(jnp.sum(total * total) / (DEEP * C) + 1e-06)
    return (out.reshape(1, 1, C, CELLS), (total * scale).reshape(1, TAPS, C, C))


def solution(mesh):
    return jax.shard_map(
        body,
        mesh=mesh,
        in_specs=(
            P("pipe", "space", None, None),
            P("space", None, None),
            P("pipe", None, None, None),
            P("space"),
        ),
        out_specs=(P("pipe", "space", None, None), P("pipe", None, None, None)),
        check_vma=False,
    )
```

```python
import functools

import jax
import jax.numpy as jnp
from jax import lax
from jax.experimental import pallas as pl
from jax.experimental.pallas import tpu as pltpu
from jax.sharding import PartitionSpec as P

C = 96
CELLS = 512
COLS = 8
ROWS = 16
SECTIONS = 4
TAPS = 27
DEEP = TAPS * C
WIDE = 128
CODE = 8
CHUNK = 384
VMEM_BYTES = 56 * 1024 * 1024
F32 = jnp.float32
BF16 = jnp.bfloat16


def call(kernel, outs, scratch=()):
    return pl.pallas_call(
        kernel,
        out_shape=[jax.ShapeDtypeStruct(shape, dtype) for shape, dtype in outs],
        scratch_shapes=[pltpu.VMEM(shape, dtype) for shape, dtype in scratch],
        compiler_params=pltpu.CompilerParams(vmem_limit_bytes=VMEM_BYTES),
    )


def lane(row, count=1):
    start = row * WIDE
    if not isinstance(start, int):
        start = pl.multiple_of(start, WIDE)
    return pl.ds(start, count * WIDE)


def turn(value, by):
    by = by % value.shape[1]
    return pltpu.roll(value, by, 1) if by else value


def shifted_rows(base_ref, row, tile):
    level = lax.broadcasted_iota(jnp.int32, (C, WIDE), 1) % 8
    for oy in (-1, 0, 1):
        for oz in (-1, 0, 1):
            if oz == 0:
                moved = turn(tile, -8 * oy)
            elif oz > 0:
                moved = jnp.where(level < 7, turn(tile, -8 * oy - 1), turn(tile, -8 * oy + 7))
            else:
                moved = jnp.where(level > 0, turn(tile, -8 * oy + 1), turn(tile, -8 * oy - 7))
            base_ref[3 * (oy + 1) + oz + 1, :, lane(row)] = moved


def make_cols(cols_ref, base_ref, mask_ref, base_row, mask_row, at=0):
    for ox in (-1, 0, 1):
        for j in range(9):
            tap = 9 * (ox + 1) + j
            tile = base_ref[j, :, lane(base_row + ox, 2)].reshape(C // 16, 16, 2 * WIDE)
            kept = tile * mask_ref[tap, :, lane(mask_row, 2)][None]
            cols_ref[C * tap : C * tap + C, lane(at, 2)] = kept.reshape(C, 2 * WIDE)


def product(weight, cols):
    return lax.dot_general(
        weight, cols, (((1,), (0,)), ((), ())), preferred_element_type=F32
    )


def weight_kernel(w_ref, fwd_ref, bwd_ref):
    for q in range(TAPS):
        fwd_ref[:, C * q : C * q + C] = w_ref[q].T
        bwd_ref[:, C * q : C * q + C] = w_ref[TAPS - 1 - q]


def pack_kernel(own_ref, left_ref, right_ref, own_out, up_out, down_out):
    lowest = lax.axis_index("pipe") == 0
    rows = []
    for i in range(8):
        at = 64 * i
        rows.append(
            jnp.concatenate(
                [
                    left_ref[:, at + 32 : at + 64],
                    own_ref[:, at : at + 64],
                    right_ref[:, at : at + 32],
                ],
                1,
            )
        )
        own_out[:, lane(i)] = rows[i]
    code = jnp.concatenate([rows[0][2 * C :]] * (C // 16), 0)
    own_code = jnp.concatenate([own_ref[2 * C :, :WIDE]] * (C // 16), 0)
    where = lax.broadcasted_iota(jnp.int32, (C, WIDE), 1)
    for out, order, tops in (
        (up_out, (3, 4, 5, None, 6, 7), (4, 5, 6, 7)),
        (down_out, (2, 3, 4, None, 0, 1), (0, 1, 2, 3)),
    ):

        @pl.when(jnp.logical_not(lowest))
        def _(out=out, order=order):
            for slot, row in enumerate(order):
                out[:, lane(slot)] = code if row is None else rows[row][:C]

        @pl.when(lowest)
        def _(out=out, order=order, tops=tops):
            tiles = [rows[row][C : 2 * C] for row in tops]
            out[:, lane(0)] = jnp.where((where < 8) | (where >= 120), code, tiles[0])
            out[:, lane(1)] = jnp.where(where < 8, own_code, tiles[1])
            out[:, lane(2)] = tiles[2]
            out[:, lane(3)] = tiles[3]
            out[:, lane(4)] = rows[order[4]][:C]
            out[:, lane(5)] = rows[order[5]][:C]


def side_code(side_ref):
    where = lax.broadcasted_iota(jnp.int32, (8, WIDE), 1)
    first, second = side_ref[0:8, lane(0)].astype(F32), side_ref[0:8, lane(1)].astype(F32)
    parts = jnp.where(
        where < 32, first[:, 0:1], jnp.where(where < 96, second[:, 0:1], first[:, 127:128])
    )
    return jnp.where(lax.axis_index("pipe") == 0, parts, side_ref[0:8, lane(3)].astype(F32))


def forward_kernel(
    own_ref, before_ref, after_ref, fwd_ref,
    slope_ref, mask_ref, x_ref,
    base_ref, cols_ref, code_ref, pre_ref,
):
    own_code = own_ref[2 * C : 2 * C + 8, :WIDE].astype(F32)
    before_code = side_code(before_ref)
    after_code = side_code(after_ref)
    for row in range(18):
        code = before_code if row < 5 else own_code if row < 13 else after_code
        code_ref[:, lane(row)] = code
    for row in range(18):
        if row < 5:
            tile = before_ref[:, lane((0, 1, 2, 4, 5)[row])]
        elif row < 13:
            tile = own_ref[:C, lane(row - 5)]
        else:
            tile = after_ref[:, lane((4, 5, 0, 1, 2)[row - 13])]
        if 4 <= row < 14:
            x_ref[:, lane(row - 4)] = tile
        shifted_rows(base_ref, row, tile)

    level = lax.broadcasted_iota(jnp.int32, (8, WIDE), 1) % 8
    rise_of = {
        -1: jnp.where(level == 0, -1.0, 0.0),
        0: jnp.zeros((8, WIDE), F32),
        1: jnp.where(level == 7, 1.0, 0.0),
    }

    def masks(row, carry):
        here = code_ref[:, lane(row + 1)]
        for ox in (-1, 0, 1):
            near = code_ref[:, lane(row + 1 + ox)]
            for oy in (-1, 0, 1):
                rise = turn(near, -8 * oy) - here
                for oz in (-1, 0, 1):
                    keep = jnp.where(rise == rise_of[oz], 1.0, 0.0)
                    tap = 9 * (ox + 1) + 3 * (oy + 1) + oz + 1
                    mask_ref[tap, :, lane(row)] = jnp.concatenate([keep, keep], 0).astype(BF16)
        return carry

    lax.fori_loop(0, 16, masks, 0)

    def forward(pair, carry):
        make_cols(cols_ref, base_ref, mask_ref, 2 * pair + 1, 2 * pair)
        pre_ref[:, lane(2 * pair, 2)] = product(fwd_ref[...], cols_ref[...])
        return carry

    lax.fori_loop(0, 8, forward, 0)
    for row in range(16):
        pre = pre_ref[:, lane(row)]
        sigma = 1.0 / (1.0 + jnp.exp(-pre))
        slope_ref[:, lane(row)] = sigma * (1.0 + pre * (1.0 - sigma))


def top_kernel(
    own_ref, before_ref, after_ref, slope_ref, mask_ref, bwd_ref,
    result_ref, grad_ref, out_ref,
    base_ref, cols_ref, top_ref,
):
    active = lax.axis_index("pipe") == SECTIONS - 1
    for row in range(1, 17):
        if row < 5:
            tile = before_ref[:, lane(row - 1)]
        elif row < 13:
            tile = own_ref[C : 2 * C, lane(row - 5)]
        else:
            tile = after_ref[:, lane(row - 13)]
        top_ref[:, lane(row - 1)] = jnp.where(active, tile, jnp.zeros_like(tile))

    def store(pair, value):
        result_ref[:, lane(2 * pair, 2)] = value

    step_rows(top_ref, slope_ref, mask_ref, bwd_ref, base_ref, cols_ref, store, 16, 1)
    for row in range(8):
        grad_ref[:, lane(row)] = base_ref[4, :, lane(row + 4)]
        out_ref[:, lane(row)] = result_ref[:, lane(row + 3)]


def step_rows(incoming_ref, slope_ref, mask_ref, bwd_ref, base_ref, cols_ref, store, count, first):
    for row in range(count):
        grad = (
            incoming_ref[:, lane(row)].astype(F32) * slope_ref[:, lane(row + first - 1)]
        ).astype(BF16)
        shifted_rows(base_ref, row, grad)

    def backward(pair, carry):
        make_cols(cols_ref, base_ref, mask_ref, 2 * pair + 1, 2 * pair + first)
        total = incoming_ref[:, lane(2 * pair + 1, 2)].astype(F32) + product(
            bwd_ref[...], cols_ref[...]
        )
        store(pair, total.astype(BF16))
        return carry

    lax.fori_loop(0, (count - 2) // 2, backward, 0)


def middle_kernel(
    count, first, incoming_ref, slope_ref, mask_ref, bwd_ref, grad_in, out_in,
    result_ref, grad_ref, out_ref, base_ref, cols_ref,
):
    def store(pair, value):
        result_ref[:, lane(2 * pair, 2)] = value

    step_rows(
        incoming_ref, slope_ref, mask_ref, bwd_ref, base_ref, cols_ref, store, count, first
    )
    for row in range(8):
        grad_ref[:, lane(row)] = grad_in[:, lane(row)] + base_ref[4, :, lane(row + 5 - first)]
        out_ref[:, lane(row)] = out_in[:, lane(row)] + result_ref[:, lane(row + 4 - first)]


def late_kernel(
    count, first, incoming_ref, slope_ref, mask_ref, bwd_ref, grad_in, out_in,
    centre_ref, left_ref, right_ref, grad_ref, out_ref, base_ref, cols_ref, result_ref,
):
    middle_kernel(
        count, first, incoming_ref, slope_ref, mask_ref, bwd_ref, grad_in, out_in,
        result_ref, grad_ref, out_ref, base_ref, cols_ref,
    )
    rows = [result_ref[:, lane(row)] for row in range(count - 2)]
    for row in range(0, count - 2, 2):
        centre_ref[:, lane(row // 2)] = jnp.concatenate(
            [rows[row][:, 32:96], rows[row + 1][:, 32:96]], 1
        )
    spare = jnp.zeros((C, WIDE - 8 * (count - 2)), BF16)
    left_ref[...] = jnp.concatenate([row[:, 32:40] for row in rows] + [spare], 1)
    right_ref[...] = jnp.concatenate([row[:, 88:96] for row in rows] + [spare], 1)


def last_kernel(
    centre_ref, from_left, from_right, slope_ref, mask_ref, bwd_ref, x_ref, grad_in, out_in,
    out_ref, terms_ref, base_ref, cols_ref, incoming_ref, sums_ref, all_ref,
):
    pad = jnp.zeros((C, 24), BF16)
    for row in range(10):
        at = 64 * row
        incoming_ref[:, lane(row)] = jnp.concatenate(
            [
                pad,
                from_left[:, 8 * row : 8 * row + 8],
                centre_ref[:, at : at + 64],
                from_right[:, 8 * row : 8 * row + 8],
                pad,
            ],
            1,
        )

    def store(pair, value):
        sums_ref[:, lane(2 * pair, 2)] = out_in[:, lane(2 * pair, 2)] + value

    step_rows(incoming_ref, slope_ref, mask_ref, bwd_ref, base_ref, cols_ref, store, 10, 4)
    for pair in range(4):
        first, second = sums_ref[:, lane(2 * pair)], sums_ref[:, lane(2 * pair + 1)]
        out_ref[:, lane(pair)] = jnp.concatenate([first[:, 32:96], second[:, 32:96]], 1)

    where = lax.broadcasted_iota(jnp.int32, (C, WIDE), 1)
    inside = (where >= 32) & (where < 96)
    grads = []
    for row in range(8):
        grad = grad_in[:, lane(row)] + base_ref[4, :, lane(row + 1)]
        grads.append(jnp.where(inside, grad, jnp.zeros_like(grad)))
    grads = jnp.concatenate(grads, 1)
    for row in range(10):
        shifted_rows(base_ref, row, x_ref[:, lane(row)])

    def gather(pair, carry):
        make_cols(all_ref, base_ref, mask_ref, 2 * pair + 1, 2 * pair + 4, 2 * pair)
        return carry

    lax.fori_loop(0, 4, gather, 0)
    for tap in range(TAPS):
        part = lax.dot_general(
            all_ref[C * tap : C * tap + C, :], grads, (((1,), (1,)), ((), ())),
            preferred_element_type=F32,
        )
        terms_ref[C * tap : C * tap + C, :] = jnp.concatenate(
            [part, jnp.zeros((C, WIDE - C), F32)], 1
        ).astype(BF16)
    terms_ref[DEEP:, :] = jnp.zeros((COLS * CHUNK - DEEP, WIDE), BF16)


def scale_kernel(whole_ref, out_ref):
    total = whole_ref[:DEEP, :C].astype(F32)
    mean = jnp.sum(total * total) / (DEEP * C)
    out_ref[...] = total * lax.rsqrt(mean + 1e-06)


def groups(devices):
    rows = devices // (2 * ROWS)
    near = [[y * 32 + z * 2 + c for y in range(rows) for c in range(2)] for z in range(ROWS)]
    far = [[y * 32 + z * 2 + c for z in range(ROWS)] for y in range(rows) for c in range(2)]
    return near, far


def body(section_input, top_grad, conv_weight, brick_height):
    devices = lax.axis_size("space")
    both = ("space", "pipe")

    def between(by_row, by_col, sections):
        pairs = []
        for x in range(ROWS):
            for y in range(COLS):
                if 0 <= x + by_row < ROWS and 0 <= y + by_col < COLS:
                    source = x * COLS + y
                    target = (x + by_row) * COLS + y + by_col
                    for a, b in sections:
                        pairs.append((source * SECTIONS + a, target * SECTIONS + b))
        return pairs

    same = [(s, s) for s in range(SECTIONS)]
    code = jnp.broadcast_to((brick_height + CODE).astype(BF16)[:, None], (16, CELLS))
    own = jnp.concatenate([section_input.reshape(C, CELLS), top_grad.reshape(C, CELLS), code], 0)
    fwd, bwd = call(weight_kernel, [((C, DEEP), BF16)] * 2)(conv_weight[0])
    left = lax.ppermute(own, both, between(0, 1, same))
    right = lax.ppermute(own, both, between(0, -1, same))
    own, up, down = call(
        pack_kernel,
        [((2 * C + 16, 8 * WIDE), BF16), ((C, 6 * WIDE), BF16), ((C, 6 * WIDE), BF16)],
    )(own, left, right)
    before = lax.ppermute(up, both, between(1, 0, same))
    after = lax.ppermute(down, both, between(-1, 0, same))
    top_before = lax.ppermute(before, both, between(0, 0, [(0, SECTIONS - 1)]))
    top_after = lax.ppermute(after, both, between(0, 0, [(0, SECTIONS - 1)]))

    core = ((C, 8 * WIDE), BF16)
    cols = ((DEEP, 2 * WIDE), BF16)
    slope, mask, x_rows = call(
        forward_kernel,
        [((C, 16 * WIDE), F32), ((TAPS, 16, 16 * WIDE), BF16), ((C, 10 * WIDE), BF16)],
        [((9, C, 18 * WIDE), BF16), cols, ((8, 18 * WIDE), F32), ((C, 16 * WIDE), F32)],
    )(own, before, after, fwd)
    result, grad, out = call(
        top_kernel,
        [((C, 14 * WIDE), BF16), core, core],
        [((9, C, 16 * WIDE), BF16), cols, ((C, 16 * WIDE), BF16)],
    )(own, top_before, top_after, slope, mask, bwd)
    incoming = lax.ppermute(result, both, between(0, 0, [(3, 2)]))
    result, grad, out = call(
        functools.partial(middle_kernel, 14, 2),
        [((C, 12 * WIDE), BF16), core, core],
        [((9, C, 14 * WIDE), BF16), cols],
    )(incoming, slope, mask, bwd, grad, out)
    incoming = lax.ppermute(result, both, between(0, 0, [(2, 1)]))
    centre, left, right, grad, out = call(
        functools.partial(late_kernel, 12, 3),
        [((C, 5 * WIDE), BF16), ((C, WIDE), BF16), ((C, WIDE), BF16), core, core],
        [((9, C, 12 * WIDE), BF16), cols, ((C, 10 * WIDE), BF16)],
    )(incoming, slope, mask, bwd, grad, out)
    centre = lax.ppermute(centre, both, between(0, 0, [(1, 0)]))
    from_left = lax.ppermute(right, both, between(0, 1, [(1, 0)]))
    from_right = lax.ppermute(left, both, between(0, -1, [(1, 0)]))
    out, terms = call(
        last_kernel,
        [((C, CELLS), BF16), ((COLS * CHUNK, WIDE), BF16)],
        [((9, C, 10 * WIDE), BF16), cols, ((C, 10 * WIDE), BF16), core, ((DEEP, 8 * WIDE), BF16)],
    )(centre, from_left, from_right, slope, mask, bwd, x_rows, grad, out)

    near, far = groups(devices)
    parts = lax.all_to_all(
        terms.reshape(COLS, CHUNK, WIDE), "space", 0, 0, axis_index_groups=near
    )
    part = jnp.sum(parts.astype(F32), 0).astype(BF16)
    pieces = lax.all_to_all(
        part.reshape(ROWS, CHUNK // ROWS, WIDE), "space", 0, 0, axis_index_groups=far
    )
    piece = jnp.sum(pieces.astype(F32), 0).astype(BF16)
    copies = jnp.broadcast_to(piece[None], (ROWS,) + piece.shape)
    part = lax.all_to_all(copies, "space", 0, 0, axis_index_groups=far)
    whole = lax.all_gather(part.reshape(CHUNK, WIDE), "space", axis_index_groups=near)
    (weight_grad,) = call(scale_kernel, [((DEEP, C), F32)])(whole.reshape(COLS * CHUNK, WIDE))
    return (out.reshape(1, 1, C, CELLS), weight_grad.reshape(1, TAPS, C, C))


def solution(mesh):
    return jax.shard_map(
        body,
        mesh=mesh,
        in_specs=(
            P("pipe", "space", None, None),
            P("space", None, None),
            P("pipe", None, None, None),
            P("space"),
        ),
        out_specs=(P("pipe", "space", None, None), P("pipe", None, None, None)),
        check_vma=False,
    )
```

```python
import functools

import jax
import jax.numpy as jnp
from jax import lax
from jax.experimental import pallas as pl
from jax.experimental.pallas import tpu as pltpu
from jax.sharding import PartitionSpec as P

C = 96
CELLS = 512
COLS = 8
ROWS = 16
SECTIONS = 4
TAPS = 27
DEEP = TAPS * C
WIDE = 128
CODE = 8
CHUNK = 256
VMEM_BYTES = 32 * 1024 * 1024
F32 = jnp.float32
BF16 = jnp.bfloat16


def call(kernel, outs, scratch=(), leave=()):
    shapes = [
        jax.ShapeDtypeStruct(shape, dtype) if n in leave else pltpu.VMEM(shape, dtype)
        for n, (shape, dtype) in enumerate(outs)
    ]

    def run(*args):
        inner = pl.pallas_call(
            kernel,
            out_shape=shapes,
            in_specs=[pl.BlockSpec(memory_space=pltpu.VMEM)] * len(args),
            out_specs=[pl.BlockSpec(memory_space=pltpu.VMEM)] * len(shapes),
            scratch_shapes=[pltpu.VMEM(shape, dtype) for shape, dtype in scratch],
            compiler_params=pltpu.CompilerParams(vmem_limit_bytes=VMEM_BYTES),
        )
        return inner(*[pltpu.with_memory_space_constraint(arg, pltpu.VMEM) for arg in args])

    return run


def lane(row, count=1):
    start = row * WIDE
    if not isinstance(start, int):
        start = pl.multiple_of(start, WIDE)
    return pl.ds(start, count * WIDE)


def turn(value, by):
    by = by % value.shape[1]
    return pltpu.roll(value, by, 1) if by else value


def shifted_rows(base_ref, row, tile):
    level = lax.broadcasted_iota(jnp.int32, (C, WIDE), 1) % 8
    for oy in (-1, 0, 1):
        for oz in (-1, 0, 1):
            if oz == 0:
                moved = turn(tile, -8 * oy)
            elif oz > 0:
                moved = jnp.where(level < 7, turn(tile, -8 * oy - 1), turn(tile, -8 * oy + 7))
            else:
                moved = jnp.where(level > 0, turn(tile, -8 * oy + 1), turn(tile, -8 * oy - 7))
            base_ref[3 * (oy + 1) + oz + 1, :, lane(row)] = moved


def make_cols(cols_ref, base_ref, mask_ref, base_row, mask_row, at=0):
    for ox in (-1, 0, 1):
        for j in range(9):
            tap = 9 * (ox + 1) + j
            tile = base_ref[j, :, lane(base_row + ox, 2)].reshape(C // 16, 16, 2 * WIDE)
            kept = tile * mask_ref[tap, :, lane(mask_row, 2)][None]
            cols_ref[C * tap : C * tap + C, lane(at, 2)] = kept.reshape(C, 2 * WIDE)


def product(weight, cols):
    return lax.dot_general(
        weight, cols, (((1,), (0,)), ((), ())), preferred_element_type=F32
    )


def weight_kernel(w_ref, fwd_ref, bwd_ref):
    for q in range(TAPS):
        fwd_ref[:, C * q : C * q + C] = w_ref[q].T
        bwd_ref[:, C * q : C * q + C] = w_ref[TAPS - 1 - q]


def pack_kernel(own_ref, left_ref, right_ref, own_out, up_out, down_out):
    lowest = lax.axis_index("pipe") == 0
    rows = []
    for i in range(8):
        at = 64 * i
        rows.append(
            jnp.concatenate(
                [
                    left_ref[:, at + 32 : at + 64],
                    own_ref[:, at : at + 64],
                    right_ref[:, at : at + 32],
                ],
                1,
            )
        )
        own_out[:, lane(i)] = rows[i]
    code = jnp.concatenate([rows[0][2 * C :]] * (C // 16), 0)
    own_code = jnp.concatenate([own_ref[2 * C :, :WIDE]] * (C // 16), 0)
    where = lax.broadcasted_iota(jnp.int32, (C, WIDE), 1)
    for out, order, tops in (
        (up_out, (3, 4, 5, None, 6, 7), (4, 5, 6, 7)),
        (down_out, (2, 3, 4, None, 0, 1), (0, 1, 2, 3)),
    ):

        @pl.when(jnp.logical_not(lowest))
        def _(out=out, order=order):
            for slot, row in enumerate(order):
                out[:, lane(slot)] = code if row is None else rows[row][:C]

        @pl.when(lowest)
        def _(out=out, order=order, tops=tops):
            tiles = [rows[row][C : 2 * C] for row in tops]
            out[:, lane(0)] = jnp.where((where < 8) | (where >= 120), code, tiles[0])
            out[:, lane(1)] = jnp.where(where < 8, own_code, tiles[1])
            out[:, lane(2)] = tiles[2]
            out[:, lane(3)] = tiles[3]
            out[:, lane(4)] = rows[order[4]][:C]
            out[:, lane(5)] = rows[order[5]][:C]


def side_code(side_ref):
    where = lax.broadcasted_iota(jnp.int32, (8, WIDE), 1)
    first, second = side_ref[0:8, lane(0)].astype(F32), side_ref[0:8, lane(1)].astype(F32)
    parts = jnp.where(
        where < 32, first[:, 0:1], jnp.where(where < 96, second[:, 0:1], first[:, 127:128])
    )
    return jnp.where(lax.axis_index("pipe") == 0, parts, side_ref[0:8, lane(3)].astype(F32))


def forward_kernel(
    own_ref, before_ref, after_ref, fwd_ref,
    slope_ref, mask_ref, x_ref,
    base_ref, cols_ref, code_ref, pre_ref,
):
    own_code = own_ref[2 * C : 2 * C + 8, :WIDE].astype(F32)
    before_code = side_code(before_ref)
    after_code = side_code(after_ref)
    for row in range(18):
        code = before_code if row < 5 else own_code if row < 13 else after_code
        code_ref[:, lane(row)] = code
    for row in range(18):
        if row < 5:
            tile = before_ref[:, lane((0, 1, 2, 4, 5)[row])]
        elif row < 13:
            tile = own_ref[:C, lane(row - 5)]
        else:
            tile = after_ref[:, lane((4, 5, 0, 1, 2)[row - 13])]
        if 4 <= row < 14:
            x_ref[:, lane(row - 4)] = tile
        shifted_rows(base_ref, row, tile)

    level = lax.broadcasted_iota(jnp.int32, (8, WIDE), 1) % 8
    rise_of = {
        -1: jnp.where(level == 0, -1.0, 0.0),
        0: jnp.zeros((8, WIDE), F32),
        1: jnp.where(level == 7, 1.0, 0.0),
    }

    def masks(row, carry):
        here = code_ref[:, lane(row + 1)]
        for ox in (-1, 0, 1):
            near = code_ref[:, lane(row + 1 + ox)]
            for oy in (-1, 0, 1):
                rise = turn(near, -8 * oy) - here
                for oz in (-1, 0, 1):
                    keep = jnp.where(rise == rise_of[oz], 1.0, 0.0)
                    tap = 9 * (ox + 1) + 3 * (oy + 1) + oz + 1
                    mask_ref[tap, :, lane(row)] = jnp.concatenate([keep, keep], 0).astype(BF16)
        return carry

    lax.fori_loop(0, 16, masks, 0)

    def forward(pair, carry):
        make_cols(cols_ref, base_ref, mask_ref, 2 * pair + 1, 2 * pair)
        pre_ref[:, lane(2 * pair, 2)] = product(fwd_ref[...], cols_ref[...])
        return carry

    lax.fori_loop(0, 8, forward, 0)
    for row in range(16):
        pre = pre_ref[:, lane(row)]
        sigma = 1.0 / (1.0 + jnp.exp(-pre))
        slope_ref[:, lane(row)] = sigma * (1.0 + pre * (1.0 - sigma))


def top_kernel(
    own_ref, before_ref, after_ref, slope_ref, mask_ref, bwd_ref,
    result_ref, grad_ref, out_ref,
    base_ref, cols_ref, top_ref,
):
    active = lax.axis_index("pipe") == SECTIONS - 1
    for row in range(1, 17):
        if row < 5:
            tile = before_ref[:, lane(row - 1)]
        elif row < 13:
            tile = own_ref[C : 2 * C, lane(row - 5)]
        else:
            tile = after_ref[:, lane(row - 13)]
        top_ref[:, lane(row - 1)] = jnp.where(active, tile, jnp.zeros_like(tile))

    def store(pair, value):
        result_ref[:, lane(2 * pair, 2)] = value

    step_rows(top_ref, slope_ref, mask_ref, bwd_ref, base_ref, cols_ref, store, 16, 1)
    for row in range(8):
        grad_ref[:, lane(row)] = base_ref[4, :, lane(row + 4)]
        out_ref[:, lane(row)] = result_ref[:, lane(row + 3)]


def step_rows(incoming_ref, slope_ref, mask_ref, bwd_ref, base_ref, cols_ref, store, count, first):
    for row in range(count):
        grad = (
            incoming_ref[:, lane(row)].astype(F32) * slope_ref[:, lane(row + first - 1)]
        ).astype(BF16)
        shifted_rows(base_ref, row, grad)

    def backward(pair, carry):
        make_cols(cols_ref, base_ref, mask_ref, 2 * pair + 1, 2 * pair + first)
        total = incoming_ref[:, lane(2 * pair + 1, 2)].astype(F32) + product(
            bwd_ref[...], cols_ref[...]
        )
        store(pair, total.astype(BF16))
        return carry

    lax.fori_loop(0, (count - 2) // 2, backward, 0)


def middle_kernel(
    count, first, incoming_ref, slope_ref, mask_ref, bwd_ref, grad_in, out_in,
    result_ref, grad_ref, out_ref, base_ref, cols_ref,
):
    def store(pair, value):
        result_ref[:, lane(2 * pair, 2)] = value

    step_rows(
        incoming_ref, slope_ref, mask_ref, bwd_ref, base_ref, cols_ref, store, count, first
    )
    for row in range(8):
        grad_ref[:, lane(row)] = grad_in[:, lane(row)] + base_ref[4, :, lane(row + 5 - first)]
        out_ref[:, lane(row)] = out_in[:, lane(row)] + result_ref[:, lane(row + 4 - first)]


def late_kernel(
    count, first, incoming_ref, slope_ref, mask_ref, bwd_ref, grad_in, out_in,
    centre_ref, left_ref, right_ref, grad_ref, out_ref, base_ref, cols_ref, result_ref,
):
    middle_kernel(
        count, first, incoming_ref, slope_ref, mask_ref, bwd_ref, grad_in, out_in,
        result_ref, grad_ref, out_ref, base_ref, cols_ref,
    )
    rows = [result_ref[:, lane(row)] for row in range(count - 2)]
    for row in range(0, count - 2, 2):
        centre_ref[:, lane(row // 2)] = jnp.concatenate(
            [rows[row][:, 32:96], rows[row + 1][:, 32:96]], 1
        )
    spare = jnp.zeros((C, WIDE - 8 * (count - 2)), BF16)
    left_ref[...] = jnp.concatenate([row[:, 32:40] for row in rows] + [spare], 1)
    right_ref[...] = jnp.concatenate([row[:, 88:96] for row in rows] + [spare], 1)


def last_kernel(
    centre_ref, from_left, from_right, slope_ref, mask_ref, bwd_ref, x_ref, grad_in, out_in,
    out_ref, terms_ref, base_ref, cols_ref, incoming_ref, sums_ref, all_ref,
):
    pad = jnp.zeros((C, 24), BF16)
    for row in range(10):
        at = 64 * row
        incoming_ref[:, lane(row)] = jnp.concatenate(
            [
                pad,
                from_left[:, 8 * row : 8 * row + 8],
                centre_ref[:, at : at + 64],
                from_right[:, 8 * row : 8 * row + 8],
                pad,
            ],
            1,
        )

    def store(pair, value):
        sums_ref[:, lane(2 * pair, 2)] = out_in[:, lane(2 * pair, 2)] + value

    step_rows(incoming_ref, slope_ref, mask_ref, bwd_ref, base_ref, cols_ref, store, 10, 4)
    for pair in range(4):
        first, second = sums_ref[:, lane(2 * pair)], sums_ref[:, lane(2 * pair + 1)]
        out_ref[:, lane(pair)] = jnp.concatenate([first[:, 32:96], second[:, 32:96]], 1)

    where = lax.broadcasted_iota(jnp.int32, (C, WIDE), 1)
    inside = (where >= 32) & (where < 96)
    grads = []
    for row in range(8):
        grad = grad_in[:, lane(row)] + base_ref[4, :, lane(row + 1)]
        grads.append(jnp.where(inside, grad, jnp.zeros_like(grad)))
    grads = jnp.concatenate(grads, 1)
    for row in range(10):
        shifted_rows(base_ref, row, x_ref[:, lane(row)])

    def gather(pair, carry):
        make_cols(all_ref, base_ref, mask_ref, 2 * pair + 1, 2 * pair + 4, 2 * pair)
        return carry

    lax.fori_loop(0, 4, gather, 0)
    for four in range(7):
        parts = []
        for tap in range(4 * four, 4 * four + 4):
            if tap < TAPS:
                part = lax.dot_general(
                    all_ref[C * tap : C * tap + C, :], grads, (((1,), (1,)), ((), ())),
                    preferred_element_type=F32,
                ).astype(BF16)
            else:
                part = jnp.zeros((C, C), BF16)
            parts.append(part)
        first, second, third, fourth = parts
        at = 3 * C * four
        terms_ref[at : at + C, :] = jnp.concatenate([first, second[:, :32]], 1)
        terms_ref[at + C : at + 2 * C, :] = jnp.concatenate([second[:, 32:], third[:, :64]], 1)
        terms_ref[at + 2 * C : at + 3 * C, :] = jnp.concatenate([third[:, 64:], fourth], 1)
    terms_ref[21 * C :, :] = jnp.zeros((COLS * CHUNK - 21 * C, WIDE), BF16)


def sum_kernel(parts_ref, out_ref):
    total = parts_ref[0].astype(F32)
    for n in range(1, parts_ref.shape[0]):
        total = total + parts_ref[n].astype(F32)
    total = total.astype(BF16)
    if len(out_ref.shape) == 2:
        out_ref[...] = total
    else:
        for n in range(out_ref.shape[0]):
            out_ref[n] = total


def scale_kernel(whole_ref, out_ref):
    whole = whole_ref[...].astype(F32)
    scale = lax.rsqrt(jnp.sum(whole * whole) / (DEEP * C) + 1e-06)
    for four in range(7):
        at = 3 * C * four
        first, second, third = (
            whole_ref[at + n * C : at + n * C + C, :].astype(F32) * scale for n in range(3)
        )
        parts = (
            first[:, :96],
            jnp.concatenate([first[:, 96:], second[:, :64]], 1),
            jnp.concatenate([second[:, 64:], third[:, :32]], 1),
            third[:, 32:],
        )
        for n, tap in enumerate(range(4 * four, min(4 * four + 4, TAPS))):
            out_ref[C * tap : C * tap + C, :] = parts[n]


def groups(devices):
    rows = devices // (2 * ROWS)
    near = [[y * 32 + z * 2 + c for y in range(rows) for c in range(2)] for z in range(ROWS)]
    far = [[y * 32 + z * 2 + c for z in range(ROWS)] for y in range(rows) for c in range(2)]
    return near, far


def body(section_input, top_grad, conv_weight, brick_height):
    devices = lax.axis_size("space")
    both = ("space", "pipe")

    def between(by_row, by_col, sections):
        pairs = []
        for x in range(ROWS):
            for y in range(COLS):
                if 0 <= x + by_row < ROWS and 0 <= y + by_col < COLS:
                    source = x * COLS + y
                    target = (x + by_row) * COLS + y + by_col
                    for a, b in sections:
                        pairs.append((source * SECTIONS + a, target * SECTIONS + b))
        return pairs

    same = [(s, s) for s in range(SECTIONS)]
    code = jnp.broadcast_to((brick_height + CODE).astype(BF16)[:, None], (16, CELLS))
    own = jnp.concatenate([section_input.reshape(C, CELLS), top_grad.reshape(C, CELLS), code], 0)
    fwd, bwd = call(weight_kernel, [((C, DEEP), BF16)] * 2)(conv_weight[0])
    left = lax.ppermute(own, both, between(0, 1, same))
    right = lax.ppermute(own, both, between(0, -1, same))
    own, up, down = call(
        pack_kernel,
        [((2 * C + 16, 8 * WIDE), BF16), ((C, 6 * WIDE), BF16), ((C, 6 * WIDE), BF16)],
    )(own, left, right)
    before = lax.ppermute(up, both, between(1, 0, same))
    after = lax.ppermute(down, both, between(-1, 0, same))
    before, after, fwd, bwd = lax.optimization_barrier((before, after, fwd, bwd))
    top_before = lax.ppermute(before, both, between(0, 0, [(0, SECTIONS - 1)]))
    top_after = lax.ppermute(after, both, between(0, 0, [(0, SECTIONS - 1)]))

    core = ((C, 8 * WIDE), BF16)
    cols = ((DEEP, 2 * WIDE), BF16)
    slope, mask, x_rows = call(
        forward_kernel,
        [((C, 16 * WIDE), F32), ((TAPS, 16, 16 * WIDE), BF16), ((C, 10 * WIDE), BF16)],
        [((9, C, 18 * WIDE), BF16), cols, ((8, 18 * WIDE), F32), ((C, 16 * WIDE), F32)],
    )(own, before, after, fwd)
    result, grad, out = call(
        top_kernel,
        [((C, 14 * WIDE), BF16), core, core],
        [((9, C, 16 * WIDE), BF16), cols, ((C, 16 * WIDE), BF16)],
    )(own, top_before, top_after, slope, mask, bwd)
    incoming = lax.ppermute(result, both, between(0, 0, [(3, 2)]))
    result, grad, out = call(
        functools.partial(middle_kernel, 14, 2),
        [((C, 12 * WIDE), BF16), core, core],
        [((9, C, 14 * WIDE), BF16), cols],
    )(incoming, slope, mask, bwd, grad, out)
    incoming = lax.ppermute(result, both, between(0, 0, [(2, 1)]))
    centre, left, right, grad, out = call(
        functools.partial(late_kernel, 12, 3),
        [((C, 5 * WIDE), BF16), ((C, WIDE), BF16), ((C, WIDE), BF16), core, core],
        [((9, C, 12 * WIDE), BF16), cols, ((C, 10 * WIDE), BF16)],
    )(incoming, slope, mask, bwd, grad, out)
    centre = lax.ppermute(centre, both, between(0, 0, [(1, 0)]))
    from_left = lax.ppermute(right, both, between(0, 1, [(1, 0)]))
    from_right = lax.ppermute(left, both, between(0, -1, [(1, 0)]))
    out, terms = call(
        last_kernel,
        [((C, CELLS), BF16), ((COLS * CHUNK, WIDE), BF16)],
        [((9, C, 10 * WIDE), BF16), cols, ((C, 10 * WIDE), BF16), core, ((DEEP, 8 * WIDE), BF16)],
        leave=(0,),
    )(centre, from_left, from_right, slope, mask, bwd, x_rows, grad, out)

    near, far = groups(devices)
    parts = lax.all_to_all(
        terms.reshape(COLS, CHUNK, WIDE), "space", 0, 0, axis_index_groups=near
    )
    (part,) = call(sum_kernel, [((CHUNK, WIDE), BF16)])(parts)
    pieces = lax.all_to_all(
        part.reshape(ROWS, CHUNK // ROWS, WIDE), "space", 0, 0, axis_index_groups=far
    )
    (copies,) = call(sum_kernel, [((ROWS, CHUNK // ROWS, WIDE), BF16)])(pieces)
    part = lax.all_to_all(copies, "space", 0, 0, axis_index_groups=far)
    whole = lax.all_gather(part.reshape(CHUNK, WIDE), "space", axis_index_groups=near)
    (weight_grad,) = call(scale_kernel, [((DEEP, C), F32)], leave=(0,))(whole.reshape(COLS * CHUNK, WIDE))
    return (out.reshape(1, 1, C, CELLS), weight_grad.reshape(1, TAPS, C, C))


def solution(mesh):
    return jax.shard_map(
        body,
        mesh=mesh,
        in_specs=(
            P("pipe", "space", None, None),
            P("space", None, None),
            P("pipe", None, None, None),
            P("space"),
        ),
        out_specs=(P("pipe", "space", None, None), P("pipe", None, None, None)),
        check_vma=False,
    )
```

```python
import functools

import jax
import jax.numpy as jnp
from jax import lax
from jax.experimental import pallas as pl
from jax.experimental.pallas import tpu as pltpu
from jax.sharding import PartitionSpec as P

C = 96
CELLS = 512
COLS = 8
ROWS = 16
SECTIONS = 4
TAPS = 27
DEEP = TAPS * C
WIDE = 128
CODE = 8
CHUNK = 256
VMEM_BYTES = 32 * 1024 * 1024
F32 = jnp.float32
BF16 = jnp.bfloat16


def call(kernel, outs, scratch=(), leave=()):
    shapes = [
        jax.ShapeDtypeStruct(shape, dtype) if n in leave else pltpu.VMEM(shape, dtype)
        for n, (shape, dtype) in enumerate(outs)
    ]

    def run(*args):
        inner = pl.pallas_call(
            kernel,
            out_shape=shapes,
            in_specs=[
                pl.BlockSpec(memory_space=pltpu.SMEM if arg.dtype == jnp.int32 else pltpu.VMEM)
                for arg in args
            ],
            out_specs=[pl.BlockSpec(memory_space=pltpu.VMEM)] * len(shapes),
            scratch_shapes=[pltpu.VMEM(shape, dtype) for shape, dtype in scratch],
            compiler_params=pltpu.CompilerParams(vmem_limit_bytes=VMEM_BYTES),
        )
        return inner(
            *[
                arg if arg.dtype == jnp.int32
                else pltpu.with_memory_space_constraint(arg, pltpu.VMEM)
                for arg in args
            ]
        )

    return run


def lane(row, count=1):
    start = row * WIDE
    if not isinstance(start, int):
        start = pl.multiple_of(start, WIDE)
    return pl.ds(start, count * WIDE)


def turn(value, by):
    by = by % value.shape[1]
    return pltpu.roll(value, by, 1) if by else value


def shifted_rows(base_ref, row, tile):
    level = lax.broadcasted_iota(jnp.int32, (C, WIDE), 1) % 8
    for oy in (-1, 0, 1):
        for oz in (-1, 0, 1):
            if oz == 0:
                moved = turn(tile, -8 * oy)
            elif oz > 0:
                moved = jnp.where(level < 7, turn(tile, -8 * oy - 1), turn(tile, -8 * oy + 7))
            else:
                moved = jnp.where(level > 0, turn(tile, -8 * oy + 1), turn(tile, -8 * oy - 7))
            base_ref[3 * (oy + 1) + oz + 1, :, lane(row)] = moved


def make_cols(cols_ref, base_ref, mask_ref, base_row, mask_row, at=0):
    for ox in (-1, 0, 1):
        for j in range(9):
            tap = 9 * (ox + 1) + j
            tile = base_ref[j, :, lane(base_row + ox, 2)].reshape(C // 16, 16, 2 * WIDE)
            kept = tile * mask_ref[tap, :, lane(mask_row, 2)][None]
            cols_ref[C * tap : C * tap + C, lane(at, 2)] = kept.reshape(C, 2 * WIDE)


def product(weight, cols):
    return lax.dot_general(
        weight, cols, (((1,), (0,)), ((), ())), preferred_element_type=F32
    )


def weight_kernel(w_ref, fwd_ref, bwd_ref):
    for q in range(TAPS):
        fwd_ref[:, C * q : C * q + C] = w_ref[q].T
        bwd_ref[:, C * q : C * q + C] = w_ref[TAPS - 1 - q]


def code_of(height_ref, shape):
    return jnp.full(shape, (height_ref[0] + CODE).astype(F32), F32)


def rows_kernel(x_ref, top_ref, height_ref, up_ref, down_ref, x_out, top_out):
    lowest = lax.axis_index("pipe") == 0
    code = code_of(height_ref, (16, 3 * WIDE)).astype(BF16)
    spare = jnp.zeros((C, 64), BF16)
    up_ref[C:, :] = code
    down_ref[C:, :] = code
    up_ref[:C, :WIDE] = x_ref[:, 384:512]
    down_ref[:C, :WIDE] = x_ref[:, 0:128]
    x_out[...] = x_ref[...]
    top_out[...] = top_ref[...]

    @pl.when(lowest)
    def _():
        up_ref[:C, WIDE:] = top_ref[:, 256:512]
        down_ref[:C, WIDE:] = top_ref[:, 0:256]

    @pl.when(jnp.logical_not(lowest))
    def _():
        up_ref[:C, WIDE:] = jnp.concatenate([x_ref[:, 192:384], spare], 1)
        down_ref[:C, WIDE:] = jnp.concatenate([x_ref[:, 128:320], spare], 1)


def x_layer(x_ref, before_ref, after_ref, row):
    if row < 5:
        at = 64 * (row - 3) if row >= 3 else WIDE + 64 * row
        return before_ref[:C, at : at + 64]
    if row < 13:
        return x_ref[:, 64 * (row - 5) : 64 * (row - 5) + 64]
    at = 64 * (row - 13) if row < 15 else WIDE + 64 * (row - 15)
    return after_ref[:C, at : at + 64]


def top_layer(top_ref, before_ref, after_ref, row):
    if row < 5:
        return before_ref[:C, WIDE + 64 * (row - 1) : WIDE + 64 * row]
    if row < 13:
        return top_ref[:, 64 * (row - 5) : 64 * (row - 5) + 64]
    return after_ref[:C, WIDE + 64 * (row - 13) : WIDE + 64 * (row - 12)]


def join(parts):
    return jnp.concatenate(parts, 1)


def cols_kernel(x_ref, top_ref, height_ref, before_ref, after_ref, right_ref, left_ref):
    lowest = lax.axis_index("pipe") == 0
    codes = join(
        [before_ref[C:, :WIDE], code_of(height_ref, (16, WIDE)).astype(BF16), after_ref[C:, :WIDE]]
    )
    for out, start in ((right_ref, 32), (left_ref, 0)):

        def piece(layer, start=start):
            return layer[:, start : start + 32]

        out[C:, : 3 * WIDE] = codes
        out[C:, 3 * WIDE :] = jnp.zeros((16, 4 * WIDE), BF16)
        for four in range(3):
            rows = range(3 + 4 * four, 7 + 4 * four)
            out[:C, lane(four)] = join(
                [piece(x_layer(x_ref, before_ref, after_ref, row)) for row in rows]
            )

        @pl.when(lowest)
        def _(out=out, piece=piece):
            for four in range(4):
                rows = range(1 + 4 * four, 5 + 4 * four)
                out[:C, lane(3 + four)] = join(
                    [piece(top_layer(top_ref, before_ref, after_ref, row)) for row in rows]
                )

        @pl.when(jnp.logical_not(lowest))
        def _(out=out, piece=piece):
            outer = [
                piece(x_layer(x_ref, before_ref, after_ref, row)) for row in (0, 1, 2, 15, 16, 17)
            ]
            out[:C, lane(3)] = join(outer[:4])
            out[:C, lane(4)] = join(outer[4:] + [jnp.zeros((C, 64), BF16)])
            out[:C, lane(5, 2)] = jnp.zeros((C, 2 * WIDE), BF16)


def x_side(side_ref, row):
    if 3 <= row < 15:
        at = 32 * (row - 3)
    else:
        at = 3 * WIDE + 32 * (row if row < 3 else row - 12)
    return side_ref[:C, at : at + 32]


def top_side(side_ref, row):
    return side_ref[:C, 3 * WIDE + 32 * (row - 1) : 3 * WIDE + 32 * row]


def halo_kernel(before_ref, after_ref, left_ref, right_ref, halo_ref):
    @pl.when(lax.axis_index("pipe") == 0)
    def _():
        for n, row in enumerate((1, 2, 3, 4, 13, 14, 15, 16)):
            middle = top_layer(None, before_ref, after_ref, row)
            halo_ref[:, lane(n)] = join([top_side(left_ref, row), middle, top_side(right_ref, row)])
        for pair in range(4):
            first, second = 5 + 2 * pair, 6 + 2 * pair
            halo_ref[:, lane(8 + pair)] = join(
                [
                    top_side(left_ref, first),
                    top_side(right_ref, first),
                    top_side(left_ref, second),
                    top_side(right_ref, second),
                ]
            )


def forward_kernel(
    x_ref, height_ref, before_ref, after_ref, left_ref, right_ref, fwd_ref,
    slope_ref, mask_ref, rows_ref,
    base_ref, cols_ref, code_ref, pre_ref,
):
    where = lax.broadcasted_iota(jnp.int32, (8, WIDE), 1)
    middle = (
        before_ref[C : C + 8, :WIDE].astype(F32),
        code_of(height_ref, (8, WIDE)),
        after_ref[C : C + 8, :WIDE].astype(F32),
    )
    codes = []
    for n in range(3):
        left = left_ref[C : C + 8, lane(n)].astype(F32)
        right = right_ref[C : C + 8, lane(n)].astype(F32)
        codes.append(jnp.where(where < 32, left, jnp.where(where < 96, middle[n], right)))
    for row in range(18):
        code_ref[:, lane(row)] = codes[0 if row < 5 else 1 if row < 13 else 2]
    for row in range(18):
        tile = join(
            [
                x_side(left_ref, row),
                x_layer(x_ref, before_ref, after_ref, row),
                x_side(right_ref, row),
            ]
        )
        if 4 <= row < 14:
            rows_ref[:, lane(row - 4)] = tile
        shifted_rows(base_ref, row, tile)

    level = lax.broadcasted_iota(jnp.int32, (8, WIDE), 1) % 8
    rise_of = {
        -1: jnp.where(level == 0, -1.0, 0.0),
        0: jnp.zeros((8, WIDE), F32),
        1: jnp.where(level == 7, 1.0, 0.0),
    }

    def masks(row, carry):
        here = code_ref[:, lane(row + 1)]
        for ox in (-1, 0, 1):
            near = code_ref[:, lane(row + 1 + ox)]
            for oy in (-1, 0, 1):
                rise = turn(near, -8 * oy) - here
                for oz in (-1, 0, 1):
                    keep = jnp.where(rise == rise_of[oz], 1.0, 0.0)
                    tap = 9 * (ox + 1) + 3 * (oy + 1) + oz + 1
                    mask_ref[tap, :, lane(row)] = jnp.concatenate([keep, keep], 0).astype(BF16)
        return carry

    lax.fori_loop(0, 16, masks, 0)

    def forward(pair, carry):
        make_cols(cols_ref, base_ref, mask_ref, 2 * pair + 1, 2 * pair)
        pre_ref[:, lane(2 * pair, 2)] = product(fwd_ref[...], cols_ref[...])
        return carry

    lax.fori_loop(0, 8, forward, 0)
    for row in range(16):
        pre = pre_ref[:, lane(row)]
        sigma = 1.0 / (1.0 + jnp.exp(-pre))
        slope_ref[:, lane(row)] = sigma * (1.0 + pre * (1.0 - sigma))


def top_kernel(
    own_ref, halo_ref, slope_ref, mask_ref, bwd_ref,
    result_ref, grad_ref, out_ref,
    base_ref, cols_ref, top_ref,
):
    active = lax.axis_index("pipe") == SECTIONS - 1
    for row in range(1, 17):
        if row < 5:
            tile = halo_ref[:, lane(row - 1)]
        elif row < 13:
            at = 8 * WIDE + 64 * (row - 5)
            middle = own_ref[:, 64 * (row - 5) : 64 * (row - 5) + 64]
            tile = join([halo_ref[:, at : at + 32], middle, halo_ref[:, at + 32 : at + 64]])
        else:
            tile = halo_ref[:, lane(row - 9)]
        top_ref[:, lane(row - 1)] = jnp.where(active, tile, jnp.zeros_like(tile))

    def store(pair, value):
        result_ref[:, lane(2 * pair, 2)] = value

    step_rows(top_ref, slope_ref, mask_ref, bwd_ref, base_ref, cols_ref, store, 16, 1)
    for row in range(8):
        grad_ref[:, lane(row)] = base_ref[4, :, lane(row + 4)]
        out_ref[:, lane(row)] = result_ref[:, lane(row + 3)]


def step_rows(incoming_ref, slope_ref, mask_ref, bwd_ref, base_ref, cols_ref, store, count, first):
    for row in range(count):
        grad = (
            incoming_ref[:, lane(row)].astype(F32) * slope_ref[:, lane(row + first - 1)]
        ).astype(BF16)
        shifted_rows(base_ref, row, grad)

    def backward(pair, carry):
        make_cols(cols_ref, base_ref, mask_ref, 2 * pair + 1, 2 * pair + first)
        total = incoming_ref[:, lane(2 * pair + 1, 2)].astype(F32) + product(
            bwd_ref[...], cols_ref[...]
        )
        store(pair, total.astype(BF16))
        return carry

    lax.fori_loop(0, (count - 2) // 2, backward, 0)


def middle_kernel(
    count, first, incoming_ref, slope_ref, mask_ref, bwd_ref, grad_in, out_in,
    result_ref, grad_ref, out_ref, base_ref, cols_ref,
):
    def store(pair, value):
        result_ref[:, lane(2 * pair, 2)] = value

    step_rows(
        incoming_ref, slope_ref, mask_ref, bwd_ref, base_ref, cols_ref, store, count, first
    )
    for row in range(8):
        grad_ref[:, lane(row)] = grad_in[:, lane(row)] + base_ref[4, :, lane(row + 5 - first)]
        out_ref[:, lane(row)] = out_in[:, lane(row)] + result_ref[:, lane(row + 4 - first)]


def late_kernel(
    count, first, incoming_ref, slope_ref, mask_ref, bwd_ref, grad_in, out_in,
    centre_ref, left_ref, right_ref, grad_ref, out_ref, base_ref, cols_ref, result_ref,
):
    middle_kernel(
        count, first, incoming_ref, slope_ref, mask_ref, bwd_ref, grad_in, out_in,
        result_ref, grad_ref, out_ref, base_ref, cols_ref,
    )
    rows = [result_ref[:, lane(row)] for row in range(count - 2)]
    for row in range(0, count - 2, 2):
        centre_ref[:, lane(row // 2)] = jnp.concatenate(
            [rows[row][:, 32:96], rows[row + 1][:, 32:96]], 1
        )
    spare = jnp.zeros((C, WIDE - 8 * (count - 2)), BF16)
    left_ref[...] = jnp.concatenate([row[:, 32:40] for row in rows] + [spare], 1)
    right_ref[...] = jnp.concatenate([row[:, 88:96] for row in rows] + [spare], 1)


def last_kernel(
    centre_ref, from_left, from_right, slope_ref, mask_ref, bwd_ref, x_ref, grad_in, out_in,
    out_ref, terms_ref, base_ref, cols_ref, incoming_ref, sums_ref, all_ref,
):
    pad = jnp.zeros((C, 24), BF16)
    for row in range(10):
        at = 64 * row
        incoming_ref[:, lane(row)] = jnp.concatenate(
            [
                pad,
                from_left[:, 8 * row : 8 * row + 8],
                centre_ref[:, at : at + 64],
                from_right[:, 8 * row : 8 * row + 8],
                pad,
            ],
            1,
        )

    def store(pair, value):
        sums_ref[:, lane(2 * pair, 2)] = out_in[:, lane(2 * pair, 2)] + value

    step_rows(incoming_ref, slope_ref, mask_ref, bwd_ref, base_ref, cols_ref, store, 10, 4)
    for pair in range(4):
        first, second = sums_ref[:, lane(2 * pair)], sums_ref[:, lane(2 * pair + 1)]
        out_ref[:, lane(pair)] = jnp.concatenate([first[:, 32:96], second[:, 32:96]], 1)

    where = lax.broadcasted_iota(jnp.int32, (C, WIDE), 1)
    inside = (where >= 32) & (where < 96)
    grads = []
    for row in range(8):
        grad = grad_in[:, lane(row)] + base_ref[4, :, lane(row + 1)]
        grads.append(jnp.where(inside, grad, jnp.zeros_like(grad)))
    grads = jnp.concatenate(grads, 1)
    for row in range(10):
        shifted_rows(base_ref, row, x_ref[:, lane(row)])

    def gather(pair, carry):
        make_cols(all_ref, base_ref, mask_ref, 2 * pair + 1, 2 * pair + 4, 2 * pair)
        return carry

    lax.fori_loop(0, 4, gather, 0)
    for four in range(7):
        parts = []
        for tap in range(4 * four, 4 * four + 4):
            if tap < TAPS:
                part = lax.dot_general(
                    all_ref[C * tap : C * tap + C, :], grads, (((1,), (1,)), ((), ())),
                    preferred_element_type=F32,
                ).astype(BF16)
            else:
                part = jnp.zeros((C, C), BF16)
            parts.append(part)
        first, second, third, fourth = parts
        at = 3 * C * four
        terms_ref[at : at + C, :] = jnp.concatenate([first, second[:, :32]], 1)
        terms_ref[at + C : at + 2 * C, :] = jnp.concatenate([second[:, 32:], third[:, :64]], 1)
        terms_ref[at + 2 * C : at + 3 * C, :] = jnp.concatenate([third[:, 64:], fourth], 1)
    terms_ref[21 * C :, :] = jnp.zeros((COLS * CHUNK - 21 * C, WIDE), BF16)


def sum_kernel(parts_ref, out_ref):
    total = parts_ref[0].astype(F32)
    for n in range(1, parts_ref.shape[0]):
        total = total + parts_ref[n].astype(F32)
    total = total.astype(BF16)
    if len(out_ref.shape) == 2:
        out_ref[...] = total
    else:
        for n in range(out_ref.shape[0]):
            out_ref[n] = total


def scale_kernel(whole_ref, out_ref):
    whole = whole_ref[...].astype(F32)
    scale = lax.rsqrt(jnp.sum(whole * whole) / (DEEP * C) + 1e-06)
    for four in range(7):
        at = 3 * C * four
        first, second, third = (
            whole_ref[at + n * C : at + n * C + C, :].astype(F32) * scale for n in range(3)
        )
        parts = (
            first[:, :96],
            jnp.concatenate([first[:, 96:], second[:, :64]], 1),
            jnp.concatenate([second[:, 64:], third[:, :32]], 1),
            third[:, 32:],
        )
        for n, tap in enumerate(range(4 * four, min(4 * four + 4, TAPS))):
            out_ref[C * tap : C * tap + C, :] = parts[n]


def groups(devices):
    rows = devices // (2 * ROWS)
    near = [[y * 32 + z * 2 + c for y in range(rows) for c in range(2)] for z in range(ROWS)]
    far = [[y * 32 + z * 2 + c for z in range(ROWS)] for y in range(rows) for c in range(2)]
    return near, far


def body(section_input, top_grad, conv_weight, brick_height):
    devices = lax.axis_size("space")
    both = ("space", "pipe")

    def between(by_row, by_col, sections):
        pairs = []
        for x in range(ROWS):
            for y in range(COLS):
                if 0 <= x + by_row < ROWS and 0 <= y + by_col < COLS:
                    source = x * COLS + y
                    target = (x + by_row) * COLS + y + by_col
                    for a, b in sections:
                        pairs.append((source * SECTIONS + a, target * SECTIONS + b))
        return pairs

    same = [(s, s) for s in range(SECTIONS)]
    x = section_input.reshape(C, CELLS)
    top = top_grad.reshape(C, CELLS)
    fwd, bwd = call(weight_kernel, [((C, DEEP), BF16)] * 2)(conv_weight[0])
    up, down, x, top = call(
        rows_kernel, [((C + 16, 3 * WIDE), BF16)] * 2 + [((C, CELLS), BF16)] * 2
    )(x, top, brick_height)
    before = lax.ppermute(up, both, between(1, 0, same))
    after = lax.ppermute(down, both, between(-1, 0, same))
    before, after, fwd, bwd = lax.optimization_barrier((before, after, fwd, bwd))
    to_right, to_left = call(cols_kernel, [((C + 16, 7 * WIDE), BF16)] * 2)(
        x, top, brick_height, before, after
    )
    left = lax.ppermute(to_right, both, between(0, 1, same))
    right = lax.ppermute(to_left, both, between(0, -1, same))
    (halo,) = call(halo_kernel, [((C, 12 * WIDE), BF16)])(before, after, left, right)
    halo = lax.ppermute(halo, both, between(0, 0, [(0, SECTIONS - 1)]))

    core = ((C, 8 * WIDE), BF16)
    cols = ((DEEP, 2 * WIDE), BF16)
    slope, mask, x_rows = call(
        forward_kernel,
        [((C, 16 * WIDE), F32), ((TAPS, 16, 16 * WIDE), BF16), ((C, 10 * WIDE), BF16)],
        [((9, C, 18 * WIDE), BF16), cols, ((8, 18 * WIDE), F32), ((C, 16 * WIDE), F32)],
    )(x, brick_height, before, after, left, right, fwd)
    result, grad, out = call(
        top_kernel,
        [((C, 14 * WIDE), BF16), core, core],
        [((9, C, 16 * WIDE), BF16), cols, ((C, 16 * WIDE), BF16)],
    )(top, halo, slope, mask, bwd)
    incoming = lax.ppermute(result, both, between(0, 0, [(3, 2)]))
    result, grad, out = call(
        functools.partial(middle_kernel, 14, 2),
        [((C, 12 * WIDE), BF16), core, core],
        [((9, C, 14 * WIDE), BF16), cols],
    )(incoming, slope, mask, bwd, grad, out)
    incoming = lax.ppermute(result, both, between(0, 0, [(2, 1)]))
    centre, left, right, grad, out = call(
        functools.partial(late_kernel, 12, 3),
        [((C, 5 * WIDE), BF16), ((C, WIDE), BF16), ((C, WIDE), BF16), core, core],
        [((9, C, 12 * WIDE), BF16), cols, ((C, 10 * WIDE), BF16)],
    )(incoming, slope, mask, bwd, grad, out)
    centre = lax.ppermute(centre, both, between(0, 0, [(1, 0)]))
    from_left = lax.ppermute(right, both, between(0, 1, [(1, 0)]))
    from_right = lax.ppermute(left, both, between(0, -1, [(1, 0)]))
    out, terms = call(
        last_kernel,
        [((C, CELLS), BF16), ((COLS * CHUNK, WIDE), BF16)],
        [((9, C, 10 * WIDE), BF16), cols, ((C, 10 * WIDE), BF16), core, ((DEEP, 8 * WIDE), BF16)],
        leave=(0,),
    )(centre, from_left, from_right, slope, mask, bwd, x_rows, grad, out)

    near, far = groups(devices)
    parts = lax.all_to_all(
        terms.reshape(COLS, CHUNK, WIDE), "space", 0, 0, axis_index_groups=near
    )
    (part,) = call(sum_kernel, [((CHUNK, WIDE), BF16)])(parts)
    pieces = lax.all_to_all(
        part.reshape(ROWS, CHUNK // ROWS, WIDE), "space", 0, 0, axis_index_groups=far
    )
    (copies,) = call(sum_kernel, [((ROWS, CHUNK // ROWS, WIDE), BF16)])(pieces)
    part = lax.all_to_all(copies, "space", 0, 0, axis_index_groups=far)
    whole = lax.all_gather(part.reshape(CHUNK, WIDE), "space", axis_index_groups=near)
    (weight_grad,) = call(scale_kernel, [((DEEP, C), F32)], leave=(0,))(whole.reshape(COLS * CHUNK, WIDE))
    return (out.reshape(1, 1, C, CELLS), weight_grad.reshape(1, TAPS, C, C))


def solution(mesh):
    return jax.shard_map(
        body,
        mesh=mesh,
        in_specs=(
            P("pipe", "space", None, None),
            P("space", None, None),
            P("pipe", None, None, None),
            P("space"),
        ),
        out_specs=(P("pipe", "space", None, None), P("pipe", None, None, None)),
        check_vma=False,
    )
```

```python
import functools

import jax
import jax.numpy as jnp
from jax import lax
from jax.experimental import pallas as pl
from jax.experimental.pallas import tpu as pltpu
from jax.sharding import PartitionSpec as P

C = 96
CELLS = 512
COLS = 8
ROWS = 16
SECTIONS = 4
TAPS = 27
DEEP = TAPS * C
WIDE = 128
CODE = 8
CHUNK = 256
VMEM_BYTES = 32 * 1024 * 1024
F32 = jnp.float32
BF16 = jnp.bfloat16


def call(kernel, outs, scratch=(), leave=(), bring=True):
    shapes = [
        jax.ShapeDtypeStruct(shape, dtype) if n in leave else pltpu.VMEM(shape, dtype)
        for n, (shape, dtype) in enumerate(outs)
    ]

    def run(*args):
        inner = pl.pallas_call(
            kernel,
            out_shape=shapes,
            in_specs=[
                pl.BlockSpec(memory_space=pltpu.SMEM if arg.dtype == jnp.int32 else pltpu.VMEM)
                for arg in args
            ],
            out_specs=[pl.BlockSpec(memory_space=pltpu.VMEM)] * len(shapes),
            scratch_shapes=[pltpu.VMEM(shape, dtype) for shape, dtype in scratch],
            compiler_params=pltpu.CompilerParams(vmem_limit_bytes=VMEM_BYTES),
        )
        return inner(
            *[
                arg if arg.dtype == jnp.int32 or not bring
                else pltpu.with_memory_space_constraint(arg, pltpu.VMEM)
                for arg in args
            ]
        )

    return run


def lane(row, count=1):
    start = row * WIDE
    if not isinstance(start, int):
        start = pl.multiple_of(start, WIDE)
    return pl.ds(start, count * WIDE)


def turn(value, by):
    by = by % value.shape[1]
    return pltpu.roll(value, by, 1) if by else value


def shifted_rows(base_ref, row, tile, low=None, high=None):
    level = lax.broadcasted_iota(jnp.int32, (C, WIDE), 1) % 8
    for oy, source in ((-1, low), (0, None), (1, high)):
        source = tile if source is None else source
        for oz in (-1, 0, 1):
            if oz == 0:
                moved = turn(source, -8 * oy)
            elif oz > 0:
                moved = jnp.where(level < 7, turn(source, -8 * oy - 1), turn(source, -8 * oy + 7))
            else:
                moved = jnp.where(level > 0, turn(source, -8 * oy + 1), turn(source, -8 * oy - 7))
            base_ref[3 * (oy + 1) + oz + 1, :, lane(row)] = moved


def make_cols(cols_ref, base_ref, mask_ref, base_row, mask_row, at=0):
    for ox in (-1, 0, 1):
        for j in range(9):
            tap = 9 * (ox + 1) + j
            tile = base_ref[j, :, lane(base_row + ox, 2)].reshape(C // 16, 16, 2 * WIDE)
            kept = tile * mask_ref[tap, :, lane(mask_row, 2)][None]
            cols_ref[C * tap : C * tap + C, lane(at, 2)] = kept.reshape(C, 2 * WIDE)


def product(weight, cols):
    return lax.dot_general(
        weight, cols, (((1,), (0,)), ((), ())), preferred_element_type=F32
    )


def weight_kernel(w_ref, fwd_ref, bwd_ref):
    for q in range(TAPS):
        fwd_ref[:, C * q : C * q + C] = w_ref[q].T
        bwd_ref[:, C * q : C * q + C] = w_ref[TAPS - 1 - q]


def code_of(height_ref, shape):
    return jnp.full(shape, (height_ref[0] + CODE).astype(F32), F32)


def rows_kernel(x_ref, top_ref, height_ref, up_ref, down_ref, x_out, top_out):
    lowest = lax.axis_index("pipe") == 0
    code = code_of(height_ref, (16, 3 * WIDE)).astype(BF16)
    spare = jnp.zeros((C, 64), BF16)
    up_ref[C:, :] = code
    down_ref[C:, :] = code
    up_ref[:C, :WIDE] = x_ref[:, 384:512]
    down_ref[:C, :WIDE] = x_ref[:, 0:128]
    x_out[...] = x_ref[...]
    top_out[...] = top_ref[...]

    @pl.when(lowest)
    def _():
        up_ref[:C, WIDE:] = top_ref[:, 256:512]
        down_ref[:C, WIDE:] = top_ref[:, 0:256]

    @pl.when(jnp.logical_not(lowest))
    def _():
        up_ref[:C, WIDE:] = jnp.concatenate([x_ref[:, 192:384], spare], 1)
        down_ref[:C, WIDE:] = jnp.concatenate([x_ref[:, 128:320], spare], 1)


def x_layer(x_ref, before_ref, after_ref, row):
    if row < 5:
        at = 64 * (row - 3) if row >= 3 else WIDE + 64 * row
        return before_ref[:C, at : at + 64]
    if row < 13:
        return x_ref[:, 64 * (row - 5) : 64 * (row - 5) + 64]
    at = 64 * (row - 13) if row < 15 else WIDE + 64 * (row - 15)
    return after_ref[:C, at : at + 64]


def top_layer(top_ref, before_ref, after_ref, row):
    if row < 5:
        return before_ref[:C, WIDE + 64 * (row - 1) : WIDE + 64 * row]
    if row < 13:
        return top_ref[:, 64 * (row - 5) : 64 * (row - 5) + 64]
    return after_ref[:C, WIDE + 64 * (row - 13) : WIDE + 64 * (row - 12)]


def join(parts):
    return jnp.concatenate(parts, 1)


def cols_kernel(x_ref, top_ref, height_ref, before_ref, after_ref, right_ref, left_ref):
    lowest = lax.axis_index("pipe") == 0
    codes = join(
        [before_ref[C:, :WIDE], code_of(height_ref, (16, WIDE)).astype(BF16), after_ref[C:, :WIDE]]
    )
    for out, start, fifth in ((right_ref, 32, 24), (left_ref, 0, 32)):

        def piece(layer, start=start):
            return layer[:, start : start + 32]

        out[C:, : 3 * WIDE] = codes
        out[C:, 3 * WIDE :] = jnp.zeros((16, 4 * WIDE), BF16)
        for four in range(3):
            rows = range(3 + 4 * four, 7 + 4 * four)
            out[:C, lane(four)] = join(
                [piece(x_layer(x_ref, before_ref, after_ref, row)) for row in rows]
            )

        @pl.when(lowest)
        def _(out=out, piece=piece):
            for four in range(4):
                rows = range(1 + 4 * four, 5 + 4 * four)
                out[:C, lane(3 + four)] = join(
                    [piece(top_layer(top_ref, before_ref, after_ref, row)) for row in rows]
                )

        @pl.when(jnp.logical_not(lowest))
        def _(out=out, piece=piece, fifth=fifth):
            outer = [
                piece(x_layer(x_ref, before_ref, after_ref, row)) for row in (0, 1, 2, 15, 16, 17)
            ]
            out[:C, lane(3)] = join(outer[:4])
            out[:C, lane(4)] = join(outer[4:] + [jnp.zeros((C, 64), BF16)])
            more = [
                x_layer(x_ref, before_ref, after_ref, row)[:, fifth : fifth + 8]
                for row in range(18)
            ]
            out[:C, lane(5)] = join(more[:16])
            out[:C, lane(6)] = join(more[16:] + [jnp.zeros((C, 112), BF16)])


def x_side(side_ref, row):
    if 3 <= row < 15:
        at = 32 * (row - 3)
    else:
        at = 3 * WIDE + 32 * (row if row < 3 else row - 12)
    return side_ref[:C, at : at + 32]


def top_side(side_ref, row):
    return side_ref[:C, 3 * WIDE + 32 * (row - 1) : 3 * WIDE + 32 * row]


def halo_kernel(before_ref, after_ref, left_ref, right_ref, halo_ref):
    @pl.when(lax.axis_index("pipe") == 0)
    def _():
        for n, row in enumerate((1, 2, 3, 4, 13, 14, 15, 16)):
            middle = top_layer(None, before_ref, after_ref, row)
            halo_ref[:, lane(n)] = join([top_side(left_ref, row), middle, top_side(right_ref, row)])
        for pair in range(4):
            first, second = 5 + 2 * pair, 6 + 2 * pair
            halo_ref[:, lane(8 + pair)] = join(
                [
                    top_side(left_ref, first),
                    top_side(right_ref, first),
                    top_side(left_ref, second),
                    top_side(right_ref, second),
                ]
            )


def forward_kernel(
    x_ref, height_ref, before_ref, after_ref, left_ref, right_ref, fwd_ref,
    slope_ref, mask_ref, rows_ref,
    base_ref, cols_ref, code_ref, pre_ref,
):
    where = lax.broadcasted_iota(jnp.int32, (8, WIDE), 1)
    middle = (
        before_ref[C : C + 8, :WIDE].astype(F32),
        code_of(height_ref, (8, WIDE)),
        after_ref[C : C + 8, :WIDE].astype(F32),
    )
    codes = []
    for n in range(3):
        left = left_ref[C : C + 8, lane(n)].astype(F32)
        right = right_ref[C : C + 8, lane(n)].astype(F32)
        codes.append(jnp.where(where < 32, left, jnp.where(where < 96, middle[n], right)))
    for row in range(18):
        code_ref[:, lane(row)] = codes[0 if row < 5 else 1 if row < 13 else 2]
    for row in range(18):
        tile = join(
            [
                x_side(left_ref, row),
                x_layer(x_ref, before_ref, after_ref, row),
                x_side(right_ref, row),
            ]
        )
        if 4 <= row < 14:
            rows_ref[:, lane(row - 4)] = tile
        at = 5 * WIDE + 8 * row
        low = join([tile[:, :120], left_ref[:C, at : at + 8]])
        high = join([right_ref[:C, at : at + 8], tile[:, 8:]])
        shifted_rows(base_ref, row, tile, low, high)

    level = lax.broadcasted_iota(jnp.int32, (8, WIDE), 1) % 8
    rise_of = {
        -1: jnp.where(level == 0, -1.0, 0.0),
        0: jnp.zeros((8, WIDE), F32),
        1: jnp.where(level == 7, 1.0, 0.0),
    }

    for rows in ((0, 1, 2), (3,), (4,), (5, 6, 7, 8, 9, 10), (11,), (12,), (13, 14, 15)):
        here = code_ref[:, lane(rows[0] + 1)]
        for ox in (-1, 0, 1):
            near = code_ref[:, lane(rows[0] + 1 + ox)]
            for oy in (-1, 0, 1):
                if oy < 0:
                    source = jnp.where(where >= 120, near[:, 0:1], near)
                elif oy > 0:
                    source = jnp.where(where < 8, near[:, 127:128], near)
                else:
                    source = near
                rise = turn(source, -8 * oy) - here
                for oz in (-1, 0, 1):
                    keep = jnp.where(rise == rise_of[oz], 1.0, 0.0)
                    keep = jnp.concatenate([keep, keep], 0).astype(BF16)
                    tap = 9 * (ox + 1) + 3 * (oy + 1) + oz + 1
                    for row in rows:
                        mask_ref[tap, :, lane(row)] = keep

    def forward(pair, carry):
        make_cols(cols_ref, base_ref, mask_ref, 2 * pair + 1, 2 * pair)
        pre_ref[:, lane(2 * pair, 2)] = product(fwd_ref[...], cols_ref[...])
        return carry

    lax.fori_loop(0, 8, forward, 0)
    for row in range(16):
        pre = pre_ref[:, lane(row)]
        sigma = 1.0 / (1.0 + jnp.exp(-pre))
        slope_ref[:, lane(row)] = sigma * (1.0 + pre * (1.0 - sigma))


def top_kernel(
    own_ref, halo_ref, slope_ref, mask_ref, bwd_ref,
    result_ref, grad_ref, out_ref,
    base_ref, cols_ref, top_ref,
):
    active = lax.axis_index("pipe") == SECTIONS - 1
    for row in range(1, 17):
        if row < 5:
            tile = halo_ref[:, lane(row - 1)]
        elif row < 13:
            at = 8 * WIDE + 64 * (row - 5)
            middle = own_ref[:, 64 * (row - 5) : 64 * (row - 5) + 64]
            tile = join([halo_ref[:, at : at + 32], middle, halo_ref[:, at + 32 : at + 64]])
        else:
            tile = halo_ref[:, lane(row - 9)]
        top_ref[:, lane(row - 1)] = jnp.where(active, tile, jnp.zeros_like(tile))

    def store(pair, value):
        result_ref[:, lane(2 * pair, 2)] = value

    step_rows(top_ref, slope_ref, mask_ref, bwd_ref, base_ref, cols_ref, store, 16, 1)
    for row in range(8):
        grad_ref[:, lane(row)] = base_ref[4, :, lane(row + 4)]
        out_ref[:, lane(row)] = result_ref[:, lane(row + 3)]


def step_rows(incoming_ref, slope_ref, mask_ref, bwd_ref, base_ref, cols_ref, store, count, first):
    for row in range(count):
        grad = (
            incoming_ref[:, lane(row)].astype(F32) * slope_ref[:, lane(row + first - 1)]
        ).astype(BF16)
        shifted_rows(base_ref, row, grad)

    def backward(pair, carry):
        make_cols(cols_ref, base_ref, mask_ref, 2 * pair + 1, 2 * pair + first)
        total = incoming_ref[:, lane(2 * pair + 1, 2)].astype(F32) + product(
            bwd_ref[...], cols_ref[...]
        )
        store(pair, total.astype(BF16))
        return carry

    lax.fori_loop(0, (count - 2) // 2, backward, 0)


def middle_kernel(
    count, first, incoming_ref, slope_ref, mask_ref, bwd_ref, grad_in, out_in,
    result_ref, grad_ref, out_ref, base_ref, cols_ref,
):
    def store(pair, value):
        result_ref[:, lane(2 * pair, 2)] = value

    step_rows(
        incoming_ref, slope_ref, mask_ref, bwd_ref, base_ref, cols_ref, store, count, first
    )
    for row in range(8):
        grad_ref[:, lane(row)] = grad_in[:, lane(row)] + base_ref[4, :, lane(row + 5 - first)]
        out_ref[:, lane(row)] = out_in[:, lane(row)] + result_ref[:, lane(row + 4 - first)]


def halves(first, second):
    where = lax.broadcasted_iota(jnp.int32, first.shape, 1)
    return jnp.where(where < 64, turn(first, -32), turn(second, 32))


def gather_kernel(x_ref, mask_ref, all_ref, base_ref):
    for row in range(10):
        shifted_rows(base_ref, row, x_ref[:, lane(row)])

    def one(pair, carry):
        for tap in range(TAPS):
            ox, j = tap // 9 - 1, tap % 9
            tiles = []
            for n in range(2):
                tile = base_ref[j, :, lane(2 * pair + 1 + n + ox)].reshape(C // 16, 16, WIDE)
                kept = tile * mask_ref[tap, :, lane(2 * pair + 4 + n)][None]
                tiles.append(kept.reshape(C, WIDE))
            all_ref[C * tap : C * tap + C, lane(pair)] = halves(*tiles)
        return carry

    lax.fori_loop(0, 4, one, 0)


def terms_kernel(incoming_ref, slope_ref, grad_in, all_ref, terms_ref):
    grads = []
    for row in range(8):
        grad = incoming_ref[:, lane(row + 1)].astype(F32) * slope_ref[:, lane(row + 4)]
        grads.append(grad_in[:, lane(row)] + grad.astype(BF16))
    grads = join([halves(grads[2 * pair], grads[2 * pair + 1]) for pair in range(4)])
    for four in range(7):
        parts = []
        for tap in range(4 * four, 4 * four + 4):
            if tap < TAPS:
                part = lax.dot_general(
                    all_ref[C * tap : C * tap + C, :], grads, (((1,), (1,)), ((), ())),
                    preferred_element_type=F32,
                ).astype(BF16)
            else:
                part = jnp.zeros((C, C), BF16)
            parts.append(part)
        first, second, third, fourth = parts
        at = 3 * C * four
        terms_ref[at : at + C, :] = jnp.concatenate([first, second[:, :32]], 1)
        terms_ref[at + C : at + 2 * C, :] = jnp.concatenate([second[:, 32:], third[:, :64]], 1)
        terms_ref[at + 2 * C : at + 3 * C, :] = jnp.concatenate([third[:, 64:], fourth], 1)
    terms_ref[21 * C :, :] = jnp.zeros((COLS * CHUNK - 21 * C, WIDE), BF16)


def last_kernel(
    incoming_ref, slope_ref, mask_ref, bwd_ref, out_in, out_ref, base_ref, cols_ref
):
    def store(pair, value):
        total = out_in[:, lane(2 * pair, 2)] + value
        out_ref[:, lane(pair)] = halves(total[:, :WIDE], total[:, WIDE:])

    step_rows(incoming_ref, slope_ref, mask_ref, bwd_ref, base_ref, cols_ref, store, 10, 4)


def sum_kernel(parts_ref, out_ref):
    total = parts_ref[0].astype(F32)
    for n in range(1, parts_ref.shape[0]):
        total = total + parts_ref[n].astype(F32)
    total = total.astype(BF16)
    if len(out_ref.shape) == 2:
        out_ref[...] = total
    else:
        for n in range(out_ref.shape[0]):
            out_ref[n] = total


def scale_kernel(whole_ref, out_ref):
    whole = whole_ref[...].astype(F32)
    scale = lax.rsqrt(jnp.sum(whole * whole) / (DEEP * C) + 1e-06)
    for four in range(7):
        at = 3 * C * four
        first, second, third = (
            whole_ref[at + n * C : at + n * C + C, :].astype(F32) * scale for n in range(3)
        )
        parts = (
            first[:, :96],
            jnp.concatenate([first[:, 96:], second[:, :64]], 1),
            jnp.concatenate([second[:, 64:], third[:, :32]], 1),
            third[:, 32:],
        )
        for n, tap in enumerate(range(4 * four, min(4 * four + 4, TAPS))):
            out_ref[C * tap : C * tap + C, :] = parts[n]


def groups(devices):
    rows = devices // (2 * ROWS)
    near = [[y * 32 + z * 2 + c for y in range(rows) for c in range(2)] for z in range(ROWS)]
    far = [[y * 32 + z * 2 + c for z in range(ROWS)] for y in range(rows) for c in range(2)]
    return near, far


def body(section_input, top_grad, conv_weight, brick_height):
    devices = lax.axis_size("space")
    both = ("space", "pipe")

    def between(by_row, by_col, sections):
        pairs = []
        for x in range(ROWS):
            for y in range(COLS):
                if 0 <= x + by_row < ROWS and 0 <= y + by_col < COLS:
                    source = x * COLS + y
                    target = (x + by_row) * COLS + y + by_col
                    for a, b in sections:
                        pairs.append((source * SECTIONS + a, target * SECTIONS + b))
        return pairs

    same = [(s, s) for s in range(SECTIONS)]
    x = section_input.reshape(C, CELLS)
    top = top_grad.reshape(C, CELLS)
    fwd, bwd = call(weight_kernel, [((C, DEEP), BF16)] * 2)(conv_weight[0])
    up, down, x, top = call(
        rows_kernel, [((C + 16, 3 * WIDE), BF16)] * 2 + [((C, CELLS), BF16)] * 2, bring=False
    )(x, top, brick_height)
    before = lax.ppermute(up, both, between(1, 0, same))
    after = lax.ppermute(down, both, between(-1, 0, same))
    before, after, fwd, bwd = lax.optimization_barrier((before, after, fwd, bwd))
    to_right, to_left = call(cols_kernel, [((C + 16, 7 * WIDE), BF16)] * 2)(
        x, top, brick_height, before, after
    )
    left = lax.ppermute(to_right, both, between(0, 1, same))
    right = lax.ppermute(to_left, both, between(0, -1, same))
    (halo,) = call(halo_kernel, [((C, 12 * WIDE), BF16)])(before, after, left, right)
    halo = lax.ppermute(halo, both, between(0, 0, [(0, SECTIONS - 1)]))

    core = ((C, 8 * WIDE), BF16)
    cols = ((DEEP, 2 * WIDE), BF16)
    slope, mask, x_rows = call(
        forward_kernel,
        [((C, 16 * WIDE), F32), ((TAPS, 16, 16 * WIDE), BF16), ((C, 10 * WIDE), BF16)],
        [((9, C, 18 * WIDE), BF16), cols, ((8, 18 * WIDE), F32), ((C, 16 * WIDE), F32)],
    )(x, brick_height, before, after, left, right, fwd)
    result, grad, out = call(
        top_kernel,
        [((C, 14 * WIDE), BF16), core, core],
        [((9, C, 16 * WIDE), BF16), cols, ((C, 16 * WIDE), BF16)],
    )(top, halo, slope, mask, bwd)
    incoming = lax.ppermute(result, both, between(0, 0, [(3, 2)]))
    result, grad, out = call(
        functools.partial(middle_kernel, 14, 2),
        [((C, 12 * WIDE), BF16), core, core],
        [((9, C, 14 * WIDE), BF16), cols],
    )(incoming, slope, mask, bwd, grad, out)
    incoming = lax.ppermute(result, both, between(0, 0, [(2, 1)]))
    result, grad, out = call(
        functools.partial(middle_kernel, 12, 3),
        [((C, 10 * WIDE), BF16), core, core],
        [((9, C, 12 * WIDE), BF16), cols],
    )(incoming, slope, mask, bwd, grad, out)
    incoming = lax.ppermute(result, both, between(0, 0, [(1, 0)]))
    x_rows, _ = lax.optimization_barrier((x_rows, result))
    (x_cols,) = call(gather_kernel, [((DEEP, CELLS), BF16)], [((9, C, 10 * WIDE), BF16)])(
        x_rows, mask
    )
    (terms,) = call(terms_kernel, [((COLS * CHUNK, WIDE), BF16)])(incoming, slope, grad, x_cols)

    near, far = groups(devices)
    parts = lax.all_to_all(
        terms.reshape(COLS, CHUNK, WIDE), "space", 0, 0, axis_index_groups=near
    )
    parts, out = lax.optimization_barrier((parts, out))
    (out,) = call(
        last_kernel, [((C, CELLS), BF16)], [((9, C, 10 * WIDE), BF16), cols], leave=(0,)
    )(incoming, slope, mask, bwd, out)
    (part,) = call(sum_kernel, [((CHUNK, WIDE), BF16)])(parts)
    pieces = lax.all_to_all(
        part.reshape(ROWS, CHUNK // ROWS, WIDE), "space", 0, 0, axis_index_groups=far
    )
    (copies,) = call(sum_kernel, [((ROWS, CHUNK // ROWS, WIDE), BF16)])(pieces)
    part = lax.all_to_all(copies, "space", 0, 0, axis_index_groups=far)
    whole = lax.all_gather(part.reshape(CHUNK, WIDE), "space", axis_index_groups=near)
    (weight_grad,) = call(scale_kernel, [((DEEP, C), F32)], leave=(0,))(whole.reshape(COLS * CHUNK, WIDE))
    return (out.reshape(1, 1, C, CELLS), weight_grad.reshape(1, TAPS, C, C))


def solution(mesh):
    return jax.shard_map(
        body,
        mesh=mesh,
        in_specs=(
            P("pipe", "space", None, None),
            P("space", None, None),
            P("pipe", None, None, None),
            P("space"),
        ),
        out_specs=(P("pipe", "space", None, None), P("pipe", None, None, None)),
        check_vma=False,
    )
```

```python
import functools

import jax
import jax.numpy as jnp
from jax import lax
from jax.experimental import pallas as pl
from jax.experimental.pallas import tpu as pltpu
from jax.sharding import PartitionSpec as P

C = 96
CELLS = 512
COLS = 8
ROWS = 16
SECTIONS = 4
TAPS = 27
DEEP = TAPS * C
WIDE = 128
CODE = 8
NEAR = 16
FAR = 8
CHUNK = 128
VMEM_BYTES = 32 * 1024 * 1024
F32 = jnp.float32
BF16 = jnp.bfloat16


def call(kernel, outs, scratch=(), leave=(), bring=True):
    shapes = [
        jax.ShapeDtypeStruct(shape, dtype) if n in leave else pltpu.VMEM(shape, dtype)
        for n, (shape, dtype) in enumerate(outs)
    ]

    def run(*args):
        inner = pl.pallas_call(
            kernel,
            out_shape=shapes,
            in_specs=[
                pl.BlockSpec(
                    memory_space=pltpu.SMEM if arg.dtype == jnp.int32
                    else pltpu.VMEM if bring else pl.ANY
                )
                for arg in args
            ],
            out_specs=[pl.BlockSpec(memory_space=pltpu.VMEM)] * len(shapes),
            scratch_shapes=[
                pltpu.VMEM(*item) if isinstance(item, tuple) else item for item in scratch
            ],
            compiler_params=pltpu.CompilerParams(vmem_limit_bytes=VMEM_BYTES),
        )
        return inner(
            *[
                arg if arg.dtype == jnp.int32
                else pltpu.with_memory_space_constraint(arg, pltpu.VMEM if bring else pltpu.HBM)
                for arg in args
            ]
        )

    return run


def lane(row, count=1):
    start = row * WIDE
    if not isinstance(start, int):
        start = pl.multiple_of(start, WIDE)
    return pl.ds(start, count * WIDE)


def turn(value, by):
    by = by % value.shape[1]
    return pltpu.roll(value, by, 1) if by else value


def shifted_rows(base_ref, row, tile, low=None, high=None):
    level = lax.broadcasted_iota(jnp.int32, (C, WIDE), 1) % 8
    for oy, source in ((-1, low), (0, None), (1, high)):
        source = tile if source is None else source
        for oz in (-1, 0, 1):
            if oz == 0:
                moved = turn(source, -8 * oy)
            elif oz > 0:
                moved = jnp.where(level < 7, turn(source, -8 * oy - 1), turn(source, -8 * oy + 7))
            else:
                moved = jnp.where(level > 0, turn(source, -8 * oy + 1), turn(source, -8 * oy - 7))
            base_ref[3 * (oy + 1) + oz + 1, :, lane(row)] = moved


def make_cols(cols_ref, base_ref, mask_ref, base_row, mask_row, at=0):
    for ox in (-1, 0, 1):
        for j in range(9):
            tap = 9 * (ox + 1) + j
            tile = base_ref[j, :, lane(base_row + ox, 2)].reshape(C // 16, 16, 2 * WIDE)
            kept = tile * mask_ref[tap, :, lane(mask_row, 2)][None]
            cols_ref[C * tap : C * tap + C, lane(at, 2)] = kept.reshape(C, 2 * WIDE)


def product(weight, cols):
    return lax.dot_general(
        weight, cols, (((1,), (0,)), ((), ())), preferred_element_type=F32
    )


def weight_kernel(w_ref, fwd_ref, bwd_ref):
    for q in range(TAPS):
        fwd_ref[:, C * q : C * q + C] = w_ref[q].T
        bwd_ref[:, C * q : C * q + C] = w_ref[TAPS - 1 - q]


def code_of(height_ref, shape):
    return jnp.full(shape, (height_ref[0] + CODE).astype(F32), F32)


def rows_kernel(x_hbm, top_hbm, height_ref, up_ref, down_ref, x_ref, top_ref, sems):
    x_copy = pltpu.make_async_copy(x_hbm, x_ref, sems.at[0])
    top_copy = pltpu.make_async_copy(top_hbm, top_ref, sems.at[1])
    x_copy.start()
    top_copy.start()
    x_copy.wait()
    top_copy.wait()
    lowest = lax.axis_index("pipe") == 0
    code = code_of(height_ref, (16, 3 * WIDE)).astype(BF16)
    spare = jnp.zeros((C, 64), BF16)
    up_ref[C:, :] = code
    down_ref[C:, :] = code
    up_ref[:C, :WIDE] = x_ref[:, 384:512]
    down_ref[:C, :WIDE] = x_ref[:, 0:128]

    @pl.when(lowest)
    def _():
        up_ref[:C, WIDE:] = top_ref[:, 256:512]
        down_ref[:C, WIDE:] = top_ref[:, 0:256]

    @pl.when(jnp.logical_not(lowest))
    def _():
        up_ref[:C, WIDE:] = jnp.concatenate([x_ref[:, 192:384], spare], 1)
        down_ref[:C, WIDE:] = jnp.concatenate([x_ref[:, 128:320], spare], 1)


def x_layer(x_ref, before_ref, after_ref, row):
    if row < 5:
        at = 64 * (row - 3) if row >= 3 else WIDE + 64 * row
        return before_ref[:C, at : at + 64]
    if row < 13:
        return x_ref[:, 64 * (row - 5) : 64 * (row - 5) + 64]
    at = 64 * (row - 13) if row < 15 else WIDE + 64 * (row - 15)
    return after_ref[:C, at : at + 64]


def top_layer(top_ref, before_ref, after_ref, row):
    if row < 5:
        return before_ref[:C, WIDE + 64 * (row - 1) : WIDE + 64 * row]
    if row < 13:
        return top_ref[:, 64 * (row - 5) : 64 * (row - 5) + 64]
    return after_ref[:C, WIDE + 64 * (row - 13) : WIDE + 64 * (row - 12)]


def join(parts):
    return jnp.concatenate(parts, 1)


def cols_kernel(x_ref, top_ref, height_ref, before_ref, after_ref, right_ref, left_ref):
    lowest = lax.axis_index("pipe") == 0
    codes = join(
        [before_ref[C:, :WIDE], code_of(height_ref, (16, WIDE)).astype(BF16), after_ref[C:, :WIDE]]
    )
    for out, start, fifth in ((right_ref, 32, 24), (left_ref, 0, 32)):

        def piece(layer, start=start):
            return layer[:, start : start + 32]

        out[C:, : 3 * WIDE] = codes
        out[C:, 3 * WIDE :] = jnp.zeros((16, 4 * WIDE), BF16)
        for four in range(3):
            rows = range(3 + 4 * four, 7 + 4 * four)
            out[:C, lane(four)] = join(
                [piece(x_layer(x_ref, before_ref, after_ref, row)) for row in rows]
            )

        @pl.when(lowest)
        def _(out=out, piece=piece):
            for four in range(4):
                rows = range(1 + 4 * four, 5 + 4 * four)
                out[:C, lane(3 + four)] = join(
                    [piece(top_layer(top_ref, before_ref, after_ref, row)) for row in rows]
                )

        @pl.when(jnp.logical_not(lowest))
        def _(out=out, piece=piece, fifth=fifth):
            outer = [
                piece(x_layer(x_ref, before_ref, after_ref, row)) for row in (0, 1, 2, 15, 16, 17)
            ]
            out[:C, lane(3)] = join(outer[:4])
            out[:C, lane(4)] = join(outer[4:] + [jnp.zeros((C, 64), BF16)])
            more = [
                x_layer(x_ref, before_ref, after_ref, row)[:, fifth : fifth + 8]
                for row in range(18)
            ]
            out[:C, lane(5)] = join(more[:16])
            out[:C, lane(6)] = join(more[16:] + [jnp.zeros((C, 112), BF16)])


def x_side(side_ref, row):
    if 3 <= row < 15:
        at = 32 * (row - 3)
    else:
        at = 3 * WIDE + 32 * (row if row < 3 else row - 12)
    return side_ref[:C, at : at + 32]


def top_side(side_ref, row):
    return side_ref[:C, 3 * WIDE + 32 * (row - 1) : 3 * WIDE + 32 * row]


def halo_kernel(before_ref, after_ref, left_ref, right_ref, halo_ref):
    @pl.when(lax.axis_index("pipe") == 0)
    def _():
        for n, row in enumerate((1, 2, 3, 4, 13, 14, 15, 16)):
            middle = top_layer(None, before_ref, after_ref, row)
            halo_ref[:, lane(n)] = join([top_side(left_ref, row), middle, top_side(right_ref, row)])
        for pair in range(4):
            first, second = 5 + 2 * pair, 6 + 2 * pair
            halo_ref[:, lane(8 + pair)] = join(
                [
                    top_side(left_ref, first),
                    top_side(right_ref, first),
                    top_side(left_ref, second),
                    top_side(right_ref, second),
                ]
            )


def forward_kernel(
    x_ref, height_ref, before_ref, after_ref, left_ref, right_ref, fwd_ref,
    slope_ref, mask_ref, rows_ref,
    base_ref, cols_ref, code_ref, pre_ref,
):
    where = lax.broadcasted_iota(jnp.int32, (8, WIDE), 1)
    middle = (
        before_ref[C : C + 8, :WIDE].astype(F32),
        code_of(height_ref, (8, WIDE)),
        after_ref[C : C + 8, :WIDE].astype(F32),
    )
    codes = []
    for n in range(3):
        left = left_ref[C : C + 8, lane(n)].astype(F32)
        right = right_ref[C : C + 8, lane(n)].astype(F32)
        codes.append(jnp.where(where < 32, left, jnp.where(where < 96, middle[n], right)))
    for row in range(18):
        code_ref[:, lane(row)] = codes[0 if row < 5 else 1 if row < 13 else 2]
    for row in range(18):
        tile = join(
            [
                x_side(left_ref, row),
                x_layer(x_ref, before_ref, after_ref, row),
                x_side(right_ref, row),
            ]
        )
        if 4 <= row < 14:
            rows_ref[:, lane(row - 4)] = tile
        at = 5 * WIDE + 8 * row
        low = join([tile[:, :120], left_ref[:C, at : at + 8]])
        high = join([right_ref[:C, at : at + 8], tile[:, 8:]])
        shifted_rows(base_ref, row, tile, low, high)

    level = lax.broadcasted_iota(jnp.int32, (8, WIDE), 1) % 8
    rise_of = {
        -1: jnp.where(level == 0, -1.0, 0.0),
        0: jnp.zeros((8, WIDE), F32),
        1: jnp.where(level == 7, 1.0, 0.0),
    }

    for rows in ((0, 1, 2), (3,), (4,), (5, 6, 7, 8, 9, 10), (11,), (12,), (13, 14, 15)):
        here = code_ref[:, lane(rows[0] + 1)]
        for ox in (-1, 0, 1):
            near = code_ref[:, lane(rows[0] + 1 + ox)]
            for oy in (-1, 0, 1):
                if oy < 0:
                    source = jnp.where(where >= 120, near[:, 0:1], near)
                elif oy > 0:
                    source = jnp.where(where < 8, near[:, 127:128], near)
                else:
                    source = near
                rise = turn(source, -8 * oy) - here
                for oz in (-1, 0, 1):
                    keep = jnp.where(rise == rise_of[oz], 1.0, 0.0)
                    keep = jnp.concatenate([keep, keep], 0).astype(BF16)
                    tap = 9 * (ox + 1) + 3 * (oy + 1) + oz + 1
                    for row in rows:
                        mask_ref[tap, :, lane(row)] = keep

    def forward(pair, carry):
        make_cols(cols_ref, base_ref, mask_ref, 2 * pair + 1, 2 * pair)
        pre_ref[:, lane(2 * pair, 2)] = product(fwd_ref[...], cols_ref[...])
        return carry

    lax.fori_loop(0, 8, forward, 0)
    for row in range(16):
        pre = pre_ref[:, lane(row)]
        sigma = 1.0 / (1.0 + jnp.exp(-pre))
        slope_ref[:, lane(row)] = sigma * (1.0 + pre * (1.0 - sigma))


def top_kernel(
    own_ref, halo_ref, slope_ref, mask_ref, bwd_ref,
    result_ref, grad_ref, out_ref,
    base_ref, cols_ref, top_ref,
):
    active = lax.axis_index("pipe") == SECTIONS - 1
    for row in range(1, 17):
        if row < 5:
            tile = halo_ref[:, lane(row - 1)]
        elif row < 13:
            at = 8 * WIDE + 64 * (row - 5)
            middle = own_ref[:, 64 * (row - 5) : 64 * (row - 5) + 64]
            tile = join([halo_ref[:, at : at + 32], middle, halo_ref[:, at + 32 : at + 64]])
        else:
            tile = halo_ref[:, lane(row - 9)]
        top_ref[:, lane(row - 1)] = jnp.where(active, tile, jnp.zeros_like(tile))

    def store(pair, value):
        result_ref[:, lane(2 * pair, 2)] = value

    step_rows(top_ref, slope_ref, mask_ref, bwd_ref, base_ref, cols_ref, store, 16, 1)
    for row in range(8):
        grad_ref[:, lane(row)] = base_ref[4, :, lane(row + 4)]
        out_ref[:, lane(row)] = result_ref[:, lane(row + 3)]


def step_rows(incoming_ref, slope_ref, mask_ref, bwd_ref, base_ref, cols_ref, store, count, first):
    for row in range(count):
        grad = (
            incoming_ref[:, lane(row)].astype(F32) * slope_ref[:, lane(row + first - 1)]
        ).astype(BF16)
        shifted_rows(base_ref, row, grad)

    def backward(pair, carry):
        make_cols(cols_ref, base_ref, mask_ref, 2 * pair + 1, 2 * pair + first)
        total = incoming_ref[:, lane(2 * pair + 1, 2)].astype(F32) + product(
            bwd_ref[...], cols_ref[...]
        )
        store(pair, total.astype(BF16))
        return carry

    lax.fori_loop(0, (count - 2) // 2, backward, 0)


def spread(packed_ref, width, row):
    spare = jnp.zeros((C, (WIDE - width) // 2), BF16)
    return join([spare, packed_ref[:, width * row : width * row + width], spare])


def middle_kernel(
    count, first, width_in, width_out, incoming_ref, slope_ref, mask_ref, bwd_ref, grad_in, out_in,
    result_ref, grad_ref, out_ref, base_ref, cols_ref, rows_ref, full_ref,
):
    for row in range(count):
        rows_ref[:, lane(row)] = (
            incoming_ref[:, lane(row)] if width_in == WIDE else spread(incoming_ref, width_in, row)
        )

    def store(pair, value):
        full_ref[:, lane(2 * pair, 2)] = value

    step_rows(rows_ref, slope_ref, mask_ref, bwd_ref, base_ref, cols_ref, store, count, first)
    skip = (WIDE - width_out) // 2
    rows = [full_ref[:, lane(row)] for row in range(count - 2)]
    packed = [row[:, skip : skip + width_out] for row in rows]
    spare = result_ref.shape[1] - width_out * (count - 2)
    result_ref[...] = join(packed + [jnp.zeros((C, spare), BF16)] if spare else packed)
    for row in range(8):
        grad_ref[:, lane(row)] = grad_in[:, lane(row)] + base_ref[4, :, lane(row + 5 - first)]
        out_ref[:, lane(row)] = out_in[:, lane(row)] + rows[row + 4 - first]


def halves(first, second):
    where = lax.broadcasted_iota(jnp.int32, first.shape, 1)
    return jnp.where(where < 64, turn(first, -32), turn(second, 32))


def gather_kernel(x_ref, mask_ref, all_ref, base_ref):
    for row in range(10):
        shifted_rows(base_ref, row, x_ref[:, lane(row)])

    def one(pair, carry):
        for tap in range(TAPS):
            ox, j = tap // 9 - 1, tap % 9
            tiles = []
            for n in range(2):
                tile = base_ref[j, :, lane(2 * pair + 1 + n + ox)].reshape(C // 16, 16, WIDE)
                kept = tile * mask_ref[tap, :, lane(2 * pair + 4 + n)][None]
                tiles.append(kept.reshape(C, WIDE))
            all_ref[C * tap : C * tap + C, lane(pair)] = halves(*tiles)
        return carry

    lax.fori_loop(0, 4, one, 0)


def terms_kernel(packed_ref, slope_ref, grad_in, all_ref, terms_ref, incoming_ref):
    for row in range(10):
        incoming_ref[:, lane(row)] = spread(packed_ref, 80, row)
    grads = []
    for row in range(8):
        grad = incoming_ref[:, lane(row + 1)].astype(F32) * slope_ref[:, lane(row + 4)]
        grads.append(grad_in[:, lane(row)] + grad.astype(BF16))
    grads = join([halves(grads[2 * pair], grads[2 * pair + 1]) for pair in range(4)])
    for four in range(7):
        parts = []
        for tap in range(4 * four, 4 * four + 4):
            if tap < TAPS:
                part = lax.dot_general(
                    all_ref[C * tap : C * tap + C, :], grads, (((1,), (1,)), ((), ())),
                    preferred_element_type=F32,
                ).astype(BF16)
            else:
                part = jnp.zeros((C, C), BF16)
            parts.append(part)
        first, second, third, fourth = parts
        at = 3 * C * four
        terms_ref[at : at + C, :] = jnp.concatenate([first, second[:, :32]], 1)
        terms_ref[at + C : at + 2 * C, :] = jnp.concatenate([second[:, 32:], third[:, :64]], 1)
        terms_ref[at + 2 * C : at + 3 * C, :] = jnp.concatenate([third[:, 64:], fourth], 1)
    terms_ref[21 * C :, :] = jnp.zeros((NEAR * CHUNK - 21 * C, WIDE), BF16)


def last_kernel(
    incoming_ref, slope_ref, mask_ref, bwd_ref, out_in, out_ref, base_ref, cols_ref
):
    def store(pair, value):
        total = out_in[:, lane(2 * pair, 2)] + value
        out_ref[:, lane(pair)] = halves(total[:, :WIDE], total[:, WIDE:])

    step_rows(incoming_ref, slope_ref, mask_ref, bwd_ref, base_ref, cols_ref, store, 10, 4)


def sum_kernel(parts_ref, out_ref):
    total = parts_ref[0].astype(F32)
    for n in range(1, parts_ref.shape[0]):
        total = total + parts_ref[n].astype(F32)
    total = total.astype(BF16)
    for n in range(out_ref.shape[0]):
        out_ref[n] = total


def scale_kernel(whole_ref, out_ref):
    whole = whole_ref[...].astype(F32)
    scale = lax.rsqrt(jnp.sum(whole * whole) / (DEEP * C) + 1e-06)
    for four in range(7):
        at = 3 * C * four
        first, second, third = (
            whole_ref[at + n * C : at + n * C + C, :].astype(F32) * scale for n in range(3)
        )
        parts = (
            first[:, :96],
            jnp.concatenate([first[:, 96:], second[:, :64]], 1),
            jnp.concatenate([second[:, 64:], third[:, :32]], 1),
            third[:, 32:],
        )
        for n, tap in enumerate(range(4 * four, min(4 * four + 4, TAPS))):
            out_ref[C * tap : C * tap + C, :] = parts[n]


def groups():
    def device(y, high, low, core):
        return y * 32 + (2 * high + low) * 2 + core

    kinds = [(y, low, core) for y in range(4) for low in range(2) for core in range(2)]
    near = [[device(y, high, low, core) for y, low, core in kinds] for high in range(FAR)]
    far = [[device(y, high, low, core) for high in range(FAR)] for y, low, core in kinds]
    return near, far


def body(section_input, top_grad, conv_weight, brick_height):
    both = ("space", "pipe")

    def between(by_row, by_col, sections):
        pairs = []
        for x in range(ROWS):
            for y in range(COLS):
                if 0 <= x + by_row < ROWS and 0 <= y + by_col < COLS:
                    source = x * COLS + y
                    target = (x + by_row) * COLS + y + by_col
                    for a, b in sections:
                        pairs.append((source * SECTIONS + a, target * SECTIONS + b))
        return pairs

    same = [(s, s) for s in range(SECTIONS)]
    x = section_input.reshape(C, CELLS)
    top = top_grad.reshape(C, CELLS)
    fwd, bwd = call(weight_kernel, [((C, DEEP), BF16)] * 2)(conv_weight[0])
    up, down, x, top = call(
        rows_kernel,
        [((C + 16, 3 * WIDE), BF16)] * 2 + [((C, CELLS), BF16)] * 2,
        [pltpu.SemaphoreType.DMA((2,))],
        bring=False,
    )(x, top, brick_height)
    before = lax.ppermute(up, both, between(1, 0, same))
    after = lax.ppermute(down, both, between(-1, 0, same))
    before, after, fwd, bwd = lax.optimization_barrier((before, after, fwd, bwd))
    to_right, to_left = call(cols_kernel, [((C + 16, 7 * WIDE), BF16)] * 2)(
        x, top, brick_height, before, after
    )
    left = lax.ppermute(to_right, both, between(0, 1, same))
    right = lax.ppermute(to_left, both, between(0, -1, same))
    (halo,) = call(halo_kernel, [((C, 12 * WIDE), BF16)])(before, after, left, right)
    halo = lax.ppermute(halo, both, between(0, 0, [(0, SECTIONS - 1)]))

    core = ((C, 8 * WIDE), BF16)
    cols = ((DEEP, 2 * WIDE), BF16)
    slope, mask, x_rows = call(
        forward_kernel,
        [((C, 16 * WIDE), F32), ((TAPS, 16, 16 * WIDE), BF16), ((C, 10 * WIDE), BF16)],
        [((9, C, 18 * WIDE), BF16), cols, ((8, 18 * WIDE), F32), ((C, 16 * WIDE), F32)],
    )(x, brick_height, before, after, left, right, fwd)
    result, grad, out = call(
        top_kernel,
        [((C, 14 * WIDE), BF16), core, core],
        [((9, C, 16 * WIDE), BF16), cols, ((C, 16 * WIDE), BF16)],
    )(top, halo, slope, mask, bwd)
    incoming = lax.ppermute(result, both, between(0, 0, [(3, 2)]))
    result, grad, out = call(
        functools.partial(middle_kernel, 14, 2, WIDE, 96),
        [((C, 12 * 96), BF16), core, core],
        [((9, C, 14 * WIDE), BF16), cols, ((C, 14 * WIDE), BF16), ((C, 12 * WIDE), BF16)],
    )(incoming, slope, mask, bwd, grad, out)
    incoming = lax.ppermute(result, both, between(0, 0, [(2, 1)]))
    result, grad, out = call(
        functools.partial(middle_kernel, 12, 3, 96, 80),
        [((C, 7 * WIDE), BF16), core, core],
        [((9, C, 12 * WIDE), BF16), cols, ((C, 12 * WIDE), BF16), ((C, 10 * WIDE), BF16)],
    )(incoming, slope, mask, bwd, grad, out)
    incoming = lax.ppermute(result, both, between(0, 0, [(1, 0)]))
    x_rows, _ = lax.optimization_barrier((x_rows, result))
    (x_cols,) = call(gather_kernel, [((DEEP, CELLS), BF16)], [((9, C, 10 * WIDE), BF16)])(
        x_rows, mask
    )
    terms, incoming = call(
        terms_kernel, [((NEAR * CHUNK, WIDE), BF16), ((C, 10 * WIDE), BF16)]
    )(incoming, slope, grad, x_cols)

    near, far = groups()
    parts = lax.all_to_all(
        terms.reshape(NEAR, CHUNK, WIDE), "space", 0, 0, axis_index_groups=near
    )
    parts, out = lax.optimization_barrier((parts, out))
    (out,) = call(
        last_kernel, [((C, CELLS), BF16)], [((9, C, 10 * WIDE), BF16), cols], leave=(0,)
    )(incoming, slope, mask, bwd, out)
    (copies,) = call(sum_kernel, [((FAR, CHUNK, WIDE), BF16)])(parts)
    parts = lax.all_to_all(copies, "space", 0, 0, axis_index_groups=far)
    (copies,) = call(sum_kernel, [((NEAR, CHUNK, WIDE), BF16)])(parts)
    whole = lax.all_to_all(copies, "space", 0, 0, axis_index_groups=near)
    (weight_grad,) = call(scale_kernel, [((DEEP, C), F32)], leave=(0,))(
        whole.reshape(NEAR * CHUNK, WIDE)
    )
    return (out.reshape(1, 1, C, CELLS), weight_grad.reshape(1, TAPS, C, C))


def solution(mesh):
    return jax.shard_map(
        body,
        mesh=mesh,
        in_specs=(
            P("pipe", "space", None, None),
            P("space", None, None),
            P("pipe", None, None, None),
            P("space"),
        ),
        out_specs=(P("pipe", "space", None, None), P("pipe", None, None, None)),
        check_vma=False,
    )
```

```python
import functools

import jax
import jax.numpy as jnp
from jax import lax
from jax.experimental import pallas as pl
from jax.experimental.pallas import tpu as pltpu
from jax.sharding import PartitionSpec as P

C = 96
CELLS = 512
COLS = 8
ROWS = 16
SECTIONS = 4
TAPS = 27
DEEP = TAPS * C
WIDE = 128
CODE = 8
NEAR = 16
FAR = 8
CHUNK = 128
VMEM_BYTES = 32 * 1024 * 1024
F32 = jnp.float32
BF16 = jnp.bfloat16


def call(kernel, outs, scratch=(), leave=(), bring=True):
    shapes = [
        jax.ShapeDtypeStruct(shape, dtype) if n in leave else pltpu.VMEM(shape, dtype)
        for n, (shape, dtype) in enumerate(outs)
    ]

    def run(*args):
        inner = pl.pallas_call(
            kernel,
            out_shape=shapes,
            in_specs=[
                pl.BlockSpec(
                    memory_space=pltpu.SMEM if arg.dtype == jnp.int32
                    else pltpu.VMEM if bring else pl.ANY
                )
                for arg in args
            ],
            out_specs=[pl.BlockSpec(memory_space=pltpu.VMEM)] * len(shapes),
            scratch_shapes=[
                pltpu.VMEM(*item) if isinstance(item, tuple) else item for item in scratch
            ],
            compiler_params=pltpu.CompilerParams(vmem_limit_bytes=VMEM_BYTES),
        )
        return inner(
            *[
                arg if arg.dtype == jnp.int32
                else pltpu.with_memory_space_constraint(arg, pltpu.VMEM if bring else pltpu.HBM)
                for arg in args
            ]
        )

    return run


def lane(row, count=1):
    start = row * WIDE
    if not isinstance(start, int):
        start = pl.multiple_of(start, WIDE)
    return pl.ds(start, count * WIDE)


def turn(value, by):
    by = by % value.shape[1]
    return pltpu.roll(value, by, 1) if by else value


def shifted_rows(base_ref, row, tile, low=None, high=None):
    level = lax.broadcasted_iota(jnp.int32, (C, WIDE), 1) % 8
    for oy, source in ((-1, low), (0, None), (1, high)):
        source = tile if source is None else source
        for oz in (-1, 0, 1):
            if oz == 0:
                moved = turn(source, -8 * oy)
            elif oz > 0:
                moved = jnp.where(level < 7, turn(source, -8 * oy - 1), turn(source, -8 * oy + 7))
            else:
                moved = jnp.where(level > 0, turn(source, -8 * oy + 1), turn(source, -8 * oy - 7))
            base_ref[3 * (oy + 1) + oz + 1, :, lane(row)] = moved


def make_cols(cols_ref, base_ref, mask_ref, base_row, mask_row, at=0):
    for ox in (-1, 0, 1):
        for j in range(9):
            tap = 9 * (ox + 1) + j
            tile = base_ref[j, :, lane(base_row + ox, 2)].reshape(C // 16, 16, 2 * WIDE)
            kept = tile * mask_ref[tap, :, lane(mask_row, 2)][None]
            cols_ref[C * tap : C * tap + C, lane(at, 2)] = kept.reshape(C, 2 * WIDE)


def product(weight, cols):
    return lax.dot_general(
        weight, cols, (((1,), (0,)), ((), ())), preferred_element_type=F32
    )


def weight_kernel(w_ref, fwd_ref, bwd_ref):
    for q in range(TAPS):
        fwd_ref[:, C * q : C * q + C] = w_ref[q].T
        bwd_ref[:, C * q : C * q + C] = w_ref[TAPS - 1 - q]


OUTER = (1, 2, 3, 4, 13, 14, 15, 16)


def code_of(height_ref, shape):
    return jnp.full(shape, (height_ref[0] + CODE).astype(F32), F32)


def rows_kernel(x_hbm, top_hbm, height_ref, up_ref, down_ref, x_ref, top_ref, sems):
    x_copy = pltpu.make_async_copy(x_hbm, x_ref, sems.at[0])
    top_copy = pltpu.make_async_copy(top_hbm, top_ref, sems.at[1])
    x_copy.start()
    top_copy.start()
    x_copy.wait()
    top_copy.wait()
    lowest = lax.axis_index("pipe") == 0
    code = code_of(height_ref, (16, 3 * WIDE)).astype(BF16)
    spare = jnp.zeros((C, 64), BF16)
    up_ref[C:, :] = code
    down_ref[C:, :] = code
    up_ref[:C, :WIDE] = x_ref[:, 384:512]
    down_ref[:C, :WIDE] = x_ref[:, 0:128]

    @pl.when(lowest)
    def _():
        up_ref[:C, WIDE:] = top_ref[:, 256:512]
        down_ref[:C, WIDE:] = top_ref[:, 0:256]

    @pl.when(jnp.logical_not(lowest))
    def _():
        up_ref[:C, WIDE:] = jnp.concatenate([x_ref[:, 192:384], spare], 1)
        down_ref[:C, WIDE:] = jnp.concatenate([x_ref[:, 128:320], spare], 1)


def x_layer(x_ref, before_ref, after_ref, row):
    if row < 5:
        at = 64 * (row - 3) if row >= 3 else WIDE + 64 * row
        return before_ref[:C, at : at + 64]
    if row < 13:
        return x_ref[:, 64 * (row - 5) : 64 * (row - 5) + 64]
    at = 64 * (row - 13) if row < 15 else WIDE + 64 * (row - 15)
    return after_ref[:C, at : at + 64]


def top_layer(before_ref, after_ref, row):
    if row < 5:
        return before_ref[:C, WIDE + 64 * (row - 1) : WIDE + 64 * row]
    return after_ref[:C, WIDE + 64 * (row - 13) : WIDE + 64 * (row - 12)]


def join(parts):
    return jnp.concatenate(parts, 1)


def cols_kernel(x_ref, top_ref, height_ref, before_ref, after_ref, right_ref, left_ref):
    lowest = lax.axis_index("pipe") == 0
    codes = join(
        [before_ref[C:, :WIDE], code_of(height_ref, (16, WIDE)).astype(BF16), after_ref[C:, :WIDE]]
    )
    for out, start, fifth in ((right_ref, 32, 24), (left_ref, 0, 32)):

        def piece(layer, start=start):
            return layer[:, start : start + 32]

        out[C:, : 3 * WIDE] = codes
        out[C:, 3 * WIDE :] = jnp.zeros((16, 5 * WIDE), BF16)
        for four in range(3):
            rows = range(3 + 4 * four, 7 + 4 * four)
            out[:C, lane(four)] = join(
                [piece(x_layer(x_ref, before_ref, after_ref, row)) for row in rows]
            )

        @pl.when(lowest)
        def _(out=out, piece=piece):
            tops = [piece(top_layer(before_ref, after_ref, row)) for row in OUTER]
            out[:C, lane(3)] = join(tops[:4])
            out[:C, lane(4)] = join(tops[4:])
            out[:C, lane(5, 3)] = jnp.zeros((C, 3 * WIDE), BF16)

        @pl.when(jnp.logical_not(lowest))
        def _(out=out, piece=piece, fifth=fifth):
            outer = [
                piece(x_layer(x_ref, before_ref, after_ref, row)) for row in (0, 1, 2, 15, 16, 17)
            ]
            more = [
                x_layer(x_ref, before_ref, after_ref, row)[:, fifth : fifth + 8]
                for row in range(18)
            ]
            tops = [piece(top_ref[:, 64 * n : 64 * n + 64]) for n in range(8)]
            out[:C, lane(3)] = join(outer[:4])
            out[:C, lane(4)] = join(outer[4:] + more[:8])
            out[:C, lane(5)] = join(more[8:] + [jnp.zeros((C, 48), BF16)])
            out[:C, lane(6)] = join(tops[:4])
            out[:C, lane(7)] = join(tops[4:])


def x_side(side_ref, row):
    if 3 <= row < 15:
        at = 32 * (row - 3)
    else:
        at = 3 * WIDE + 32 * (row if row < 3 else row - 12)
    return side_ref[:C, at : at + 32]


def halo_kernel(before_ref, after_ref, left_ref, right_ref, halo_ref):
    @pl.when(lax.axis_index("pipe") == 0)
    def _():
        for n, row in enumerate(OUTER):
            at = 3 * WIDE + 32 * n
            middle = top_layer(before_ref, after_ref, row)
            sides = left_ref[:C, at : at + 32], right_ref[:C, at : at + 32]
            halo_ref[:, lane(n)] = join([sides[0], middle, sides[1]])


def forward_kernel(
    x_ref, height_ref, before_ref, after_ref, left_ref, right_ref, fwd_ref,
    slope_ref, mask_ref, rows_ref,
    base_ref, cols_ref, code_ref, pre_ref,
):
    where = lax.broadcasted_iota(jnp.int32, (8, WIDE), 1)
    middle = (
        before_ref[C : C + 8, :WIDE].astype(F32),
        code_of(height_ref, (8, WIDE)),
        after_ref[C : C + 8, :WIDE].astype(F32),
    )
    codes = []
    for n in range(3):
        left = left_ref[C : C + 8, lane(n)].astype(F32)
        right = right_ref[C : C + 8, lane(n)].astype(F32)
        codes.append(jnp.where(where < 32, left, jnp.where(where < 96, middle[n], right)))
    for row in range(18):
        code_ref[:, lane(row)] = codes[0 if row < 5 else 1 if row < 13 else 2]
    for row in range(18):
        tile = join(
            [
                x_side(left_ref, row),
                x_layer(x_ref, before_ref, after_ref, row),
                x_side(right_ref, row),
            ]
        )
        if 4 <= row < 14:
            rows_ref[:, lane(row - 4)] = tile
        at = 4 * WIDE + 64 + 8 * row
        low = join([tile[:, :120], left_ref[:C, at : at + 8]])
        high = join([right_ref[:C, at : at + 8], tile[:, 8:]])
        shifted_rows(base_ref, row, tile, low, high)

    level = lax.broadcasted_iota(jnp.int32, (8, WIDE), 1) % 8
    rise_of = {
        -1: jnp.where(level == 0, -1.0, 0.0),
        0: jnp.zeros((8, WIDE), F32),
        1: jnp.where(level == 7, 1.0, 0.0),
    }

    for rows in ((0, 1, 2), (3,), (4,), (5, 6, 7, 8, 9, 10), (11,), (12,), (13, 14, 15)):
        here = code_ref[:, lane(rows[0] + 1)]
        for ox in (-1, 0, 1):
            near = code_ref[:, lane(rows[0] + 1 + ox)]
            for oy in (-1, 0, 1):
                if oy < 0:
                    source = jnp.where(where >= 120, near[:, 0:1], near)
                elif oy > 0:
                    source = jnp.where(where < 8, near[:, 127:128], near)
                else:
                    source = near
                rise = turn(source, -8 * oy) - here
                for oz in (-1, 0, 1):
                    keep = jnp.where(rise == rise_of[oz], 1.0, 0.0)
                    keep = jnp.concatenate([keep, keep], 0).astype(BF16)
                    tap = 9 * (ox + 1) + 3 * (oy + 1) + oz + 1
                    for row in rows:
                        mask_ref[tap, :, lane(row)] = keep

    def forward(pair, carry):
        make_cols(cols_ref, base_ref, mask_ref, 2 * pair + 1, 2 * pair)
        pre_ref[:, lane(2 * pair, 2)] = product(fwd_ref[...], cols_ref[...])
        return carry

    lax.fori_loop(0, 8, forward, 0)
    for row in range(16):
        pre = pre_ref[:, lane(row)]
        sigma = 1.0 / (1.0 + jnp.exp(-pre))
        slope_ref[:, lane(row)] = sigma * (1.0 + pre * (1.0 - sigma))


def top_row(top_ref, halo_ref, left_ref, right_ref, row):
    if 5 <= row < 13:
        at, side = 64 * (row - 5), 6 * WIDE + 32 * (row - 5)
        tile = join(
            [
                left_ref[:C, side : side + 32],
                top_ref[:, at : at + 64],
                right_ref[:C, side : side + 32],
            ]
        )
    else:
        tile = halo_ref[:, lane(OUTER.index(row))]
    return jnp.where(lax.axis_index("pipe") == SECTIONS - 1, tile, jnp.zeros_like(tile))


def step_rows(incoming_ref, slope_ref, mask_ref, bwd_ref, base_ref, cols_ref, store, count, first):
    for row in range(count):
        grad = (
            incoming_ref[:, lane(row)].astype(F32) * slope_ref[:, lane(row + first - 1)]
        ).astype(BF16)
        shifted_rows(base_ref, row, grad)

    def backward(pair, carry):
        make_cols(cols_ref, base_ref, mask_ref, 2 * pair + 1, 2 * pair + first)
        total = incoming_ref[:, lane(2 * pair + 1, 2)].astype(F32) + product(
            bwd_ref[...], cols_ref[...]
        )
        store(pair, total.astype(BF16))
        return carry

    lax.fori_loop(0, (count - 2) // 2, backward, 0)


def spread(packed_ref, width, row):
    spare = jnp.zeros((C, (WIDE - width) // 2), BF16)
    return join([spare, packed_ref[:, width * row : width * row + width], spare])


def pieces_row(pieces, row):
    for ref, first, count, width in pieces:
        if first <= row < first + count:
            if width == WIDE:
                return ref[:, lane(row - first)]
            return spread(ref, width, row - first)


def step_part(row_of, low, count, width, result_ref, slope_ref, mask_ref, bwd_ref, scratch):
    base_ref, cols_ref, rows_ref, full_ref = scratch
    for n in range(count + 2):
        rows_ref[:, lane(n)] = row_of(low - 1 + n)

    def store(pair, value):
        full_ref[:, lane(2 * pair, 2)] = value

    step_rows(
        rows_ref, slope_ref, mask_ref, bwd_ref, base_ref, cols_ref, store, count + 2, low - 1
    )
    skip = (WIDE - width) // 2
    packed = [full_ref[:, lane(n)][:, skip : skip + width] for n in range(count)]
    spare = result_ref.shape[1] - width * count
    result_ref[...] = join(packed + [jnp.zeros((C, spare), BF16)] if spare else packed)


def keep_own(row_of, result_of, slope_ref, grad_in, out_in, grad_ref, out_ref):
    for n in range(8):
        grad = (row_of(n + 5).astype(F32) * slope_ref[:, lane(n + 4)]).astype(BF16)
        out = result_of(n + 5)
        if grad_in is not None:
            grad, out = grad + grad_in[:, lane(n)], out + out_in[:, lane(n)]
        grad_ref[:, lane(n)] = grad
        out_ref[:, lane(n)] = out


def top_first_kernel(
    top_ref, halo_ref, left_ref, right_ref, slope_ref, mask_ref, bwd_ref, result_ref, *scratch
):
    def row_of(row):
        return top_row(top_ref, halo_ref, left_ref, right_ref, row)

    step_part(row_of, 2, 8, WIDE, result_ref, slope_ref, mask_ref, bwd_ref, scratch)


def top_second_kernel(
    top_ref, halo_ref, left_ref, right_ref, slope_ref, mask_ref, bwd_ref, earlier_ref,
    result_ref, grad_ref, out_ref, *scratch,
):
    def row_of(row):
        return top_row(top_ref, halo_ref, left_ref, right_ref, row)

    def result_of(row):
        return pieces_row(((earlier_ref, 2, 8, WIDE), (result_ref, 10, 6, WIDE)), row)

    step_part(row_of, 10, 6, WIDE, result_ref, slope_ref, mask_ref, bwd_ref, scratch)
    keep_own(row_of, result_of, slope_ref, None, None, grad_ref, out_ref)


def first_kernel(piece, low, count, width, piece_ref, slope_ref, mask_ref, bwd_ref, result_ref,
                 *scratch):
    def row_of(row):
        return pieces_row(((piece_ref,) + piece,), row)

    step_part(row_of, low, count, width, result_ref, slope_ref, mask_ref, bwd_ref, scratch)


def second_kernel(
    pieces, early, low, count, width,
    first_ref, second_ref, slope_ref, mask_ref, bwd_ref, earlier_ref, grad_in, out_in,
    result_ref, grad_ref, out_ref, *scratch,
):
    def row_of(row):
        return pieces_row(((first_ref,) + pieces[0], (second_ref,) + pieces[1]), row)

    def result_of(row):
        later = (result_ref, low, count, width)
        return pieces_row(((earlier_ref, early, low - early, width), later), row)

    step_part(row_of, low, count, width, result_ref, slope_ref, mask_ref, bwd_ref, scratch)
    keep_own(row_of, result_of, slope_ref, grad_in, out_in, grad_ref, out_ref)


def halves(first, second):
    where = lax.broadcasted_iota(jnp.int32, first.shape, 1)
    return jnp.where(where < 64, turn(first, -32), turn(second, 32))


def gather_kernel(x_ref, mask_ref, all_ref, base_ref):
    for row in range(10):
        shifted_rows(base_ref, row, x_ref[:, lane(row)])

    def one(pair, carry):
        for tap in range(TAPS):
            ox, j = tap // 9 - 1, tap % 9
            tiles = []
            for n in range(2):
                tile = base_ref[j, :, lane(2 * pair + 1 + n + ox)].reshape(C // 16, 16, WIDE)
                kept = tile * mask_ref[tap, :, lane(2 * pair + 4 + n)][None]
                tiles.append(kept.reshape(C, WIDE))
            all_ref[C * tap : C * tap + C, lane(pair)] = halves(*tiles)
        return carry

    lax.fori_loop(0, 4, one, 0)


def terms_kernel(
    first_ref, second_ref, slope_ref, grad_in, all_ref, terms_ref, incoming_ref
):
    for row in range(10):
        incoming_ref[:, lane(row)] = pieces_row(
            ((first_ref, 4, 4, 80), (second_ref, 8, 6, 80)), row + 4
        )
    grads = []
    for row in range(8):
        grad = incoming_ref[:, lane(row + 1)].astype(F32) * slope_ref[:, lane(row + 4)]
        grads.append(grad_in[:, lane(row)] + grad.astype(BF16))
    grads = join([halves(grads[2 * pair], grads[2 * pair + 1]) for pair in range(4)])
    for four in range(7):
        parts = []
        for tap in range(4 * four, 4 * four + 4):
            if tap < TAPS:
                part = lax.dot_general(
                    all_ref[C * tap : C * tap + C, :], grads, (((1,), (1,)), ((), ())),
                    preferred_element_type=F32,
                ).astype(BF16)
            else:
                part = jnp.zeros((C, C), BF16)
            parts.append(part)
        first, second, third, fourth = parts
        at = 3 * C * four
        terms_ref[at : at + C, :] = jnp.concatenate([first, second[:, :32]], 1)
        terms_ref[at + C : at + 2 * C, :] = jnp.concatenate([second[:, 32:], third[:, :64]], 1)
        terms_ref[at + 2 * C : at + 3 * C, :] = jnp.concatenate([third[:, 64:], fourth], 1)
    terms_ref[21 * C :, :] = jnp.zeros((NEAR * CHUNK - 21 * C, WIDE), BF16)


def last_kernel(
    incoming_ref, slope_ref, mask_ref, bwd_ref, out_in, out_ref, base_ref, cols_ref
):
    def store(pair, value):
        total = out_in[:, lane(2 * pair, 2)] + value
        out_ref[:, lane(pair)] = halves(total[:, :WIDE], total[:, WIDE:])

    step_rows(incoming_ref, slope_ref, mask_ref, bwd_ref, base_ref, cols_ref, store, 10, 4)


def sum_kernel(parts_ref, out_ref):
    total = parts_ref[0].astype(F32)
    for n in range(1, parts_ref.shape[0]):
        total = total + parts_ref[n].astype(F32)
    total = total.astype(BF16)
    for n in range(out_ref.shape[0]):
        out_ref[n] = total


def scale_kernel(whole_ref, out_ref):
    whole = whole_ref[...].astype(F32)
    scale = lax.rsqrt(jnp.sum(whole * whole) / (DEEP * C) + 1e-06)
    for four in range(7):
        at = 3 * C * four
        first, second, third = (
            whole_ref[at + n * C : at + n * C + C, :].astype(F32) * scale for n in range(3)
        )
        parts = (
            first[:, :96],
            jnp.concatenate([first[:, 96:], second[:, :64]], 1),
            jnp.concatenate([second[:, 64:], third[:, :32]], 1),
            third[:, 32:],
        )
        for n, tap in enumerate(range(4 * four, min(4 * four + 4, TAPS))):
            out_ref[C * tap : C * tap + C, :] = parts[n]


def groups():
    def device(y, high, low, core):
        return y * 32 + (2 * high + low) * 2 + core

    kinds = [(y, low, core) for y in range(4) for low in range(2) for core in range(2)]
    near = [[device(y, high, low, core) for y, low, core in kinds] for high in range(FAR)]
    far = [[device(y, high, low, core) for high in range(FAR)] for y, low, core in kinds]
    return near, far


def body(section_input, top_grad, conv_weight, brick_height):
    both = ("space", "pipe")

    def between(by_row, by_col, sections):
        pairs = []
        for x in range(ROWS):
            for y in range(COLS):
                if 0 <= x + by_row < ROWS and 0 <= y + by_col < COLS:
                    source = x * COLS + y
                    target = (x + by_row) * COLS + y + by_col
                    for a, b in sections:
                        pairs.append((source * SECTIONS + a, target * SECTIONS + b))
        return pairs

    same = [(s, s) for s in range(SECTIONS)]
    x = section_input.reshape(C, CELLS)
    top = top_grad.reshape(C, CELLS)
    fwd, bwd = call(weight_kernel, [((C, DEEP), BF16)] * 2)(conv_weight[0])
    up, down, x, top = call(
        rows_kernel,
        [((C + 16, 3 * WIDE), BF16)] * 2 + [((C, CELLS), BF16)] * 2,
        [pltpu.SemaphoreType.DMA((2,))],
        bring=False,
    )(x, top, brick_height)
    before = lax.ppermute(up, both, between(1, 0, same))
    after = lax.ppermute(down, both, between(-1, 0, same))
    before, after, fwd, bwd = lax.optimization_barrier((before, after, fwd, bwd))
    to_right, to_left = call(cols_kernel, [((C + 16, 8 * WIDE), BF16)] * 2)(
        x, top, brick_height, before, after
    )
    left = lax.ppermute(to_right, both, between(0, 1, same))
    right = lax.ppermute(to_left, both, between(0, -1, same))
    (halo,) = call(halo_kernel, [((C, 8 * WIDE), BF16)])(before, after, left, right)
    halo = lax.ppermute(halo, both, between(0, 0, [(0, SECTIONS - 1)]))

    core = ((C, 8 * WIDE), BF16)
    cols = ((DEEP, 2 * WIDE), BF16)
    slope, mask, x_rows = call(
        forward_kernel,
        [((C, 16 * WIDE), F32), ((TAPS, 16, 16 * WIDE), BF16), ((C, 10 * WIDE), BF16)],
        [((9, C, 18 * WIDE), BF16), cols, ((8, 18 * WIDE), F32), ((C, 16 * WIDE), F32)],
    )(x, brick_height, before, after, left, right, fwd)
    def scratch(count):
        return [
            ((9, C, (count + 2) * WIDE), BF16), cols, ((C, (count + 2) * WIDE), BF16),
            ((C, count * WIDE), BF16),
        ]

    def hand_on(value, source):
        return lax.ppermute(value, both, between(0, 0, [(source, source - 1)]))

    tops = (top, halo, left, right, slope, mask, bwd)
    (result,) = call(top_first_kernel, [((C, 8 * WIDE), BF16)], scratch(8))(*tops)
    first = hand_on(result, 3)
    result, grad, out = call(
        top_second_kernel, [((C, 6 * WIDE), BF16), core, core], scratch(6)
    )(*tops, result)
    second = hand_on(result, 3)

    pieces = (2, 8, WIDE), (10, 6, WIDE)
    (result,) = call(
        functools.partial(first_kernel, pieces[0], 3, 6, 96), [((C, 5 * WIDE), BF16)], scratch(6)
    )(first, slope, mask, bwd)
    next_first = hand_on(result, 2)
    result, grad, out = call(
        functools.partial(second_kernel, pieces, 3, 9, 6, 96),
        [((C, 5 * WIDE), BF16), core, core],
        scratch(6),
    )(first, second, slope, mask, bwd, result, grad, out)
    next_second = hand_on(result, 2)
    first, second = next_first, next_second

    pieces = (3, 6, 96), (9, 6, 96)
    (result,) = call(
        functools.partial(first_kernel, pieces[0], 4, 4, 80), [((C, 3 * WIDE), BF16)], scratch(4)
    )(first, slope, mask, bwd)
    next_first = hand_on(result, 1)
    result, grad, out = call(
        functools.partial(second_kernel, pieces, 4, 8, 6, 80),
        [((C, 4 * WIDE), BF16), core, core],
        scratch(6),
    )(first, second, slope, mask, bwd, result, grad, out)
    next_second = hand_on(result, 1)
    first, second = next_first, next_second
    x_rows, _ = lax.optimization_barrier((x_rows, result))
    (x_cols,) = call(gather_kernel, [((DEEP, CELLS), BF16)], [((9, C, 10 * WIDE), BF16)])(
        x_rows, mask
    )
    terms, incoming = call(
        terms_kernel, [((NEAR * CHUNK, WIDE), BF16), ((C, 10 * WIDE), BF16)]
    )(first, second, slope, grad, x_cols)

    near, far = groups()
    parts = lax.all_to_all(
        terms.reshape(NEAR, CHUNK, WIDE), "space", 0, 0, axis_index_groups=near
    )
    parts, out = lax.optimization_barrier((parts, out))
    (out,) = call(
        last_kernel, [((C, CELLS), BF16)], [((9, C, 10 * WIDE), BF16), cols], leave=(0,)
    )(incoming, slope, mask, bwd, out)
    (copies,) = call(sum_kernel, [((FAR, CHUNK, WIDE), BF16)])(parts)
    parts = lax.all_to_all(copies, "space", 0, 0, axis_index_groups=far)
    (copies,) = call(sum_kernel, [((NEAR, CHUNK, WIDE), BF16)])(parts)
    whole = lax.all_to_all(copies, "space", 0, 0, axis_index_groups=near)
    (weight_grad,) = call(scale_kernel, [((DEEP, C), F32)], leave=(0,))(
        whole.reshape(NEAR * CHUNK, WIDE)
    )
    return (out.reshape(1, 1, C, CELLS), weight_grad.reshape(1, TAPS, C, C))


def solution(mesh):
    return jax.shard_map(
        body,
        mesh=mesh,
        in_specs=(
            P("pipe", "space", None, None),
            P("space", None, None),
            P("pipe", None, None, None),
            P("space"),
        ),
        out_specs=(P("pipe", "space", None, None), P("pipe", None, None, None)),
        check_vma=False,
    )
```

```python
import functools

import jax
import jax.numpy as jnp
from jax import lax
from jax.experimental import pallas as pl
from jax.experimental.pallas import tpu as pltpu
from jax.sharding import PartitionSpec as P

C = 96
CELLS = 512
COLS = 8
ROWS = 16
SECTIONS = 4
TAPS = 27
DEEP = TAPS * C
WIDE = 128
CODE = 8
NEAR = 16
FAR = 8
CHUNK = 128
VMEM_BYTES = 32 * 1024 * 1024
F32 = jnp.float32
BF16 = jnp.bfloat16


def call(kernel, outs, scratch=(), leave=(), bring=True):
    shapes = [
        jax.ShapeDtypeStruct(shape, dtype) if n in leave else pltpu.VMEM(shape, dtype)
        for n, (shape, dtype) in enumerate(outs)
    ]

    def run(*args):
        inner = pl.pallas_call(
            kernel,
            out_shape=shapes,
            in_specs=[
                pl.BlockSpec(
                    memory_space=pltpu.SMEM if arg.dtype == jnp.int32
                    else pltpu.VMEM if bring else pl.ANY
                )
                for arg in args
            ],
            out_specs=[pl.BlockSpec(memory_space=pltpu.VMEM)] * len(shapes),
            scratch_shapes=[
                pltpu.VMEM(*item) if isinstance(item, tuple) else item for item in scratch
            ],
            compiler_params=pltpu.CompilerParams(vmem_limit_bytes=VMEM_BYTES),
        )
        return inner(
            *[
                arg if arg.dtype == jnp.int32
                else pltpu.with_memory_space_constraint(arg, pltpu.VMEM if bring else pltpu.HBM)
                for arg in args
            ]
        )

    return run


def lane(row, count=1):
    start = row * WIDE
    if not isinstance(start, int):
        start = pl.multiple_of(start, WIDE)
    return pl.ds(start, count * WIDE)


def turn(value, by):
    by = by % value.shape[1]
    return pltpu.roll(value, by, 1) if by else value


def shifted_rows(base_ref, row, tile, low=None, high=None):
    level = lax.broadcasted_iota(jnp.int32, (C, WIDE), 1) % 8
    for oy, source in ((-1, low), (0, None), (1, high)):
        source = tile if source is None else source
        for oz in (-1, 0, 1):
            if oz == 0:
                moved = turn(source, -8 * oy)
            elif oz > 0:
                moved = jnp.where(level < 7, turn(source, -8 * oy - 1), turn(source, -8 * oy + 7))
            else:
                moved = jnp.where(level > 0, turn(source, -8 * oy + 1), turn(source, -8 * oy - 7))
            base_ref[3 * (oy + 1) + oz + 1, :, lane(row)] = moved


def make_cols(cols_ref, base_ref, mask_ref, base_row, mask_row, at=0):
    for ox in (-1, 0, 1):
        for j in range(9):
            tap = 9 * (ox + 1) + j
            tile = base_ref[j, :, lane(base_row + ox, 2)].reshape(C // 16, 16, 2 * WIDE)
            kept = tile * mask_ref[tap, :, lane(mask_row, 2)][None]
            cols_ref[C * tap : C * tap + C, lane(at, 2)] = kept.reshape(C, 2 * WIDE)


def product(weight, cols):
    return lax.dot_general(
        weight, cols, (((1,), (0,)), ((), ())), preferred_element_type=F32
    )


def weight_kernel(w_ref, fwd_ref, bwd_ref):
    for q in range(TAPS):
        fwd_ref[:, C * q : C * q + C] = w_ref[q].T
        bwd_ref[:, C * q : C * q + C] = w_ref[TAPS - 1 - q]


OUTER = (1, 2, 3, 4, 13, 14, 15, 16)


def code_of(height_ref, shape):
    return jnp.full(shape, (height_ref[0] + CODE).astype(F32), F32)


def rows_kernel(x_hbm, top_hbm, height_ref, up_ref, down_ref, x_ref, top_ref, sems):
    x_copy = pltpu.make_async_copy(x_hbm, x_ref, sems.at[0])
    top_copy = pltpu.make_async_copy(top_hbm, top_ref, sems.at[1])
    x_copy.start()
    top_copy.start()
    x_copy.wait()
    top_copy.wait()
    lowest = lax.axis_index("pipe") == 0
    code = code_of(height_ref, (16, 3 * WIDE)).astype(BF16)
    spare = jnp.zeros((C, 64), BF16)
    up_ref[C:, :] = code
    down_ref[C:, :] = code
    up_ref[:C, :WIDE] = x_ref[:, 384:512]
    down_ref[:C, :WIDE] = x_ref[:, 0:128]

    @pl.when(lowest)
    def _():
        up_ref[:C, WIDE:] = top_ref[:, 256:512]
        down_ref[:C, WIDE:] = top_ref[:, 0:256]

    @pl.when(jnp.logical_not(lowest))
    def _():
        up_ref[:C, WIDE:] = jnp.concatenate([x_ref[:, 192:384], spare], 1)
        down_ref[:C, WIDE:] = jnp.concatenate([x_ref[:, 128:320], spare], 1)


def x_layer(x_ref, before_ref, after_ref, row):
    if row < 5:
        at = 64 * (row - 3) if row >= 3 else WIDE + 64 * row
        return before_ref[:C, at : at + 64]
    if row < 13:
        return x_ref[:, 64 * (row - 5) : 64 * (row - 5) + 64]
    at = 64 * (row - 13) if row < 15 else WIDE + 64 * (row - 15)
    return after_ref[:C, at : at + 64]


def top_layer(before_ref, after_ref, row):
    if row < 5:
        return before_ref[:C, WIDE + 64 * (row - 1) : WIDE + 64 * row]
    return after_ref[:C, WIDE + 64 * (row - 13) : WIDE + 64 * (row - 12)]


def join(parts):
    return jnp.concatenate(parts, 1)


def cols_kernel(x_ref, top_ref, height_ref, before_ref, after_ref, right_ref, left_ref):
    lowest = lax.axis_index("pipe") == 0
    codes = join(
        [before_ref[C:, :WIDE], code_of(height_ref, (16, WIDE)).astype(BF16), after_ref[C:, :WIDE]]
    )
    for out, start, fifth in ((right_ref, 32, 24), (left_ref, 0, 32)):

        def piece(layer, start=start):
            return layer[:, start : start + 32]

        out[C:, : 3 * WIDE] = codes
        out[C:, 3 * WIDE :] = jnp.zeros((16, 5 * WIDE), BF16)
        for four in range(3):
            rows = range(3 + 4 * four, 7 + 4 * four)
            out[:C, lane(four)] = join(
                [piece(x_layer(x_ref, before_ref, after_ref, row)) for row in rows]
            )

        @pl.when(lowest)
        def _(out=out, piece=piece):
            tops = [piece(top_layer(before_ref, after_ref, row)) for row in OUTER]
            out[:C, lane(3)] = join(tops[:4])
            out[:C, lane(4)] = join(tops[4:])
            out[:C, lane(5, 3)] = jnp.zeros((C, 3 * WIDE), BF16)

        @pl.when(jnp.logical_not(lowest))
        def _(out=out, piece=piece, fifth=fifth):
            outer = [
                piece(x_layer(x_ref, before_ref, after_ref, row)) for row in (0, 1, 2, 15, 16, 17)
            ]
            more = [
                x_layer(x_ref, before_ref, after_ref, row)[:, fifth : fifth + 8]
                for row in range(18)
            ]
            tops = [piece(top_ref[:, 64 * n : 64 * n + 64]) for n in range(8)]
            out[:C, lane(3)] = join(outer[:4])
            out[:C, lane(4)] = join(outer[4:] + more[:8])
            out[:C, lane(5)] = join(more[8:] + [jnp.zeros((C, 48), BF16)])
            out[:C, lane(6)] = join(tops[:4])
            out[:C, lane(7)] = join(tops[4:])


def x_side(side_ref, row):
    if 3 <= row < 15:
        at = 32 * (row - 3)
    else:
        at = 3 * WIDE + 32 * (row if row < 3 else row - 12)
    return side_ref[:C, at : at + 32]


def halo_kernel(before_ref, after_ref, left_ref, right_ref, halo_ref):
    @pl.when(lax.axis_index("pipe") == 0)
    def _():
        for n, row in enumerate(OUTER):
            at = 3 * WIDE + 32 * n
            middle = top_layer(before_ref, after_ref, row)
            sides = left_ref[:C, at : at + 32], right_ref[:C, at : at + 32]
            halo_ref[:, lane(n)] = join([sides[0], middle, sides[1]])


def forward_kernel(
    x_ref, height_ref, before_ref, after_ref, left_ref, right_ref, fwd_ref,
    slope_ref, mask_ref, rows_ref,
    base_ref, cols_ref, code_ref, pre_ref,
):
    where = lax.broadcasted_iota(jnp.int32, (8, WIDE), 1)
    middle = (
        before_ref[C : C + 8, :WIDE].astype(F32),
        code_of(height_ref, (8, WIDE)),
        after_ref[C : C + 8, :WIDE].astype(F32),
    )
    codes = []
    for n in range(3):
        left = left_ref[C : C + 8, lane(n)].astype(F32)
        right = right_ref[C : C + 8, lane(n)].astype(F32)
        codes.append(jnp.where(where < 32, left, jnp.where(where < 96, middle[n], right)))
    for row in range(18):
        code_ref[:, lane(row)] = codes[0 if row < 5 else 1 if row < 13 else 2]
    for row in range(18):
        tile = join(
            [
                x_side(left_ref, row),
                x_layer(x_ref, before_ref, after_ref, row),
                x_side(right_ref, row),
            ]
        )
        if 4 <= row < 14:
            rows_ref[:, lane(row - 4)] = tile
        at = 4 * WIDE + 64 + 8 * row
        low = join([tile[:, :120], left_ref[:C, at : at + 8]])
        high = join([right_ref[:C, at : at + 8], tile[:, 8:]])
        shifted_rows(base_ref, row, tile, low, high)

    level = lax.broadcasted_iota(jnp.int32, (8, WIDE), 1) % 8
    rise_of = {
        -1: jnp.where(level == 0, -1.0, 0.0),
        0: jnp.zeros((8, WIDE), F32),
        1: jnp.where(level == 7, 1.0, 0.0),
    }

    for rows in ((0, 1, 2), (3,), (4,), (5, 6, 7, 8, 9, 10), (11,), (12,), (13, 14, 15)):
        here = code_ref[:, lane(rows[0] + 1)]
        for ox in (-1, 0, 1):
            near = code_ref[:, lane(rows[0] + 1 + ox)]
            for oy in (-1, 0, 1):
                if oy < 0:
                    source = jnp.where(where >= 120, near[:, 0:1], near)
                elif oy > 0:
                    source = jnp.where(where < 8, near[:, 127:128], near)
                else:
                    source = near
                rise = turn(source, -8 * oy) - here
                for oz in (-1, 0, 1):
                    keep = jnp.where(rise == rise_of[oz], 1.0, 0.0)
                    keep = jnp.concatenate([keep, keep], 0).astype(BF16)
                    tap = 9 * (ox + 1) + 3 * (oy + 1) + oz + 1
                    for row in rows:
                        mask_ref[tap, :, lane(row)] = keep

    def forward(pair, carry):
        make_cols(cols_ref, base_ref, mask_ref, 2 * pair + 1, 2 * pair)
        pre_ref[:, lane(2 * pair, 2)] = product(fwd_ref[...], cols_ref[...])
        return carry

    lax.fori_loop(0, 8, forward, 0)
    for row in range(16):
        pre = pre_ref[:, lane(row)]
        sigma = 1.0 / (1.0 + jnp.exp(-pre))
        slope_ref[:, lane(row)] = sigma * (1.0 + pre * (1.0 - sigma))


def top_row(top_ref, halo_ref, left_ref, right_ref, row):
    if 5 <= row < 13:
        at, side = 64 * (row - 5), 6 * WIDE + 32 * (row - 5)
        tile = join(
            [
                left_ref[:C, side : side + 32],
                top_ref[:, at : at + 64],
                right_ref[:C, side : side + 32],
            ]
        )
    else:
        tile = halo_ref[:, lane(OUTER.index(row))]
    return jnp.where(lax.axis_index("pipe") == SECTIONS - 1, tile, jnp.zeros_like(tile))


def step_rows(incoming_ref, slope_ref, mask_ref, bwd_ref, base_ref, cols_ref, store, count, first):
    for row in range(count):
        grad = (
            incoming_ref[:, lane(row)].astype(F32) * slope_ref[:, lane(row + first - 1)]
        ).astype(BF16)
        shifted_rows(base_ref, row, grad)

    def backward(pair, carry):
        make_cols(cols_ref, base_ref, mask_ref, 2 * pair + 1, 2 * pair + first)
        total = incoming_ref[:, lane(2 * pair + 1, 2)].astype(F32) + product(
            bwd_ref[...], cols_ref[...]
        )
        store(pair, total.astype(BF16))
        return carry

    lax.fori_loop(0, (count - 2) // 2, backward, 0)


def spread(packed_ref, width, row):
    spare = jnp.zeros((C, (WIDE - width) // 2), BF16)
    return join([spare, packed_ref[:, width * row : width * row + width], spare])


def pieces_row(pieces, row):
    for ref, first, count, width in pieces:
        if first <= row < first + count:
            if width == WIDE:
                return ref[:, lane(row - first)]
            return spread(ref, width, row - first)


def step_part(row_of, low, count, width, result_ref, slope_ref, mask_ref, bwd_ref, scratch):
    base_ref, cols_ref, rows_ref, full_ref = scratch
    for n in range(count + 2):
        rows_ref[:, lane(n)] = row_of(low - 1 + n)

    def store(pair, value):
        full_ref[:, lane(2 * pair, 2)] = value

    step_rows(
        rows_ref, slope_ref, mask_ref, bwd_ref, base_ref, cols_ref, store, count + 2, low - 1
    )
    skip = (WIDE - width) // 2
    packed = [full_ref[:, lane(n)][:, skip : skip + width] for n in range(count)]
    spare = result_ref.shape[1] - width * count
    result_ref[...] = join(packed + [jnp.zeros((C, spare), BF16)] if spare else packed)


def keep_own(row_of, result_of, slope_ref, grad_in, out_in, grad_ref, out_ref):
    for n in range(8):
        grad = (row_of(n + 5).astype(F32) * slope_ref[:, lane(n + 4)]).astype(BF16)
        out = result_of(n + 5)
        if grad_in is not None:
            grad, out = grad + grad_in[:, lane(n)], out + out_in[:, lane(n)]
        grad_ref[:, lane(n)] = grad
        out_ref[:, lane(n)] = out


def top_first_kernel(
    top_ref, halo_ref, left_ref, right_ref, slope_ref, mask_ref, bwd_ref, result_ref, *scratch
):
    def row_of(row):
        return top_row(top_ref, halo_ref, left_ref, right_ref, row)

    step_part(row_of, 2, 8, WIDE, result_ref, slope_ref, mask_ref, bwd_ref, scratch)


def top_second_kernel(
    top_ref, halo_ref, left_ref, right_ref, slope_ref, mask_ref, bwd_ref, earlier_ref,
    result_ref, grad_ref, out_ref, *scratch,
):
    def row_of(row):
        return top_row(top_ref, halo_ref, left_ref, right_ref, row)

    def result_of(row):
        return pieces_row(((earlier_ref, 2, 8, WIDE), (result_ref, 10, 6, WIDE)), row)

    step_part(row_of, 10, 6, WIDE, result_ref, slope_ref, mask_ref, bwd_ref, scratch)
    keep_own(row_of, result_of, slope_ref, None, None, grad_ref, out_ref)


def first_kernel(piece, low, count, width, piece_ref, slope_ref, mask_ref, bwd_ref, result_ref,
                 *scratch):
    def row_of(row):
        return pieces_row(((piece_ref,) + piece,), row)

    step_part(row_of, low, count, width, result_ref, slope_ref, mask_ref, bwd_ref, scratch)


def second_kernel(
    pieces, early, low, count, width,
    first_ref, second_ref, slope_ref, mask_ref, bwd_ref, earlier_ref, grad_in, out_in,
    result_ref, grad_ref, out_ref, *scratch,
):
    def row_of(row):
        return pieces_row(((first_ref,) + pieces[0], (second_ref,) + pieces[1]), row)

    def result_of(row):
        later = (result_ref, low, count, width)
        return pieces_row(((earlier_ref, early, low - early, width), later), row)

    step_part(row_of, low, count, width, result_ref, slope_ref, mask_ref, bwd_ref, scratch)
    keep_own(row_of, result_of, slope_ref, grad_in, out_in, grad_ref, out_ref)


def halves(first, second):
    where = lax.broadcasted_iota(jnp.int32, first.shape, 1)
    return jnp.where(where < 64, turn(first, -32), turn(second, 32))


def gather_kernel(x_ref, mask_ref, all_ref, base_ref):
    for row in range(10):
        shifted_rows(base_ref, row, x_ref[:, lane(row)])

    def one(pair, carry):
        for tap in range(TAPS):
            ox, j = tap // 9 - 1, tap % 9
            tiles = []
            for n in range(2):
                tile = base_ref[j, :, lane(2 * pair + 1 + n + ox)].reshape(C // 16, 16, WIDE)
                kept = tile * mask_ref[tap, :, lane(2 * pair + 4 + n)][None]
                tiles.append(kept.reshape(C, WIDE))
            all_ref[C * tap : C * tap + C, lane(pair)] = halves(*tiles)
        return carry

    lax.fori_loop(0, 4, one, 0)


def terms_kernel(
    first_ref, second_ref, slope_ref, grad_in, all_ref, terms_ref, incoming_ref
):
    for row in range(10):
        incoming_ref[:, lane(row)] = pieces_row(
            ((first_ref, 4, 4, 80), (second_ref, 8, 6, 80)), row + 4
        )
    grads = []
    for row in range(8):
        grad = incoming_ref[:, lane(row + 1)].astype(F32) * slope_ref[:, lane(row + 4)]
        grads.append(grad_in[:, lane(row)] + grad.astype(BF16))
    grads = join([halves(grads[2 * pair], grads[2 * pair + 1]) for pair in range(4)])
    for four in range(7):
        parts = []
        for tap in range(4 * four, 4 * four + 4):
            if tap < TAPS:
                part = lax.dot_general(
                    all_ref[C * tap : C * tap + C, :], grads, (((1,), (1,)), ((), ())),
                    preferred_element_type=F32,
                ).astype(BF16)
            else:
                part = jnp.zeros((C, C), BF16)
            parts.append(part)
        first, second, third, fourth = parts
        at = 3 * C * four
        terms_ref[at : at + C, :] = jnp.concatenate([first, second[:, :32]], 1)
        terms_ref[at + C : at + 2 * C, :] = jnp.concatenate([second[:, 32:], third[:, :64]], 1)
        terms_ref[at + 2 * C : at + 3 * C, :] = jnp.concatenate([third[:, 64:], fourth], 1)
    terms_ref[21 * C :, :] = jnp.zeros((NEAR * CHUNK - 21 * C, WIDE), BF16)


def last_kernel(
    incoming_ref, slope_ref, mask_ref, bwd_ref, out_in, out_ref, base_ref, cols_ref
):
    def store(pair, value):
        total = out_in[:, lane(2 * pair, 2)] + value
        out_ref[:, lane(pair)] = halves(total[:, :WIDE], total[:, WIDE:])

    step_rows(incoming_ref, slope_ref, mask_ref, bwd_ref, base_ref, cols_ref, store, 10, 4)


def sum_kernel(parts_ref, out_ref):
    total = parts_ref[0].astype(F32)
    for n in range(1, parts_ref.shape[0]):
        total = total + parts_ref[n].astype(F32)
    total = total.astype(BF16)
    for n in range(out_ref.shape[0]):
        out_ref[n] = total


def scale_kernel(whole_ref, out_ref):
    whole = whole_ref[...].astype(F32)
    scale = lax.rsqrt(jnp.sum(whole * whole) / (DEEP * C) + 1e-06)
    for four in range(7):
        at = 3 * C * four
        first, second, third = (whole_ref[at + n * C : at + n * C + C, :] for n in range(3))
        parts = (
            first[:, :96],
            jnp.concatenate([first[:, 96:], second[:, :64]], 1),
            jnp.concatenate([second[:, 64:], third[:, :32]], 1),
            third[:, 32:],
        )
        for n, tap in enumerate(range(4 * four, min(4 * four + 4, TAPS))):
            out_ref[C * tap : C * tap + C, :] = parts[n].astype(F32) * scale


def groups():
    def device(y, high, low, core):
        return y * 32 + (2 * high + low) * 2 + core

    kinds = [(y, low, core) for y in range(4) for low in range(2) for core in range(2)]
    near = [[device(y, high, low, core) for y, low, core in kinds] for high in range(FAR)]
    far = [[device(y, high, low, core) for high in range(FAR)] for y, low, core in kinds]
    return near, far


def body(section_input, top_grad, conv_weight, brick_height):
    both = ("space", "pipe")

    def between(by_row, by_col, sections):
        pairs = []
        for x in range(ROWS):
            for y in range(COLS):
                if 0 <= x + by_row < ROWS and 0 <= y + by_col < COLS:
                    source = x * COLS + y
                    target = (x + by_row) * COLS + y + by_col
                    for a, b in sections:
                        pairs.append((source * SECTIONS + a, target * SECTIONS + b))
        return pairs

    same = [(s, s) for s in range(SECTIONS)]
    x = section_input.reshape(C, CELLS)
    top = top_grad.reshape(C, CELLS)
    fwd, bwd = call(weight_kernel, [((C, DEEP), BF16)] * 2)(conv_weight[0])
    up, down, x, top = call(
        rows_kernel,
        [((C + 16, 3 * WIDE), BF16)] * 2 + [((C, CELLS), BF16)] * 2,
        [pltpu.SemaphoreType.DMA((2,))],
        bring=False,
    )(x, top, brick_height)
    before = lax.ppermute(up, both, between(1, 0, same))
    after = lax.ppermute(down, both, between(-1, 0, same))
    before, after, fwd, bwd = lax.optimization_barrier((before, after, fwd, bwd))
    to_right, to_left = call(cols_kernel, [((C + 16, 8 * WIDE), BF16)] * 2)(
        x, top, brick_height, before, after
    )
    left = lax.ppermute(to_right, both, between(0, 1, same))
    right = lax.ppermute(to_left, both, between(0, -1, same))
    (halo,) = call(halo_kernel, [((C, 8 * WIDE), BF16)])(before, after, left, right)
    halo = lax.ppermute(halo, both, between(0, 0, [(0, SECTIONS - 1)]))

    core = ((C, 8 * WIDE), BF16)
    cols = ((DEEP, 2 * WIDE), BF16)
    slope, mask, x_rows = call(
        forward_kernel,
        [((C, 16 * WIDE), F32), ((TAPS, 16, 16 * WIDE), BF16), ((C, 10 * WIDE), BF16)],
        [((9, C, 18 * WIDE), BF16), cols, ((8, 18 * WIDE), F32), ((C, 16 * WIDE), F32)],
    )(x, brick_height, before, after, left, right, fwd)
    def scratch(count):
        return [
            ((9, C, (count + 2) * WIDE), BF16), cols, ((C, (count + 2) * WIDE), BF16),
            ((C, count * WIDE), BF16),
        ]

    def hand_on(value, source):
        return lax.ppermute(value, both, between(0, 0, [(source, source - 1)]))

    tops = (top, halo, left, right, slope, mask, bwd)
    (result,) = call(top_first_kernel, [((C, 8 * WIDE), BF16)], scratch(8))(*tops)
    first = hand_on(result, 3)
    result, grad, out = call(
        top_second_kernel, [((C, 6 * WIDE), BF16), core, core], scratch(6)
    )(*tops, result)
    second = hand_on(result, 3)

    pieces = (2, 8, WIDE), (10, 6, WIDE)
    (result,) = call(
        functools.partial(first_kernel, pieces[0], 3, 6, 96), [((C, 5 * WIDE), BF16)], scratch(6)
    )(first, slope, mask, bwd)
    next_first = hand_on(result, 2)
    result, grad, out = call(
        functools.partial(second_kernel, pieces, 3, 9, 6, 96),
        [((C, 5 * WIDE), BF16), core, core],
        scratch(6),
    )(first, second, slope, mask, bwd, result, grad, out)
    next_second = hand_on(result, 2)
    first, second = next_first, next_second

    pieces = (3, 6, 96), (9, 6, 96)
    (result,) = call(
        functools.partial(first_kernel, pieces[0], 4, 4, 80), [((C, 3 * WIDE), BF16)], scratch(4)
    )(first, slope, mask, bwd)
    next_first = hand_on(result, 1)
    result, grad, out = call(
        functools.partial(second_kernel, pieces, 4, 8, 6, 80),
        [((C, 4 * WIDE), BF16), core, core],
        scratch(6),
    )(first, second, slope, mask, bwd, result, grad, out)
    next_second = hand_on(result, 1)
    first, second = next_first, next_second
    x_rows, _ = lax.optimization_barrier((x_rows, result))
    (x_cols,) = call(gather_kernel, [((DEEP, CELLS), BF16)], [((9, C, 10 * WIDE), BF16)])(
        x_rows, mask
    )
    terms, incoming = call(
        terms_kernel, [((NEAR * CHUNK, WIDE), BF16), ((C, 10 * WIDE), BF16)]
    )(first, second, slope, grad, x_cols)

    near, far = groups()
    parts = lax.all_to_all(
        terms.reshape(NEAR, CHUNK, WIDE), "space", 0, 0, axis_index_groups=near
    )
    parts, out = lax.optimization_barrier((parts, out))
    (out,) = call(
        last_kernel, [((C, CELLS), BF16)], [((9, C, 10 * WIDE), BF16), cols], leave=(0,)
    )(incoming, slope, mask, bwd, out)
    (copies,) = call(sum_kernel, [((FAR, CHUNK, WIDE), BF16)])(parts)
    parts = lax.all_to_all(copies, "space", 0, 0, axis_index_groups=far)
    parts, out = lax.optimization_barrier((parts, out))
    (copies,) = call(sum_kernel, [((NEAR, CHUNK, WIDE), BF16)])(parts)
    whole = lax.all_to_all(copies, "space", 0, 0, axis_index_groups=near)
    (weight_grad,) = call(scale_kernel, [((DEEP, C), F32)], leave=(0,))(
        whole.reshape(NEAR * CHUNK, WIDE)
    )
    return (out.reshape(1, 1, C, CELLS), weight_grad.reshape(1, TAPS, C, C))


def solution(mesh):
    return jax.shard_map(
        body,
        mesh=mesh,
        in_specs=(
            P("pipe", "space", None, None),
            P("space", None, None),
            P("pipe", None, None, None),
            P("space"),
        ),
        out_specs=(P("pipe", "space", None, None), P("pipe", None, None, None)),
        check_vma=False,
    )
```

```python
import functools

import jax
import jax.numpy as jnp
from jax import lax
from jax.experimental import pallas as pl
from jax.experimental.pallas import tpu as pltpu
from jax.sharding import PartitionSpec as P

C = 96
CELLS = 512
COLS = 8
ROWS = 16
SECTIONS = 4
TAPS = 27
DEEP = TAPS * C
WIDE = 128
CODE = 8
NEAR = 16
FAR = 8
CHUNK = 128
VMEM_BYTES = 32 * 1024 * 1024
F32 = jnp.float32
BF16 = jnp.bfloat16


def call(kernel, outs, scratch=(), leave=(), bring=True):
    shapes = [
        jax.ShapeDtypeStruct(shape, dtype) if n in leave else pltpu.VMEM(shape, dtype)
        for n, (shape, dtype) in enumerate(outs)
    ]

    def run(*args):
        inner = pl.pallas_call(
            kernel,
            out_shape=shapes,
            in_specs=[
                pl.BlockSpec(
                    memory_space=pltpu.SMEM if arg.dtype == jnp.int32
                    else pltpu.VMEM if bring else pl.ANY
                )
                for arg in args
            ],
            out_specs=[pl.BlockSpec(memory_space=pltpu.VMEM)] * len(shapes),
            scratch_shapes=[
                pltpu.VMEM(*item) if isinstance(item, tuple) else item for item in scratch
            ],
            compiler_params=pltpu.CompilerParams(vmem_limit_bytes=VMEM_BYTES),
        )
        return inner(
            *[
                arg if arg.dtype == jnp.int32
                else pltpu.with_memory_space_constraint(arg, pltpu.VMEM if bring else pltpu.HBM)
                for arg in args
            ]
        )

    return run


def lane(row, count=1):
    start = row * WIDE
    if not isinstance(start, int):
        start = pl.multiple_of(start, WIDE)
    return pl.ds(start, count * WIDE)


def turn(value, by):
    by = by % value.shape[1]
    return pltpu.roll(value, by, 1) if by else value


def shifted_rows(base_ref, row, tile, low=None, high=None):
    level = lax.broadcasted_iota(jnp.int32, (C, WIDE), 1) % 8
    if low is None:
        along = (
            jnp.where(level > 0, turn(tile, 1), turn(tile, -7)),
            tile,
            jnp.where(level < 7, turn(tile, -1), turn(tile, 7)),
        )
        for oy in (-1, 0, 1):
            for n in range(3):
                base_ref[3 * (oy + 1) + n, :, lane(row)] = turn(along[n], -8 * oy)
        return
    for oy, source in ((-1, low), (0, tile), (1, high)):
        for oz in (-1, 0, 1):
            if oz == 0:
                moved = turn(source, -8 * oy)
            elif oz > 0:
                moved = jnp.where(level < 7, turn(source, -8 * oy - 1), turn(source, -8 * oy + 7))
            else:
                moved = jnp.where(level > 0, turn(source, -8 * oy + 1), turn(source, -8 * oy - 7))
            base_ref[3 * (oy + 1) + oz + 1, :, lane(row)] = moved


def make_cols(cols_ref, base_ref, mask_ref, base_row, mask_row, at=0):
    for ox in (-1, 0, 1):
        for j in range(9):
            tap = 9 * (ox + 1) + j
            tile = base_ref[j, :, lane(base_row + ox, 2)].reshape(C // 16, 16, 2 * WIDE)
            kept = tile * mask_ref[tap, :, lane(mask_row, 2)][None]
            cols_ref[C * tap : C * tap + C, lane(at, 2)] = kept.reshape(C, 2 * WIDE)


def product(weight, cols):
    return lax.dot_general(
        weight, cols, (((1,), (0,)), ((), ())), preferred_element_type=F32
    )


def weight_kernel(w_ref, fwd_ref, bwd_ref):
    for q in range(TAPS):
        fwd_ref[:, C * q : C * q + C] = w_ref[q].T
        bwd_ref[:, C * q : C * q + C] = w_ref[TAPS - 1 - q]


OUTER = (1, 2, 3, 4, 13, 14, 15, 16)


def code_of(height_ref, shape):
    return jnp.full(shape, (height_ref[0] + CODE).astype(F32), F32)


def rows_kernel(x_hbm, top_hbm, height_ref, up_ref, down_ref, x_ref, top_ref, sems):
    x_copy = pltpu.make_async_copy(x_hbm, x_ref, sems.at[0])
    top_copy = pltpu.make_async_copy(top_hbm, top_ref, sems.at[1])
    x_copy.start()
    top_copy.start()
    x_copy.wait()
    top_copy.wait()
    lowest = lax.axis_index("pipe") == 0
    code = code_of(height_ref, (16, 3 * WIDE)).astype(BF16)
    spare = jnp.zeros((C, 64), BF16)
    up_ref[C:, :] = code
    down_ref[C:, :] = code
    up_ref[:C, :WIDE] = x_ref[:, 384:512]
    down_ref[:C, :WIDE] = x_ref[:, 0:128]

    @pl.when(lowest)
    def _():
        up_ref[:C, WIDE:] = top_ref[:, 256:512]
        down_ref[:C, WIDE:] = top_ref[:, 0:256]

    @pl.when(jnp.logical_not(lowest))
    def _():
        up_ref[:C, WIDE:] = jnp.concatenate([x_ref[:, 192:384], spare], 1)
        down_ref[:C, WIDE:] = jnp.concatenate([x_ref[:, 128:320], spare], 1)


def x_layer(x_ref, before_ref, after_ref, row):
    if row < 5:
        at = 64 * (row - 3) if row >= 3 else WIDE + 64 * row
        return before_ref[:C, at : at + 64]
    if row < 13:
        return x_ref[:, 64 * (row - 5) : 64 * (row - 5) + 64]
    at = 64 * (row - 13) if row < 15 else WIDE + 64 * (row - 15)
    return after_ref[:C, at : at + 64]


def top_layer(before_ref, after_ref, row):
    if row < 5:
        return before_ref[:C, WIDE + 64 * (row - 1) : WIDE + 64 * row]
    return after_ref[:C, WIDE + 64 * (row - 13) : WIDE + 64 * (row - 12)]


def join(parts):
    return jnp.concatenate(parts, 1)


def cols_kernel(x_ref, top_ref, height_ref, before_ref, after_ref, right_ref, left_ref):
    lowest = lax.axis_index("pipe") == 0
    codes = join(
        [before_ref[C:, :WIDE], code_of(height_ref, (16, WIDE)).astype(BF16), after_ref[C:, :WIDE]]
    )
    for out, start, fifth in ((right_ref, 32, 24), (left_ref, 0, 32)):

        def piece(layer, start=start):
            return layer[:, start : start + 32]

        out[C:, : 3 * WIDE] = codes
        out[C:, 3 * WIDE :] = jnp.zeros((16, 5 * WIDE), BF16)
        for four in range(3):
            rows = range(3 + 4 * four, 7 + 4 * four)
            out[:C, lane(four)] = join(
                [piece(x_layer(x_ref, before_ref, after_ref, row)) for row in rows]
            )

        @pl.when(lowest)
        def _(out=out, piece=piece):
            tops = [piece(top_layer(before_ref, after_ref, row)) for row in OUTER]
            out[:C, lane(3)] = join(tops[:4])
            out[:C, lane(4)] = join(tops[4:])
            out[:C, lane(5, 3)] = jnp.zeros((C, 3 * WIDE), BF16)

        @pl.when(jnp.logical_not(lowest))
        def _(out=out, piece=piece, fifth=fifth):
            outer = [
                piece(x_layer(x_ref, before_ref, after_ref, row)) for row in (0, 1, 2, 15, 16, 17)
            ]
            more = [
                x_layer(x_ref, before_ref, after_ref, row)[:, fifth : fifth + 8]
                for row in range(18)
            ]
            tops = [piece(top_ref[:, 64 * n : 64 * n + 64]) for n in range(8)]
            out[:C, lane(3)] = join(outer[:4])
            out[:C, lane(4)] = join(outer[4:] + more[:8])
            out[:C, lane(5)] = join(more[8:] + [jnp.zeros((C, 48), BF16)])
            out[:C, lane(6)] = join(tops[:4])
            out[:C, lane(7)] = join(tops[4:])


def x_side(side_ref, row):
    if 3 <= row < 15:
        at = 32 * (row - 3)
    else:
        at = 3 * WIDE + 32 * (row if row < 3 else row - 12)
    return side_ref[:C, at : at + 32]


def halo_kernel(before_ref, after_ref, left_ref, right_ref, halo_ref):
    @pl.when(lax.axis_index("pipe") == 0)
    def _():
        for n, row in enumerate(OUTER):
            at = 3 * WIDE + 32 * n
            middle = top_layer(before_ref, after_ref, row)
            sides = left_ref[:C, at : at + 32], right_ref[:C, at : at + 32]
            halo_ref[:, lane(n)] = join([sides[0], middle, sides[1]])


def forward_kernel(
    x_ref, height_ref, before_ref, after_ref, left_ref, right_ref, fwd_ref,
    slope_ref, mask_ref, rows_ref,
    base_ref, cols_ref, code_ref, pre_ref,
):
    where = lax.broadcasted_iota(jnp.int32, (8, WIDE), 1)
    middle = (
        before_ref[C : C + 8, :WIDE].astype(F32),
        code_of(height_ref, (8, WIDE)),
        after_ref[C : C + 8, :WIDE].astype(F32),
    )
    codes = []
    for n in range(3):
        left = left_ref[C : C + 8, lane(n)].astype(F32)
        right = right_ref[C : C + 8, lane(n)].astype(F32)
        codes.append(jnp.where(where < 32, left, jnp.where(where < 96, middle[n], right)))
    for row in range(18):
        code_ref[:, lane(row)] = codes[0 if row < 5 else 1 if row < 13 else 2]
    for row in range(18):
        tile = join(
            [
                x_side(left_ref, row),
                x_layer(x_ref, before_ref, after_ref, row),
                x_side(right_ref, row),
            ]
        )
        if 4 <= row < 14:
            rows_ref[:, lane(row - 4)] = tile
        at = 4 * WIDE + 64 + 8 * row
        low = join([tile[:, :120], left_ref[:C, at : at + 8]])
        high = join([right_ref[:C, at : at + 8], tile[:, 8:]])
        shifted_rows(base_ref, row, tile, low, high)

    level = lax.broadcasted_iota(jnp.int32, (8, WIDE), 1) % 8
    rise_of = {
        -1: jnp.where(level == 0, -1.0, 0.0),
        0: jnp.zeros((8, WIDE), F32),
        1: jnp.where(level == 7, 1.0, 0.0),
    }

    for rows in ((0, 1, 2), (3,), (4,), (5, 6, 7, 8, 9, 10), (11,), (12,), (13, 14, 15)):
        here = code_ref[:, lane(rows[0] + 1)]
        for ox in (-1, 0, 1):
            near = code_ref[:, lane(rows[0] + 1 + ox)]
            for oy in (-1, 0, 1):
                if oy < 0:
                    source = jnp.where(where >= 120, near[:, 0:1], near)
                elif oy > 0:
                    source = jnp.where(where < 8, near[:, 127:128], near)
                else:
                    source = near
                rise = turn(source, -8 * oy) - here
                for oz in (-1, 0, 1):
                    keep = jnp.where(rise == rise_of[oz], 1.0, 0.0)
                    keep = jnp.concatenate([keep, keep], 0).astype(BF16)
                    tap = 9 * (ox + 1) + 3 * (oy + 1) + oz + 1
                    for row in rows:
                        mask_ref[tap, :, lane(row)] = keep

    def forward(pair, carry):
        make_cols(cols_ref, base_ref, mask_ref, 2 * pair + 1, 2 * pair)
        pre_ref[:, lane(2 * pair, 2)] = product(fwd_ref[...], cols_ref[...])
        return carry

    lax.fori_loop(0, 8, forward, 0)
    for row in range(16):
        pre = pre_ref[:, lane(row)]
        sigma = 1.0 / (1.0 + jnp.exp(-pre))
        slope_ref[:, lane(row)] = sigma * (1.0 + pre * (1.0 - sigma))


def top_row(top_ref, halo_ref, left_ref, right_ref, row):
    if 5 <= row < 13:
        at, side = 64 * (row - 5), 6 * WIDE + 32 * (row - 5)
        tile = join(
            [
                left_ref[:C, side : side + 32],
                top_ref[:, at : at + 64],
                right_ref[:C, side : side + 32],
            ]
        )
    else:
        tile = halo_ref[:, lane(OUTER.index(row))]
    return jnp.where(lax.axis_index("pipe") == SECTIONS - 1, tile, jnp.zeros_like(tile))


def step_rows(incoming_ref, slope_ref, mask_ref, bwd_ref, base_ref, cols_ref, store, count, first):
    for row in range(count):
        grad = (
            incoming_ref[:, lane(row)].astype(F32) * slope_ref[:, lane(row + first - 1)]
        ).astype(BF16)
        shifted_rows(base_ref, row, grad)

    def backward(pair, carry):
        make_cols(cols_ref, base_ref, mask_ref, 2 * pair + 1, 2 * pair + first)
        total = incoming_ref[:, lane(2 * pair + 1, 2)].astype(F32) + product(
            bwd_ref[...], cols_ref[...]
        )
        store(pair, total.astype(BF16))
        return carry

    lax.fori_loop(0, (count - 2) // 2, backward, 0)


def spread(packed_ref, width, row):
    spare = jnp.zeros((C, (WIDE - width) // 2), BF16)
    return join([spare, packed_ref[:, width * row : width * row + width], spare])


TOP_PIECES = (2, 8, WIDE), (10, 6, WIDE)
MIDDLE_PIECES = (3, 6, 96), (9, 6, 96)
LATE_PIECES = (4, 4, 80), (8, 6, 80)


def pieces_row(pieces, row):
    for ref, first, count, width in pieces:
        if first <= row < first + count:
            if width == WIDE:
                return ref[:, lane(row - first)]
            return spread(ref, width, row - first)


def step_part(row_of, low, count, width, result_ref, slope_ref, mask_ref, bwd_ref, scratch):
    base_ref, cols_ref, rows_ref, full_ref = scratch
    for n in range(count + 2):
        rows_ref[:, lane(n)] = row_of(low - 1 + n)

    def store(pair, value):
        full_ref[:, lane(2 * pair, 2)] = value

    step_rows(
        rows_ref, slope_ref, mask_ref, bwd_ref, base_ref, cols_ref, store, count + 2, low - 1
    )
    skip = (WIDE - width) // 2
    packed = [full_ref[:, lane(n)][:, skip : skip + width] for n in range(count)]
    spare = result_ref.shape[1] - width * count
    result_ref[...] = join(packed + [jnp.zeros((C, spare), BF16)] if spare else packed)


def top_kernel(
    low, count, top_ref, halo_ref, left_ref, right_ref, slope_ref, mask_ref, bwd_ref,
    result_ref, *scratch,
):
    def row_of(row):
        return top_row(top_ref, halo_ref, left_ref, right_ref, row)

    step_part(row_of, low, count, WIDE, result_ref, slope_ref, mask_ref, bwd_ref, scratch)


def middle_kernel(pieces, low, count, width, *refs):
    given, refs = refs[: len(pieces)], refs[len(pieces) :]
    slope_ref, mask_ref, bwd_ref, result_ref, *scratch = refs

    def row_of(row):
        return pieces_row([(ref,) + piece for ref, piece in zip(given, pieces)], row)

    step_part(row_of, low, count, width, result_ref, slope_ref, mask_ref, bwd_ref, scratch)


def halves(first, second):
    where = lax.broadcasted_iota(jnp.int32, first.shape, 1)
    return jnp.where(where < 64, turn(first, -32), turn(second, 32))


def gather_kernel(
    top_ref, halo_ref, left_ref, right_ref, slope_ref, mask_ref, x_ref, *refs
):
    kinds = TOP_PIECES + MIDDLE_PIECES + LATE_PIECES
    pieces = [(ref,) + piece for ref, piece in zip(refs[:6], kinds)]
    incoming = [(ref,) + piece for ref, piece in zip(refs[6:10], TOP_PIECES + MIDDLE_PIECES)]
    all_ref, grad_ref, out_ref, base_ref = refs[10:]
    for n in range(8):
        row = n + 5
        scale = slope_ref[:, lane(n + 4)]
        tiles = (
            top_row(top_ref, halo_ref, left_ref, right_ref, row),
            pieces_row(incoming[:2], row),
            pieces_row(incoming[2:], row),
        )
        grads = [(tile.astype(F32) * scale).astype(BF16) for tile in tiles]
        grad_ref[:, lane(n)] = grads[0] + grads[1] + grads[2]
        outs = [pieces_row(pieces[at : at + 2], row) for at in (0, 2, 4)]
        out_ref[:, lane(n)] = outs[0] + outs[1] + outs[2]
    for row in range(10):
        shifted_rows(base_ref, row, x_ref[:, lane(row)])

    def one(pair, carry):
        for tap in range(TAPS):
            ox, j = tap // 9 - 1, tap % 9
            tiles = []
            for n in range(2):
                tile = base_ref[j, :, lane(2 * pair + 1 + n + ox)].reshape(C // 16, 16, WIDE)
                kept = tile * mask_ref[tap, :, lane(2 * pair + 4 + n)][None]
                tiles.append(kept.reshape(C, WIDE))
            all_ref[C * tap : C * tap + C, lane(pair)] = halves(*tiles)
        return carry

    lax.fori_loop(0, 4, one, 0)


def terms_kernel(
    first_ref, second_ref, slope_ref, grad_in, all_ref, terms_ref, incoming_ref
):
    for row in range(10):
        incoming_ref[:, lane(row)] = pieces_row(
            ((first_ref,) + LATE_PIECES[0], (second_ref,) + LATE_PIECES[1]), row + 4
        )
    grads = []
    for row in range(8):
        grad = incoming_ref[:, lane(row + 1)].astype(F32) * slope_ref[:, lane(row + 4)]
        grads.append(grad_in[:, lane(row)] + grad.astype(BF16))
    grads = join([halves(grads[2 * pair], grads[2 * pair + 1]) for pair in range(4)])
    for four in range(7):
        parts = []
        for tap in range(4 * four, 4 * four + 4):
            if tap < TAPS:
                part = lax.dot_general(
                    all_ref[C * tap : C * tap + C, :], grads, (((1,), (1,)), ((), ())),
                    preferred_element_type=F32,
                ).astype(BF16)
            else:
                part = jnp.zeros((C, C), BF16)
            parts.append(part)
        first, second, third, fourth = parts
        at = 3 * C * four
        terms_ref[at : at + C, :] = jnp.concatenate([first, second[:, :32]], 1)
        terms_ref[at + C : at + 2 * C, :] = jnp.concatenate([second[:, 32:], third[:, :64]], 1)
        terms_ref[at + 2 * C : at + 3 * C, :] = jnp.concatenate([third[:, 64:], fourth], 1)
    terms_ref[21 * C :, :] = jnp.zeros((NEAR * CHUNK - 21 * C, WIDE), BF16)


def last_kernel(
    incoming_ref, slope_ref, mask_ref, bwd_ref, out_in, out_ref, base_ref, cols_ref
):
    def store(pair, value):
        total = out_in[:, lane(2 * pair, 2)] + value
        out_ref[:, lane(pair)] = halves(total[:, :WIDE], total[:, WIDE:])

    step_rows(incoming_ref, slope_ref, mask_ref, bwd_ref, base_ref, cols_ref, store, 10, 4)


def sum_kernel(parts_ref, out_ref):
    total = parts_ref[0].astype(F32)
    for n in range(1, parts_ref.shape[0]):
        total = total + parts_ref[n].astype(F32)
    total = total.astype(BF16)
    for n in range(out_ref.shape[0]):
        out_ref[n] = total


def scale_kernel(whole_ref, out_ref):
    whole = whole_ref[...].astype(F32)
    scale = lax.rsqrt(jnp.sum(whole * whole) / (DEEP * C) + 1e-06)
    for four in range(7):
        at = 3 * C * four
        first, second, third = (whole_ref[at + n * C : at + n * C + C, :] for n in range(3))
        parts = (
            first[:, :96],
            jnp.concatenate([first[:, 96:], second[:, :64]], 1),
            jnp.concatenate([second[:, 64:], third[:, :32]], 1),
            third[:, 32:],
        )
        for n, tap in enumerate(range(4 * four, min(4 * four + 4, TAPS))):
            out_ref[C * tap : C * tap + C, :] = parts[n].astype(F32) * scale


def groups():
    def device(y, high, low, core):
        return y * 32 + (2 * high + low) * 2 + core

    kinds = [(y, low, core) for y in range(4) for low in range(2) for core in range(2)]
    near = [[device(y, high, low, core) for y, low, core in kinds] for high in range(FAR)]
    far = [[device(y, high, low, core) for high in range(FAR)] for y, low, core in kinds]
    return near, far


def body(section_input, top_grad, conv_weight, brick_height):
    both = ("space", "pipe")

    def between(by_row, by_col, sections):
        pairs = []
        for x in range(ROWS):
            for y in range(COLS):
                if 0 <= x + by_row < ROWS and 0 <= y + by_col < COLS:
                    source = x * COLS + y
                    target = (x + by_row) * COLS + y + by_col
                    for a, b in sections:
                        pairs.append((source * SECTIONS + a, target * SECTIONS + b))
        return pairs

    same = [(s, s) for s in range(SECTIONS)]
    x = section_input.reshape(C, CELLS)
    top = top_grad.reshape(C, CELLS)
    fwd, bwd = call(weight_kernel, [((C, DEEP), BF16)] * 2)(conv_weight[0])
    up, down, x, top = call(
        rows_kernel,
        [((C + 16, 3 * WIDE), BF16)] * 2 + [((C, CELLS), BF16)] * 2,
        [pltpu.SemaphoreType.DMA((2,))],
        bring=False,
    )(x, top, brick_height)
    before = lax.ppermute(up, both, between(1, 0, same))
    after = lax.ppermute(down, both, between(-1, 0, same))
    before, after, fwd, bwd = lax.optimization_barrier((before, after, fwd, bwd))
    to_right, to_left = call(cols_kernel, [((C + 16, 8 * WIDE), BF16)] * 2)(
        x, top, brick_height, before, after
    )
    left = lax.ppermute(to_right, both, between(0, 1, same))
    right = lax.ppermute(to_left, both, between(0, -1, same))
    (halo,) = call(halo_kernel, [((C, 8 * WIDE), BF16)])(before, after, left, right)
    halo = lax.ppermute(halo, both, between(0, 0, [(0, SECTIONS - 1)]))

    core = ((C, 8 * WIDE), BF16)
    cols = ((DEEP, 2 * WIDE), BF16)
    slope, mask, x_rows = call(
        forward_kernel,
        [((C, 16 * WIDE), F32), ((TAPS, 16, 16 * WIDE), BF16), ((C, 10 * WIDE), BF16)],
        [((9, C, 18 * WIDE), BF16), cols, ((8, 18 * WIDE), F32), ((C, 16 * WIDE), F32)],
    )(x, brick_height, before, after, left, right, fwd)
    def scratch(count):
        return [
            ((9, C, (count + 2) * WIDE), BF16), cols, ((C, (count + 2) * WIDE), BF16),
            ((C, count * WIDE), BF16),
        ]

    def hand_on(value, source):
        return lax.ppermute(value, both, between(0, 0, [(source, source - 1)]))

    def behind(kernel, count):
        return lambda *refs: kernel(*refs[:count], *refs[count + 1 :])

    def parts_of(kernels, args, pieces, source):
        made = []
        for kernel, given, (low, count, width) in zip(kernels, args, pieces):
            if made:
                kernel, given = behind(kernel, len(given)), given + (made[0][0],)
            lanes = -(-count * width // WIDE) * WIDE
            (result,) = call(kernel, [((C, lanes), BF16)], scratch(count))(*given)
            made.append((result, hand_on(result, source)))
        return [result for result, _ in made], [moved for _, moved in made]

    def middle(given, pieces, low, count, width):
        return functools.partial(middle_kernel, pieces[:given], low, count, width)

    rest = (slope, mask, bwd)
    tops, moved = parts_of(
        [functools.partial(top_kernel, low, count) for low, count, _ in TOP_PIECES],
        [(top, halo, left, right) + rest] * 2,
        TOP_PIECES,
        3,
    )
    middles, moved_on = parts_of(
        [middle(n + 1, TOP_PIECES, *MIDDLE_PIECES[n]) for n in range(2)],
        [tuple(moved[: n + 1]) + rest for n in range(2)],
        MIDDLE_PIECES,
        2,
    )
    lates, (first, second) = parts_of(
        [middle(n + 1, MIDDLE_PIECES, *LATE_PIECES[n]) for n in range(2)],
        [tuple(moved_on[: n + 1]) + rest for n in range(2)],
        LATE_PIECES,
        1,
    )
    x_rows, result = lax.optimization_barrier((x_rows, lates[1]))
    x_cols, grad, out = call(
        gather_kernel, [((DEEP, CELLS), BF16), core, core], [((9, C, 10 * WIDE), BF16)]
    )(
        top, halo, left, right, slope, mask, x_rows,
        *tops, *middles, lates[0], result, *moved, *moved_on,
    )
    terms, incoming = call(
        terms_kernel, [((NEAR * CHUNK, WIDE), BF16), ((C, 10 * WIDE), BF16)]
    )(first, second, slope, grad, x_cols)

    near, far = groups()
    parts = lax.all_to_all(
        terms.reshape(NEAR, CHUNK, WIDE), "space", 0, 0, axis_index_groups=near
    )
    parts, out = lax.optimization_barrier((parts, out))
    (out,) = call(
        last_kernel, [((C, CELLS), BF16)], [((9, C, 10 * WIDE), BF16), cols], leave=(0,)
    )(incoming, slope, mask, bwd, out)
    (copies,) = call(sum_kernel, [((FAR, CHUNK, WIDE), BF16)])(parts)
    parts = lax.all_to_all(copies, "space", 0, 0, axis_index_groups=far)
    parts, out = lax.optimization_barrier((parts, out))
    (copies,) = call(sum_kernel, [((NEAR, CHUNK, WIDE), BF16)])(parts)
    whole = lax.all_to_all(copies, "space", 0, 0, axis_index_groups=near)
    (weight_grad,) = call(scale_kernel, [((DEEP, C), F32)], leave=(0,))(
        whole.reshape(NEAR * CHUNK, WIDE)
    )
    return (out.reshape(1, 1, C, CELLS), weight_grad.reshape(1, TAPS, C, C))


def solution(mesh):
    return jax.shard_map(
        body,
        mesh=mesh,
        in_specs=(
            P("pipe", "space", None, None),
            P("space", None, None),
            P("pipe", None, None, None),
            P("space"),
        ),
        out_specs=(P("pipe", "space", None, None), P("pipe", None, None, None)),
        check_vma=False,
    )
```

```python
import functools

import jax
import jax.numpy as jnp
from jax import lax
from jax.experimental import pallas as pl
from jax.experimental.pallas import tpu as pltpu
from jax.sharding import PartitionSpec as P

C = 96
CELLS = 512
COLS = 8
ROWS = 16
SECTIONS = 4
TAPS = 27
DEEP = TAPS * C
WIDE = 128
CODE = 8
NEAR = 16
FAR = 8
CHUNK = 128
VMEM_BYTES = 32 * 1024 * 1024
F32 = jnp.float32
BF16 = jnp.bfloat16


def call(kernel, outs, scratch=(), leave=(), bring=True):
    shapes = [
        jax.ShapeDtypeStruct(shape, dtype) if n in leave else pltpu.VMEM(shape, dtype)
        for n, (shape, dtype) in enumerate(outs)
    ]

    def run(*args):
        inner = pl.pallas_call(
            kernel,
            out_shape=shapes,
            in_specs=[
                pl.BlockSpec(
                    memory_space=pltpu.SMEM if arg.dtype == jnp.int32
                    else pltpu.VMEM if bring else pl.ANY
                )
                for arg in args
            ],
            out_specs=[pl.BlockSpec(memory_space=pltpu.VMEM)] * len(shapes),
            scratch_shapes=[
                pltpu.VMEM(*item) if isinstance(item, tuple) else item for item in scratch
            ],
            compiler_params=pltpu.CompilerParams(vmem_limit_bytes=VMEM_BYTES),
        )
        return inner(
            *[
                arg if arg.dtype == jnp.int32
                else pltpu.with_memory_space_constraint(arg, pltpu.VMEM if bring else pltpu.HBM)
                for arg in args
            ]
        )

    return run


def lane(row, count=1):
    start = row * WIDE
    if not isinstance(start, int):
        start = pl.multiple_of(start, WIDE)
    return pl.ds(start, count * WIDE)


def turn(value, by):
    by = by % value.shape[1]
    return pltpu.roll(value, by, 1) if by else value


def shifted_rows(base_ref, row, tile, low=None, high=None):
    level = lax.broadcasted_iota(jnp.int32, (C, WIDE), 1) % 8
    for oy, source in ((-1, low), (0, None), (1, high)):
        source = tile if source is None else source
        for oz in (-1, 0, 1):
            if oz == 0:
                moved = turn(source, -8 * oy)
            elif oz > 0:
                moved = jnp.where(level < 7, turn(source, -8 * oy - 1), turn(source, -8 * oy + 7))
            else:
                moved = jnp.where(level > 0, turn(source, -8 * oy + 1), turn(source, -8 * oy - 7))
            base_ref[3 * (oy + 1) + oz + 1, :, lane(row)] = moved


def make_cols(cols_ref, base_ref, mask_ref, base_row, mask_row, at=0):
    for ox in (-1, 0, 1):
        for j in range(9):
            tap = 9 * (ox + 1) + j
            tile = base_ref[j, :, lane(base_row + ox, 2)].reshape(C // 16, 16, 2 * WIDE)
            kept = tile * mask_ref[tap, :, lane(mask_row, 2)][None]
            cols_ref[C * tap : C * tap + C, lane(at, 2)] = kept.reshape(C, 2 * WIDE)


def product(weight, cols):
    return lax.dot_general(
        weight, cols, (((1,), (0,)), ((), ())), preferred_element_type=F32
    )


def weight_kernel(w_ref, fwd_ref, bwd_ref):
    for q in range(TAPS):
        fwd_ref[:, C * q : C * q + C] = w_ref[q].T
        bwd_ref[:, C * q : C * q + C] = w_ref[TAPS - 1 - q]


OUTER = (1, 2, 3, 4, 13, 14, 15, 16)


def code_of(height_ref, shape):
    return jnp.full(shape, (height_ref[0] + CODE).astype(F32), F32)


def rows_kernel(x_hbm, top_hbm, height_ref, up_ref, down_ref, x_ref, top_ref, sems):
    x_copy = pltpu.make_async_copy(x_hbm, x_ref, sems.at[0])
    top_copy = pltpu.make_async_copy(top_hbm, top_ref, sems.at[1])
    x_copy.start()
    top_copy.start()
    x_copy.wait()
    top_copy.wait()
    lowest = lax.axis_index("pipe") == 0
    code = code_of(height_ref, (16, 3 * WIDE)).astype(BF16)
    spare = jnp.zeros((C, 64), BF16)
    up_ref[C:, :] = code
    down_ref[C:, :] = code
    up_ref[:C, :WIDE] = x_ref[:, 384:512]
    down_ref[:C, :WIDE] = x_ref[:, 0:128]

    @pl.when(lowest)
    def _():
        up_ref[:C, WIDE:] = top_ref[:, 256:512]
        down_ref[:C, WIDE:] = top_ref[:, 0:256]

    @pl.when(jnp.logical_not(lowest))
    def _():
        up_ref[:C, WIDE:] = jnp.concatenate([x_ref[:, 192:384], spare], 1)
        down_ref[:C, WIDE:] = jnp.concatenate([x_ref[:, 128:320], spare], 1)


def x_layer(x_ref, before_ref, after_ref, row):
    if row < 5:
        at = 64 * (row - 3) if row >= 3 else WIDE + 64 * row
        return before_ref[:C, at : at + 64]
    if row < 13:
        return x_ref[:, 64 * (row - 5) : 64 * (row - 5) + 64]
    at = 64 * (row - 13) if row < 15 else WIDE + 64 * (row - 15)
    return after_ref[:C, at : at + 64]


def top_layer(before_ref, after_ref, row):
    if row < 5:
        return before_ref[:C, WIDE + 64 * (row - 1) : WIDE + 64 * row]
    return after_ref[:C, WIDE + 64 * (row - 13) : WIDE + 64 * (row - 12)]


def join(parts):
    return jnp.concatenate(parts, 1)


def cols_kernel(x_ref, top_ref, height_ref, before_ref, after_ref, right_ref, left_ref):
    lowest = lax.axis_index("pipe") == 0
    codes = join(
        [before_ref[C:, :WIDE], code_of(height_ref, (16, WIDE)).astype(BF16), after_ref[C:, :WIDE]]
    )
    for out, start, fifth in ((right_ref, 32, 24), (left_ref, 0, 32)):

        def piece(layer, start=start):
            return layer[:, start : start + 32]

        out[C:, : 3 * WIDE] = codes
        out[C:, 3 * WIDE :] = jnp.zeros((16, 5 * WIDE), BF16)
        for four in range(3):
            rows = range(3 + 4 * four, 7 + 4 * four)
            out[:C, lane(four)] = join(
                [piece(x_layer(x_ref, before_ref, after_ref, row)) for row in rows]
            )

        @pl.when(lowest)
        def _(out=out, piece=piece):
            tops = [piece(top_layer(before_ref, after_ref, row)) for row in OUTER]
            out[:C, lane(3)] = join(tops[:4])
            out[:C, lane(4)] = join(tops[4:])
            out[:C, lane(5, 3)] = jnp.zeros((C, 3 * WIDE), BF16)

        @pl.when(jnp.logical_not(lowest))
        def _(out=out, piece=piece, fifth=fifth):
            outer = [
                piece(x_layer(x_ref, before_ref, after_ref, row)) for row in (0, 1, 2, 15, 16, 17)
            ]
            more = [
                x_layer(x_ref, before_ref, after_ref, row)[:, fifth : fifth + 8]
                for row in range(18)
            ]
            tops = [piece(top_ref[:, 64 * n : 64 * n + 64]) for n in range(8)]
            out[:C, lane(3)] = join(outer[:4])
            out[:C, lane(4)] = join(outer[4:] + more[:8])
            out[:C, lane(5)] = join(more[8:] + [jnp.zeros((C, 48), BF16)])
            out[:C, lane(6)] = join(tops[:4])
            out[:C, lane(7)] = join(tops[4:])


def x_side(side_ref, row):
    if 3 <= row < 15:
        at = 32 * (row - 3)
    else:
        at = 3 * WIDE + 32 * (row if row < 3 else row - 12)
    return side_ref[:C, at : at + 32]


def halo_kernel(before_ref, after_ref, left_ref, right_ref, halo_ref):
    @pl.when(lax.axis_index("pipe") == 0)
    def _():
        for n, row in enumerate(OUTER):
            at = 3 * WIDE + 32 * n
            middle = top_layer(before_ref, after_ref, row)
            sides = left_ref[:C, at : at + 32], right_ref[:C, at : at + 32]
            halo_ref[:, lane(n)] = join([sides[0], middle, sides[1]])


def forward_kernel(
    x_ref, height_ref, before_ref, after_ref, left_ref, right_ref, fwd_ref,
    slope_ref, mask_ref, rows_ref,
    base_ref, cols_ref, code_ref, pre_ref,
):
    where = lax.broadcasted_iota(jnp.int32, (8, WIDE), 1)
    middle = (
        before_ref[C : C + 8, :WIDE].astype(F32),
        code_of(height_ref, (8, WIDE)),
        after_ref[C : C + 8, :WIDE].astype(F32),
    )
    codes = []
    for n in range(3):
        left = left_ref[C : C + 8, lane(n)].astype(F32)
        right = right_ref[C : C + 8, lane(n)].astype(F32)
        codes.append(jnp.where(where < 32, left, jnp.where(where < 96, middle[n], right)))
    for row in range(18):
        code_ref[:, lane(row)] = codes[0 if row < 5 else 1 if row < 13 else 2]
    for row in range(18):
        tile = join(
            [
                x_side(left_ref, row),
                x_layer(x_ref, before_ref, after_ref, row),
                x_side(right_ref, row),
            ]
        )
        if 4 <= row < 14:
            rows_ref[:, lane(row - 4)] = tile
        at = 4 * WIDE + 64 + 8 * row
        low = join([tile[:, :120], left_ref[:C, at : at + 8]])
        high = join([right_ref[:C, at : at + 8], tile[:, 8:]])
        shifted_rows(base_ref, row, tile, low, high)

    level = lax.broadcasted_iota(jnp.int32, (8, WIDE), 1) % 8
    rise_of = {
        -1: jnp.where(level == 0, -1.0, 0.0),
        0: jnp.zeros((8, WIDE), F32),
        1: jnp.where(level == 7, 1.0, 0.0),
    }

    for rows in ((0, 1, 2), (3,), (4,), (5, 6, 7, 8, 9, 10), (11,), (12,), (13, 14, 15)):
        here = code_ref[:, lane(rows[0] + 1)]
        for ox in (-1, 0, 1):
            near = code_ref[:, lane(rows[0] + 1 + ox)]
            for oy in (-1, 0, 1):
                if oy < 0:
                    source = jnp.where(where >= 120, near[:, 0:1], near)
                elif oy > 0:
                    source = jnp.where(where < 8, near[:, 127:128], near)
                else:
                    source = near
                rise = turn(source, -8 * oy) - here
                for oz in (-1, 0, 1):
                    keep = jnp.where(rise == rise_of[oz], 1.0, 0.0)
                    keep = jnp.concatenate([keep, keep], 0).astype(BF16)
                    tap = 9 * (ox + 1) + 3 * (oy + 1) + oz + 1
                    for row in rows:
                        mask_ref[tap, :, lane(row)] = keep

    def forward(pair, carry):
        make_cols(cols_ref, base_ref, mask_ref, 2 * pair + 1, 2 * pair)
        pre_ref[:, lane(2 * pair, 2)] = product(fwd_ref[...], cols_ref[...])
        return carry

    lax.fori_loop(0, 8, forward, 0)
    for row in range(16):
        pre = pre_ref[:, lane(row)]
        sigma = 1.0 / (1.0 + jnp.exp(-pre))
        slope_ref[:, lane(row)] = sigma * (1.0 + pre * (1.0 - sigma))


def top_row(top_ref, halo_ref, left_ref, right_ref, row):
    if 5 <= row < 13:
        at, side = 64 * (row - 5), 6 * WIDE + 32 * (row - 5)
        tile = join(
            [
                left_ref[:C, side : side + 32],
                top_ref[:, at : at + 64],
                right_ref[:C, side : side + 32],
            ]
        )
    else:
        tile = halo_ref[:, lane(OUTER.index(row))]
    return jnp.where(lax.axis_index("pipe") == SECTIONS - 1, tile, jnp.zeros_like(tile))


def step_rows(incoming_ref, slope_ref, mask_ref, bwd_ref, base_ref, cols_ref, store, count, first):
    for row in range(count):
        grad = (
            incoming_ref[:, lane(row)].astype(F32) * slope_ref[:, lane(row + first - 1)]
        ).astype(BF16)
        shifted_rows(base_ref, row, grad)

    def backward(pair, carry):
        make_cols(cols_ref, base_ref, mask_ref, 2 * pair + 1, 2 * pair + first)
        total = incoming_ref[:, lane(2 * pair + 1, 2)].astype(F32) + product(
            bwd_ref[...], cols_ref[...]
        )
        store(pair, total.astype(BF16))
        return carry

    lax.fori_loop(0, (count - 2) // 2, backward, 0)


def spread(packed_ref, width, row):
    spare = jnp.zeros((C, (WIDE - width) // 2), BF16)
    return join([spare, packed_ref[:, width * row : width * row + width], spare])


TOP_PIECES = (2, 8, WIDE), (10, 6, WIDE)
MIDDLE_PIECES = (3, 6, 96), (9, 6, 96)
LATE_PIECES = (4, 4, 80), (8, 6, 80)


def pieces_row(pieces, row):
    for ref, first, count, width in pieces:
        if first <= row < first + count:
            if width == WIDE:
                return ref[:, lane(row - first)]
            return spread(ref, width, row - first)


def step_part(row_of, low, count, width, result_ref, slope_ref, mask_ref, bwd_ref, scratch):
    base_ref, cols_ref, rows_ref, full_ref = scratch
    for n in range(count + 2):
        rows_ref[:, lane(n)] = row_of(low - 1 + n)

    def store(pair, value):
        full_ref[:, lane(2 * pair, 2)] = value

    step_rows(
        rows_ref, slope_ref, mask_ref, bwd_ref, base_ref, cols_ref, store, count + 2, low - 1
    )
    skip = (WIDE - width) // 2
    packed = [full_ref[:, lane(n)][:, skip : skip + width] for n in range(count)]
    spare = result_ref.shape[1] - width * count
    result_ref[...] = join(packed + [jnp.zeros((C, spare), BF16)] if spare else packed)


def top_kernel(
    low, count, top_ref, halo_ref, left_ref, right_ref, slope_ref, mask_ref, bwd_ref,
    result_ref, *scratch,
):
    def row_of(row):
        return top_row(top_ref, halo_ref, left_ref, right_ref, row)

    step_part(row_of, low, count, WIDE, result_ref, slope_ref, mask_ref, bwd_ref, scratch)


def middle_kernel(pieces, low, count, width, *refs):
    given, refs = refs[: len(pieces)], refs[len(pieces) :]
    slope_ref, mask_ref, bwd_ref, result_ref, *scratch = refs

    def row_of(row):
        return pieces_row([(ref,) + piece for ref, piece in zip(given, pieces)], row)

    step_part(row_of, low, count, width, result_ref, slope_ref, mask_ref, bwd_ref, scratch)


def halves(first, second):
    where = lax.broadcasted_iota(jnp.int32, first.shape, 1)
    return jnp.where(where < 64, turn(first, -32), turn(second, 32))


def gather_kernel(
    top_ref, halo_ref, left_ref, right_ref, slope_ref, mask_ref, x_ref, *refs
):
    kinds = TOP_PIECES + MIDDLE_PIECES + LATE_PIECES
    pieces = [(ref,) + piece for ref, piece in zip(refs[:6], kinds)]
    incoming = [(ref,) + piece for ref, piece in zip(refs[6:10], TOP_PIECES + MIDDLE_PIECES)]
    all_ref, grad_ref, out_ref, base_ref = refs[10:]
    for n in range(8):
        row = n + 5
        scale = slope_ref[:, lane(n + 4)]
        tiles = (
            top_row(top_ref, halo_ref, left_ref, right_ref, row),
            pieces_row(incoming[:2], row),
            pieces_row(incoming[2:], row),
        )
        grads = [(tile.astype(F32) * scale).astype(BF16) for tile in tiles]
        grad_ref[:, lane(n)] = grads[0] + grads[1] + grads[2]
        outs = [pieces_row(pieces[at : at + 2], row) for at in (0, 2, 4)]
        out_ref[:, lane(n)] = outs[0] + outs[1] + outs[2]
    for row in range(10):
        shifted_rows(base_ref, row, x_ref[:, lane(row)])

    def one(pair, carry):
        for tap in range(TAPS):
            ox, j = tap // 9 - 1, tap % 9
            tiles = []
            for n in range(2):
                tile = base_ref[j, :, lane(2 * pair + 1 + n + ox)].reshape(C // 16, 16, WIDE)
                kept = tile * mask_ref[tap, :, lane(2 * pair + 4 + n)][None]
                tiles.append(kept.reshape(C, WIDE))
            all_ref[C * tap : C * tap + C, lane(pair)] = halves(*tiles)
        return carry

    lax.fori_loop(0, 4, one, 0)


def terms_kernel(
    first_ref, second_ref, slope_ref, grad_in, all_ref, terms_ref, incoming_ref
):
    for row in range(10):
        incoming_ref[:, lane(row)] = pieces_row(
            ((first_ref,) + LATE_PIECES[0], (second_ref,) + LATE_PIECES[1]), row + 4
        )
    grads = []
    for row in range(8):
        grad = incoming_ref[:, lane(row + 1)].astype(F32) * slope_ref[:, lane(row + 4)]
        grads.append(grad_in[:, lane(row)] + grad.astype(BF16))
    grads = join([halves(grads[2 * pair], grads[2 * pair + 1]) for pair in range(4)])
    for four in range(7):
        parts = []
        for tap in range(4 * four, 4 * four + 4):
            if tap < TAPS:
                part = lax.dot_general(
                    all_ref[C * tap : C * tap + C, :], grads, (((1,), (1,)), ((), ())),
                    preferred_element_type=F32,
                ).astype(BF16)
            else:
                part = jnp.zeros((C, C), BF16)
            parts.append(part)
        first, second, third, fourth = parts
        at = 3 * C * four
        terms_ref[at : at + C, :] = jnp.concatenate([first, second[:, :32]], 1)
        terms_ref[at + C : at + 2 * C, :] = jnp.concatenate([second[:, 32:], third[:, :64]], 1)
        terms_ref[at + 2 * C : at + 3 * C, :] = jnp.concatenate([third[:, 64:], fourth], 1)
    terms_ref[21 * C :, :] = jnp.zeros((NEAR * CHUNK - 21 * C, WIDE), BF16)


def last_kernel(
    incoming_ref, slope_ref, mask_ref, bwd_ref, out_in, out_ref, base_ref, cols_ref
):
    def store(pair, value):
        total = out_in[:, lane(2 * pair, 2)] + value
        out_ref[:, lane(pair)] = halves(total[:, :WIDE], total[:, WIDE:])

    step_rows(incoming_ref, slope_ref, mask_ref, bwd_ref, base_ref, cols_ref, store, 10, 4)


def sum_kernel(parts_ref, out_ref):
    total = parts_ref[0].astype(F32)
    for n in range(1, parts_ref.shape[0]):
        total = total + parts_ref[n].astype(F32)
    total = total.astype(BF16)
    for n in range(out_ref.shape[0]):
        out_ref[n] = total


def scale_kernel(whole_ref, out_ref):
    whole = whole_ref[...].astype(F32)
    scale = lax.rsqrt(jnp.sum(whole * whole) / (DEEP * C) + 1e-06)
    for four in range(7):
        at = 3 * C * four
        first, second, third = (whole_ref[at + n * C : at + n * C + C, :] for n in range(3))
        parts = (
            first[:, :96],
            jnp.concatenate([first[:, 96:], second[:, :64]], 1),
            jnp.concatenate([second[:, 64:], third[:, :32]], 1),
            third[:, 32:],
        )
        for n, tap in enumerate(range(4 * four, min(4 * four + 4, TAPS))):
            out_ref[C * tap : C * tap + C, :] = parts[n].astype(F32) * scale


def groups():
    def device(y, high, low, core):
        return y * 32 + (2 * high + low) * 2 + core

    kinds = [(y, low, core) for y in range(4) for low in range(2) for core in range(2)]
    near = [[device(y, high, low, core) for y, low, core in kinds] for high in range(FAR)]
    far = [[device(y, high, low, core) for high in range(FAR)] for y, low, core in kinds]
    return near, far


def body(section_input, top_grad, conv_weight, brick_height):
    both = ("space", "pipe")

    def between(by_row, by_col, sections):
        pairs = []
        for x in range(ROWS):
            for y in range(COLS):
                if 0 <= x + by_row < ROWS and 0 <= y + by_col < COLS:
                    source = x * COLS + y
                    target = (x + by_row) * COLS + y + by_col
                    for a, b in sections:
                        pairs.append((source * SECTIONS + a, target * SECTIONS + b))
        return pairs

    same = [(s, s) for s in range(SECTIONS)]
    x = section_input.reshape(C, CELLS)
    top = top_grad.reshape(C, CELLS)
    fwd, bwd = call(weight_kernel, [((C, DEEP), BF16)] * 2)(conv_weight[0])
    up, down, x, top = call(
        rows_kernel,
        [((C + 16, 3 * WIDE), BF16)] * 2 + [((C, CELLS), BF16)] * 2,
        [pltpu.SemaphoreType.DMA((2,))],
        bring=False,
    )(x, top, brick_height)
    before = lax.ppermute(up, both, between(1, 0, same))
    after = lax.ppermute(down, both, between(-1, 0, same))
    before, after, fwd, bwd = lax.optimization_barrier((before, after, fwd, bwd))
    to_right, to_left = call(cols_kernel, [((C + 16, 8 * WIDE), BF16)] * 2)(
        x, top, brick_height, before, after
    )
    left = lax.ppermute(to_right, both, between(0, 1, same))
    right = lax.ppermute(to_left, both, between(0, -1, same))
    (halo,) = call(halo_kernel, [((C, 8 * WIDE), BF16)])(before, after, left, right)
    halo = lax.ppermute(halo, both, between(0, 0, [(0, SECTIONS - 1)]))

    core = ((C, 8 * WIDE), BF16)
    cols = ((DEEP, 2 * WIDE), BF16)
    slope, mask, x_rows = call(
        forward_kernel,
        [((C, 16 * WIDE), F32), ((TAPS, 16, 16 * WIDE), BF16), ((C, 10 * WIDE), BF16)],
        [((9, C, 18 * WIDE), BF16), cols, ((8, 18 * WIDE), F32), ((C, 16 * WIDE), F32)],
    )(x, brick_height, before, after, left, right, fwd)
    def scratch(count):
        return [
            ((9, C, (count + 2) * WIDE), BF16), cols, ((C, (count + 2) * WIDE), BF16),
            ((C, count * WIDE), BF16),
        ]

    def hand_on(value, source):
        return lax.ppermute(value, both, between(0, 0, [(source, source - 1)]))

    def behind(kernel, count):
        return lambda *refs: kernel(*refs[:count], *refs[count + 1 :])

    def parts_of(kernels, args, pieces, source):
        made = []
        for kernel, given, (low, count, width) in zip(kernels, args, pieces):
            if made:
                kernel, given = behind(kernel, len(given)), given + (made[0][0],)
            lanes = -(-count * width // WIDE) * WIDE
            (result,) = call(kernel, [((C, lanes), BF16)], scratch(count))(*given)
            made.append((result, hand_on(result, source)))
        return [result for result, _ in made], [moved for _, moved in made]

    def middle(given, pieces, low, count, width):
        return functools.partial(middle_kernel, pieces[:given], low, count, width)

    rest = (slope, mask, bwd)
    tops, moved = parts_of(
        [functools.partial(top_kernel, low, count) for low, count, _ in TOP_PIECES],
        [(top, halo, left, right) + rest] * 2,
        TOP_PIECES,
        3,
    )
    middles, moved_on = parts_of(
        [middle(n + 1, TOP_PIECES, *MIDDLE_PIECES[n]) for n in range(2)],
        [tuple(moved[: n + 1]) + rest for n in range(2)],
        MIDDLE_PIECES,
        2,
    )
    lates, (first, second) = parts_of(
        [middle(n + 1, MIDDLE_PIECES, *LATE_PIECES[n]) for n in range(2)],
        [tuple(moved_on[: n + 1]) + rest for n in range(2)],
        LATE_PIECES,
        1,
    )
    x_rows, result = lax.optimization_barrier((x_rows, lates[1]))
    x_cols, grad, out = call(
        gather_kernel, [((DEEP, CELLS), BF16), core, core], [((9, C, 10 * WIDE), BF16)]
    )(
        top, halo, left, right, slope, mask, x_rows,
        *tops, *middles, lates[0], result, *moved, *moved_on,
    )
    terms, incoming = call(
        terms_kernel, [((NEAR * CHUNK, WIDE), BF16), ((C, 10 * WIDE), BF16)]
    )(first, second, slope, grad, x_cols)

    near, far = groups()
    parts = lax.all_to_all(
        terms.reshape(NEAR, CHUNK, WIDE), "space", 0, 0, axis_index_groups=near
    )
    parts, out = lax.optimization_barrier((parts, out))
    (out,) = call(
        last_kernel, [((C, CELLS), BF16)], [((9, C, 10 * WIDE), BF16), cols], leave=(0,)
    )(incoming, slope, mask, bwd, out)
    (copies,) = call(sum_kernel, [((FAR, CHUNK, WIDE), BF16)])(parts)
    parts = lax.all_to_all(copies, "space", 0, 0, axis_index_groups=far)
    parts, out = lax.optimization_barrier((parts, out))
    (copies,) = call(sum_kernel, [((NEAR, CHUNK, WIDE), BF16)])(parts)
    whole = lax.all_to_all(copies, "space", 0, 0, axis_index_groups=near)
    (weight_grad,) = call(scale_kernel, [((DEEP, C), F32)], leave=(0,))(
        whole.reshape(NEAR * CHUNK, WIDE)
    )
    return (out.reshape(1, 1, C, CELLS), weight_grad.reshape(1, TAPS, C, C))


def solution(mesh):
    return jax.shard_map(
        body,
        mesh=mesh,
        in_specs=(
            P("pipe", "space", None, None),
            P("space", None, None),
            P("pipe", None, None, None),
            P("space"),
        ),
        out_specs=(P("pipe", "space", None, None), P("pipe", None, None, None)),
        check_vma=False,
    )
```

```python
import functools

import jax
import jax.numpy as jnp
from jax import lax
from jax.experimental import pallas as pl
from jax.experimental.pallas import tpu as pltpu
from jax.sharding import PartitionSpec as P

C = 96
CELLS = 512
COLS = 8
ROWS = 16
SECTIONS = 4
TAPS = 27
DEEP = TAPS * C
WIDE = 128
CODE = 8
NEAR = 16
FAR = 8
CHUNK = 128
VMEM_BYTES = 32 * 1024 * 1024
F32 = jnp.float32
BF16 = jnp.bfloat16


def call(kernel, outs, scratch=(), leave=(), bring=True):
    shapes = [
        jax.ShapeDtypeStruct(shape, dtype) if n in leave else pltpu.VMEM(shape, dtype)
        for n, (shape, dtype) in enumerate(outs)
    ]

    def run(*args):
        inner = pl.pallas_call(
            kernel,
            out_shape=shapes,
            in_specs=[
                pl.BlockSpec(
                    memory_space=pltpu.SMEM if arg.dtype == jnp.int32
                    else pltpu.VMEM if bring else pl.ANY
                )
                for arg in args
            ],
            out_specs=[pl.BlockSpec(memory_space=pltpu.VMEM)] * len(shapes),
            scratch_shapes=[
                pltpu.VMEM(*item) if isinstance(item, tuple) else item for item in scratch
            ],
            compiler_params=pltpu.CompilerParams(vmem_limit_bytes=VMEM_BYTES),
        )
        return inner(
            *[
                arg if arg.dtype == jnp.int32
                else pltpu.with_memory_space_constraint(arg, pltpu.VMEM if bring else pltpu.HBM)
                for arg in args
            ]
        )

    return run


def lane(row, count=1):
    start = row * WIDE
    if not isinstance(start, int):
        start = pl.multiple_of(start, WIDE)
    return pl.ds(start, count * WIDE)


def turn(value, by):
    by = by % value.shape[1]
    return pltpu.roll(value, by, 1) if by else value


def shifted_rows(base_ref, row, tile, low=None, high=None):
    level = lax.broadcasted_iota(jnp.int32, (C, WIDE), 1) % 8
    for oy, source in ((-1, low), (0, None), (1, high)):
        source = tile if source is None else source
        for oz in (-1, 0, 1):
            if oz == 0:
                moved = turn(source, -8 * oy)
            elif oz > 0:
                moved = jnp.where(level < 7, turn(source, -8 * oy - 1), turn(source, -8 * oy + 7))
            else:
                moved = jnp.where(level > 0, turn(source, -8 * oy + 1), turn(source, -8 * oy - 7))
            base_ref[3 * (oy + 1) + oz + 1, :, lane(row)] = moved


def make_cols(cols_ref, base_ref, mask_ref, base_row, mask_row, at=0):
    for ox in (-1, 0, 1):
        for j in range(9):
            tap = 9 * (ox + 1) + j
            tile = base_ref[j, :, lane(base_row + ox, 2)].reshape(C // 16, 16, 2 * WIDE)
            kept = tile * mask_ref[tap, :, lane(mask_row, 2)][None]
            cols_ref[C * tap : C * tap + C, lane(at, 2)] = kept.reshape(C, 2 * WIDE)


def product(weight, cols):
    return lax.dot_general(
        weight, cols, (((1,), (0,)), ((), ())), preferred_element_type=F32
    )


def weight_kernel(w_ref, fwd_ref, bwd_ref):
    for q in range(TAPS):
        fwd_ref[:, C * q : C * q + C] = w_ref[q].T
        bwd_ref[:, C * q : C * q + C] = w_ref[TAPS - 1 - q]


OUTER = (1, 2, 3, 4, 13, 14, 15, 16)


def code_of(height_ref, shape):
    return jnp.full(shape, (height_ref[0] + CODE).astype(F32), F32)


def rows_kernel(x_hbm, top_hbm, height_ref, up_ref, down_ref, x_ref, top_ref, sems):
    x_copy = pltpu.make_async_copy(x_hbm, x_ref, sems.at[0])
    top_copy = pltpu.make_async_copy(top_hbm, top_ref, sems.at[1])
    x_copy.start()
    top_copy.start()
    x_copy.wait()
    top_copy.wait()
    lowest = lax.axis_index("pipe") == 0
    code = code_of(height_ref, (16, 3 * WIDE)).astype(BF16)
    spare = jnp.zeros((C, 64), BF16)
    up_ref[C:, :] = code
    down_ref[C:, :] = code
    up_ref[:C, :WIDE] = x_ref[:, 384:512]
    down_ref[:C, :WIDE] = x_ref[:, 0:128]

    @pl.when(lowest)
    def _():
        up_ref[:C, WIDE:] = top_ref[:, 256:512]
        down_ref[:C, WIDE:] = top_ref[:, 0:256]

    @pl.when(jnp.logical_not(lowest))
    def _():
        up_ref[:C, WIDE:] = jnp.concatenate([x_ref[:, 192:384], spare], 1)
        down_ref[:C, WIDE:] = jnp.concatenate([x_ref[:, 128:320], spare], 1)


def x_layer(x_ref, before_ref, after_ref, row):
    if row < 5:
        at = 64 * (row - 3) if row >= 3 else WIDE + 64 * row
        return before_ref[:C, at : at + 64]
    if row < 13:
        return x_ref[:, 64 * (row - 5) : 64 * (row - 5) + 64]
    at = 64 * (row - 13) if row < 15 else WIDE + 64 * (row - 15)
    return after_ref[:C, at : at + 64]


def top_layer(before_ref, after_ref, row):
    if row < 5:
        return before_ref[:C, WIDE + 64 * (row - 1) : WIDE + 64 * row]
    return after_ref[:C, WIDE + 64 * (row - 13) : WIDE + 64 * (row - 12)]


def join(parts):
    return jnp.concatenate(parts, 1)


def cols_kernel(x_ref, top_ref, height_ref, before_ref, after_ref, right_ref, left_ref):
    lowest = lax.axis_index("pipe") == 0
    codes = join(
        [before_ref[C:, :WIDE], code_of(height_ref, (16, WIDE)).astype(BF16), after_ref[C:, :WIDE]]
    )
    for out, start, fifth in ((right_ref, 32, 24), (left_ref, 0, 32)):

        def piece(layer, start=start):
            return layer[:, start : start + 32]

        out[C:, : 3 * WIDE] = codes
        out[C:, 3 * WIDE :] = jnp.zeros((16, 5 * WIDE), BF16)
        for four in range(3):
            rows = range(3 + 4 * four, 7 + 4 * four)
            out[:C, lane(four)] = join(
                [piece(x_layer(x_ref, before_ref, after_ref, row)) for row in rows]
            )

        @pl.when(lowest)
        def _(out=out, piece=piece):
            tops = [piece(top_layer(before_ref, after_ref, row)) for row in OUTER]
            out[:C, lane(3)] = join(tops[:4])
            out[:C, lane(4)] = join(tops[4:])
            out[:C, lane(5, 3)] = jnp.zeros((C, 3 * WIDE), BF16)

        @pl.when(jnp.logical_not(lowest))
        def _(out=out, piece=piece, fifth=fifth):
            outer = [
                piece(x_layer(x_ref, before_ref, after_ref, row)) for row in (0, 1, 2, 15, 16, 17)
            ]
            more = [
                x_layer(x_ref, before_ref, after_ref, row)[:, fifth : fifth + 8]
                for row in range(18)
            ]
            tops = [piece(top_ref[:, 64 * n : 64 * n + 64]) for n in range(8)]
            out[:C, lane(3)] = join(outer[:4])
            out[:C, lane(4)] = join(outer[4:] + more[:8])
            out[:C, lane(5)] = join(more[8:] + [jnp.zeros((C, 48), BF16)])
            out[:C, lane(6)] = join(tops[:4])
            out[:C, lane(7)] = join(tops[4:])


def x_side(side_ref, row):
    if 3 <= row < 15:
        at = 32 * (row - 3)
    else:
        at = 3 * WIDE + 32 * (row if row < 3 else row - 12)
    return side_ref[:C, at : at + 32]


def halo_kernel(before_ref, after_ref, left_ref, right_ref, halo_ref):
    @pl.when(lax.axis_index("pipe") == 0)
    def _():
        for n, row in enumerate(OUTER):
            at = 3 * WIDE + 32 * n
            middle = top_layer(before_ref, after_ref, row)
            sides = left_ref[:C, at : at + 32], right_ref[:C, at : at + 32]
            halo_ref[:, lane(n)] = join([sides[0], middle, sides[1]])


def forward_kernel(
    x_ref, height_ref, before_ref, after_ref, left_ref, right_ref, fwd_ref,
    slope_ref, mask_ref, rows_ref,
    base_ref, cols_ref, code_ref, pre_ref,
):
    where = lax.broadcasted_iota(jnp.int32, (8, WIDE), 1)
    middle = (
        before_ref[C : C + 8, :WIDE].astype(F32),
        code_of(height_ref, (8, WIDE)),
        after_ref[C : C + 8, :WIDE].astype(F32),
    )
    codes = []
    for n in range(3):
        left = left_ref[C : C + 8, lane(n)].astype(F32)
        right = right_ref[C : C + 8, lane(n)].astype(F32)
        codes.append(jnp.where(where < 32, left, jnp.where(where < 96, middle[n], right)))
    for row in range(18):
        code_ref[:, lane(row)] = codes[0 if row < 5 else 1 if row < 13 else 2]
    for row in range(18):
        tile = join(
            [
                x_side(left_ref, row),
                x_layer(x_ref, before_ref, after_ref, row),
                x_side(right_ref, row),
            ]
        )
        if 4 <= row < 14:
            rows_ref[:, lane(row - 4)] = tile
        at = 4 * WIDE + 64 + 8 * row
        low = join([tile[:, :120], left_ref[:C, at : at + 8]])
        high = join([right_ref[:C, at : at + 8], tile[:, 8:]])
        shifted_rows(base_ref, row, tile, low, high)

    level = lax.broadcasted_iota(jnp.int32, (8, WIDE), 1) % 8
    rise_of = {
        -1: jnp.where(level == 0, -1.0, 0.0),
        0: jnp.zeros((8, WIDE), F32),
        1: jnp.where(level == 7, 1.0, 0.0),
    }

    for rows in ((0, 1, 2), (3,), (4,), (5, 6, 7, 8, 9, 10), (11,), (12,), (13, 14, 15)):
        here = code_ref[:, lane(rows[0] + 1)]
        for ox in (-1, 0, 1):
            near = code_ref[:, lane(rows[0] + 1 + ox)]
            for oy in (-1, 0, 1):
                if oy < 0:
                    source = jnp.where(where >= 120, near[:, 0:1], near)
                elif oy > 0:
                    source = jnp.where(where < 8, near[:, 127:128], near)
                else:
                    source = near
                rise = turn(source, -8 * oy) - here
                for oz in (-1, 0, 1):
                    keep = jnp.where(rise == rise_of[oz], 1.0, 0.0)
                    keep = jnp.concatenate([keep, keep], 0).astype(BF16)
                    tap = 9 * (ox + 1) + 3 * (oy + 1) + oz + 1
                    for row in rows:
                        mask_ref[tap, :, lane(row)] = keep

    for pair in range(8):
        make_cols(cols_ref, base_ref, mask_ref, 2 * pair + 1, 2 * pair, 2 * pair)
    pre_ref[...] = product(fwd_ref[...], cols_ref[...])
    for row in range(16):
        pre = pre_ref[:, lane(row)]
        sigma = 1.0 / (1.0 + jnp.exp(-pre))
        slope_ref[:, lane(row)] = sigma * (1.0 + pre * (1.0 - sigma))


def top_row(top_ref, halo_ref, left_ref, right_ref, row):
    if 5 <= row < 13:
        at, side = 64 * (row - 5), 6 * WIDE + 32 * (row - 5)
        tile = join(
            [
                left_ref[:C, side : side + 32],
                top_ref[:, at : at + 64],
                right_ref[:C, side : side + 32],
            ]
        )
    else:
        tile = halo_ref[:, lane(OUTER.index(row))]
    return jnp.where(lax.axis_index("pipe") == SECTIONS - 1, tile, jnp.zeros_like(tile))


def step_rows(incoming_ref, slope_ref, mask_ref, bwd_ref, base_ref, cols_ref, store, count, first):
    for row in range(count):
        grad = (
            incoming_ref[:, lane(row)].astype(F32) * slope_ref[:, lane(row + first - 1)]
        ).astype(BF16)
        shifted_rows(base_ref, row, grad)

    for pair in range((count - 2) // 2):
        make_cols(cols_ref, base_ref, mask_ref, 2 * pair + 1, 2 * pair + first, 2 * pair)
    rows = lane(1, count - 2)
    total = incoming_ref[:, rows].astype(F32) + product(bwd_ref[...], cols_ref[...])
    for pair in range((count - 2) // 2):
        store(pair, total[:, 2 * pair * WIDE : 2 * (pair + 1) * WIDE].astype(BF16))


def spread(packed_ref, width, row):
    spare = jnp.zeros((C, (WIDE - width) // 2), BF16)
    return join([spare, packed_ref[:, width * row : width * row + width], spare])


TOP_PIECES = (2, 8, WIDE), (10, 6, WIDE)
MIDDLE_PIECES = (3, 6, 96), (9, 6, 96)
LATE_PIECES = (4, 4, 80), (8, 6, 80)


def pieces_row(pieces, row):
    for ref, first, count, width in pieces:
        if first <= row < first + count:
            if width == WIDE:
                return ref[:, lane(row - first)]
            return spread(ref, width, row - first)


def step_part(row_of, low, count, width, result_ref, slope_ref, mask_ref, bwd_ref, scratch):
    base_ref, cols_ref, rows_ref, full_ref = scratch
    for n in range(count + 2):
        rows_ref[:, lane(n)] = row_of(low - 1 + n)

    def store(pair, value):
        full_ref[:, lane(2 * pair, 2)] = value

    step_rows(
        rows_ref, slope_ref, mask_ref, bwd_ref, base_ref, cols_ref, store, count + 2, low - 1
    )
    skip = (WIDE - width) // 2
    packed = [full_ref[:, lane(n)][:, skip : skip + width] for n in range(count)]
    spare = result_ref.shape[1] - width * count
    result_ref[...] = join(packed + [jnp.zeros((C, spare), BF16)] if spare else packed)


def top_kernel(
    low, count, top_ref, halo_ref, left_ref, right_ref, slope_ref, mask_ref, bwd_ref,
    result_ref, *scratch,
):
    def row_of(row):
        return top_row(top_ref, halo_ref, left_ref, right_ref, row)

    step_part(row_of, low, count, WIDE, result_ref, slope_ref, mask_ref, bwd_ref, scratch)


def middle_kernel(pieces, low, count, width, *refs):
    given, refs = refs[: len(pieces)], refs[len(pieces) :]
    slope_ref, mask_ref, bwd_ref, result_ref, *scratch = refs

    def row_of(row):
        return pieces_row([(ref,) + piece for ref, piece in zip(given, pieces)], row)

    step_part(row_of, low, count, width, result_ref, slope_ref, mask_ref, bwd_ref, scratch)


def halves(first, second):
    where = lax.broadcasted_iota(jnp.int32, first.shape, 1)
    return jnp.where(where < 64, turn(first, -32), turn(second, 32))


def gather_kernel(
    top_ref, halo_ref, left_ref, right_ref, slope_ref, mask_ref, x_ref, *refs
):
    kinds = TOP_PIECES + MIDDLE_PIECES + LATE_PIECES
    pieces = [(ref,) + piece for ref, piece in zip(refs[:6], kinds)]
    incoming = [(ref,) + piece for ref, piece in zip(refs[6:10], TOP_PIECES + MIDDLE_PIECES)]
    all_ref, grad_ref, out_ref, base_ref = refs[10:]
    for n in range(8):
        row = n + 5
        scale = slope_ref[:, lane(n + 4)]
        tiles = (
            top_row(top_ref, halo_ref, left_ref, right_ref, row),
            pieces_row(incoming[:2], row),
            pieces_row(incoming[2:], row),
        )
        grads = [(tile.astype(F32) * scale).astype(BF16) for tile in tiles]
        grad_ref[:, lane(n)] = grads[0] + grads[1] + grads[2]
        outs = [pieces_row(pieces[at : at + 2], row) for at in (0, 2, 4)]
        out_ref[:, lane(n)] = outs[0] + outs[1] + outs[2]
    for row in range(10):
        shifted_rows(base_ref, row, x_ref[:, lane(row)])

    def one(pair, carry):
        for tap in range(TAPS):
            ox, j = tap // 9 - 1, tap % 9
            tiles = []
            for n in range(2):
                tile = base_ref[j, :, lane(2 * pair + 1 + n + ox)].reshape(C // 16, 16, WIDE)
                kept = tile * mask_ref[tap, :, lane(2 * pair + 4 + n)][None]
                tiles.append(kept.reshape(C, WIDE))
            all_ref[C * tap : C * tap + C, lane(pair)] = halves(*tiles)
        return carry

    lax.fori_loop(0, 4, one, 0)


def terms_kernel(
    first_ref, second_ref, slope_ref, grad_in, all_ref, terms_ref, incoming_ref
):
    for row in range(10):
        incoming_ref[:, lane(row)] = pieces_row(
            ((first_ref,) + LATE_PIECES[0], (second_ref,) + LATE_PIECES[1]), row + 4
        )
    grads = []
    for row in range(8):
        grad = incoming_ref[:, lane(row + 1)].astype(F32) * slope_ref[:, lane(row + 4)]
        grads.append(grad_in[:, lane(row)] + grad.astype(BF16))
    grads = join([halves(grads[2 * pair], grads[2 * pair + 1]) for pair in range(4)])
    for four in range(7):
        parts = []
        for tap in range(4 * four, 4 * four + 4):
            if tap < TAPS:
                part = lax.dot_general(
                    all_ref[C * tap : C * tap + C, :], grads, (((1,), (1,)), ((), ())),
                    preferred_element_type=F32,
                ).astype(BF16)
            else:
                part = jnp.zeros((C, C), BF16)
            parts.append(part)
        first, second, third, fourth = parts
        at = 3 * C * four
        terms_ref[at : at + C, :] = jnp.concatenate([first, second[:, :32]], 1)
        terms_ref[at + C : at + 2 * C, :] = jnp.concatenate([second[:, 32:], third[:, :64]], 1)
        terms_ref[at + 2 * C : at + 3 * C, :] = jnp.concatenate([third[:, 64:], fourth], 1)
    terms_ref[21 * C :, :] = jnp.zeros((NEAR * CHUNK - 21 * C, WIDE), BF16)


def last_kernel(
    incoming_ref, slope_ref, mask_ref, bwd_ref, out_in, out_ref, base_ref, cols_ref
):
    def store(pair, value):
        total = out_in[:, lane(2 * pair, 2)] + value
        out_ref[:, lane(pair)] = halves(total[:, :WIDE], total[:, WIDE:])

    step_rows(incoming_ref, slope_ref, mask_ref, bwd_ref, base_ref, cols_ref, store, 10, 4)


def sum_kernel(parts_ref, out_ref):
    total = parts_ref[0].astype(F32)
    for n in range(1, parts_ref.shape[0]):
        total = total + parts_ref[n].astype(F32)
    total = total.astype(BF16)
    for n in range(out_ref.shape[0]):
        out_ref[n] = total


def scale_kernel(whole_ref, out_ref):
    whole = whole_ref[...].astype(F32)
    scale = lax.rsqrt(jnp.sum(whole * whole) / (DEEP * C) + 1e-06)
    for four in range(7):
        at = 3 * C * four
        first, second, third = (whole_ref[at + n * C : at + n * C + C, :] for n in range(3))
        parts = (
            first[:, :96],
            jnp.concatenate([first[:, 96:], second[:, :64]], 1),
            jnp.concatenate([second[:, 64:], third[:, :32]], 1),
            third[:, 32:],
        )
        for n, tap in enumerate(range(4 * four, min(4 * four + 4, TAPS))):
            out_ref[C * tap : C * tap + C, :] = parts[n].astype(F32) * scale


def groups():
    def device(y, high, low, core):
        return y * 32 + (2 * high + low) * 2 + core

    kinds = [(y, low, core) for y in range(4) for low in range(2) for core in range(2)]
    near = [[device(y, high, low, core) for y, low, core in kinds] for high in range(FAR)]
    far = [[device(y, high, low, core) for high in range(FAR)] for y, low, core in kinds]
    return near, far


def body(section_input, top_grad, conv_weight, brick_height):
    both = ("space", "pipe")

    def between(by_row, by_col, sections):
        pairs = []
        for x in range(ROWS):
            for y in range(COLS):
                if 0 <= x + by_row < ROWS and 0 <= y + by_col < COLS:
                    source = x * COLS + y
                    target = (x + by_row) * COLS + y + by_col
                    for a, b in sections:
                        pairs.append((source * SECTIONS + a, target * SECTIONS + b))
        return pairs

    same = [(s, s) for s in range(SECTIONS)]
    x = section_input.reshape(C, CELLS)
    top = top_grad.reshape(C, CELLS)
    fwd, bwd = call(weight_kernel, [((C, DEEP), BF16)] * 2)(conv_weight[0])
    up, down, x, top = call(
        rows_kernel,
        [((C + 16, 3 * WIDE), BF16)] * 2 + [((C, CELLS), BF16)] * 2,
        [pltpu.SemaphoreType.DMA((2,))],
        bring=False,
    )(x, top, brick_height)
    before = lax.ppermute(up, both, between(1, 0, same))
    after = lax.ppermute(down, both, between(-1, 0, same))
    before, after, fwd, bwd = lax.optimization_barrier((before, after, fwd, bwd))
    to_right, to_left = call(cols_kernel, [((C + 16, 8 * WIDE), BF16)] * 2)(
        x, top, brick_height, before, after
    )
    left = lax.ppermute(to_right, both, between(0, 1, same))
    right = lax.ppermute(to_left, both, between(0, -1, same))
    (halo,) = call(halo_kernel, [((C, 8 * WIDE), BF16)])(before, after, left, right)
    halo = lax.ppermute(halo, both, between(0, 0, [(0, SECTIONS - 1)]))

    core = ((C, 8 * WIDE), BF16)
    slope, mask, x_rows = call(
        forward_kernel,
        [((C, 16 * WIDE), F32), ((TAPS, 16, 16 * WIDE), BF16), ((C, 10 * WIDE), BF16)],
        [((9, C, 18 * WIDE), BF16), ((DEEP, 16 * WIDE), BF16), ((8, 18 * WIDE), F32),
         ((C, 16 * WIDE), F32)],
    )(x, brick_height, before, after, left, right, fwd)
    def scratch(count):
        return [
            ((9, C, (count + 2) * WIDE), BF16), ((DEEP, count * WIDE), BF16),
            ((C, (count + 2) * WIDE), BF16),
            ((C, count * WIDE), BF16),
        ]

    def hand_on(value, source):
        return lax.ppermute(value, both, between(0, 0, [(source, source - 1)]))

    def behind(kernel, count):
        return lambda *refs: kernel(*refs[:count], *refs[count + 1 :])

    def parts_of(kernels, args, pieces, source):
        made = []
        for kernel, given, (low, count, width) in zip(kernels, args, pieces):
            if made:
                kernel, given = behind(kernel, len(given)), given + (made[0][0],)
            lanes = -(-count * width // WIDE) * WIDE
            (result,) = call(kernel, [((C, lanes), BF16)], scratch(count))(*given)
            made.append((result, hand_on(result, source)))
        return [result for result, _ in made], [moved for _, moved in made]

    def middle(given, pieces, low, count, width):
        return functools.partial(middle_kernel, pieces[:given], low, count, width)

    rest = (slope, mask, bwd)
    tops, moved = parts_of(
        [functools.partial(top_kernel, low, count) for low, count, _ in TOP_PIECES],
        [(top, halo, left, right) + rest] * 2,
        TOP_PIECES,
        3,
    )
    middles, moved_on = parts_of(
        [middle(n + 1, TOP_PIECES, *MIDDLE_PIECES[n]) for n in range(2)],
        [tuple(moved[: n + 1]) + rest for n in range(2)],
        MIDDLE_PIECES,
        2,
    )
    lates, (first, second) = parts_of(
        [middle(n + 1, MIDDLE_PIECES, *LATE_PIECES[n]) for n in range(2)],
        [tuple(moved_on[: n + 1]) + rest for n in range(2)],
        LATE_PIECES,
        1,
    )
    x_rows, result = lax.optimization_barrier((x_rows, lates[1]))
    x_cols, grad, out = call(
        gather_kernel, [((DEEP, CELLS), BF16), core, core], [((9, C, 10 * WIDE), BF16)]
    )(
        top, halo, left, right, slope, mask, x_rows,
        *tops, *middles, lates[0], result, *moved, *moved_on,
    )
    terms, incoming = call(
        terms_kernel, [((NEAR * CHUNK, WIDE), BF16), ((C, 10 * WIDE), BF16)]
    )(first, second, slope, grad, x_cols)

    near, far = groups()
    parts = lax.all_to_all(
        terms.reshape(NEAR, CHUNK, WIDE), "space", 0, 0, axis_index_groups=near
    )
    parts, out = lax.optimization_barrier((parts, out))
    (out,) = call(
        last_kernel,
        [((C, CELLS), BF16)],
        [((9, C, 10 * WIDE), BF16), ((DEEP, 8 * WIDE), BF16)],
        leave=(0,),
    )(incoming, slope, mask, bwd, out)
    (copies,) = call(sum_kernel, [((FAR, CHUNK, WIDE), BF16)])(parts)
    parts = lax.all_to_all(copies, "space", 0, 0, axis_index_groups=far)
    parts, out = lax.optimization_barrier((parts, out))
    (copies,) = call(sum_kernel, [((NEAR, CHUNK, WIDE), BF16)])(parts)
    whole = lax.all_to_all(copies, "space", 0, 0, axis_index_groups=near)
    (weight_grad,) = call(scale_kernel, [((DEEP, C), F32)], leave=(0,))(
        whole.reshape(NEAR * CHUNK, WIDE)
    )
    return (out.reshape(1, 1, C, CELLS), weight_grad.reshape(1, TAPS, C, C))


def solution(mesh):
    return jax.shard_map(
        body,
        mesh=mesh,
        in_specs=(
            P("pipe", "space", None, None),
            P("space", None, None),
            P("pipe", None, None, None),
            P("space"),
        ),
        out_specs=(P("pipe", "space", None, None), P("pipe", None, None, None)),
        check_vma=False,
    )
```

```python
import functools

import jax
import jax.numpy as jnp
from jax import lax
from jax.experimental import pallas as pl
from jax.experimental.pallas import tpu as pltpu
from jax.sharding import PartitionSpec as P

C = 96
CELLS = 512
COLS = 8
ROWS = 16
SECTIONS = 4
TAPS = 27
DEEP = TAPS * C
WIDE = 128
CODE = 8
NEAR = 16
FAR = 8
CHUNK = 128
VMEM_BYTES = 32 * 1024 * 1024
F32 = jnp.float32
BF16 = jnp.bfloat16


def call(kernel, outs, scratch=(), leave=(), bring=True):
    shapes = [
        jax.ShapeDtypeStruct(shape, dtype) if n in leave else pltpu.VMEM(shape, dtype)
        for n, (shape, dtype) in enumerate(outs)
    ]

    def run(*args):
        inner = pl.pallas_call(
            kernel,
            out_shape=shapes,
            in_specs=[
                pl.BlockSpec(
                    memory_space=pltpu.SMEM if arg.dtype == jnp.int32
                    else pltpu.VMEM if bring else pl.ANY
                )
                for arg in args
            ],
            out_specs=[pl.BlockSpec(memory_space=pltpu.VMEM)] * len(shapes),
            scratch_shapes=[
                pltpu.VMEM(*item) if isinstance(item, tuple) else item for item in scratch
            ],
            compiler_params=pltpu.CompilerParams(vmem_limit_bytes=VMEM_BYTES),
        )
        return inner(
            *[
                arg if arg.dtype == jnp.int32
                else pltpu.with_memory_space_constraint(arg, pltpu.VMEM if bring else pltpu.HBM)
                for arg in args
            ]
        )

    return run


def lane(row, count=1):
    start = row * WIDE
    if not isinstance(start, int):
        start = pl.multiple_of(start, WIDE)
    return pl.ds(start, count * WIDE)


def turn(value, by):
    by = by % value.shape[1]
    return pltpu.roll(value, by, 1) if by else value


def shifted_rows(base_ref, row, tile, low=None, high=None):
    level = lax.broadcasted_iota(jnp.int32, (C, WIDE), 1) % 8
    for oy, source in ((-1, low), (0, None), (1, high)):
        source = tile if source is None else source
        for oz in (-1, 0, 1):
            if oz == 0:
                moved = turn(source, -8 * oy)
            elif oz > 0:
                moved = jnp.where(level < 7, turn(source, -8 * oy - 1), turn(source, -8 * oy + 7))
            else:
                moved = jnp.where(level > 0, turn(source, -8 * oy + 1), turn(source, -8 * oy - 7))
            base_ref[3 * (oy + 1) + oz + 1, :, lane(row)] = moved


def make_cols(cols_ref, base_ref, mask_ref, base_row, mask_row, at=0):
    for ox in (-1, 0, 1):
        for j in range(9):
            tap = 9 * (ox + 1) + j
            tile = base_ref[j, :, lane(base_row + ox, 2)].reshape(C // 16, 16, 2 * WIDE)
            kept = tile * mask_ref[tap, :, lane(mask_row, 2)][None]
            cols_ref[C * tap : C * tap + C, lane(at, 2)] = kept.reshape(C, 2 * WIDE)


def product(weight, cols):
    return lax.dot_general(
        weight, cols, (((1,), (0,)), ((), ())), preferred_element_type=F32
    )


def weight_kernel(w_ref, fwd_ref, bwd_ref):
    for q in range(TAPS):
        fwd_ref[:, C * q : C * q + C] = w_ref[q].T
        bwd_ref[:, C * q : C * q + C] = w_ref[TAPS - 1 - q]


OUTER = (1, 2, 3, 4, 13, 14, 15, 16)


def code_of(height_ref, shape):
    return jnp.full(shape, (height_ref[0] + CODE).astype(F32), F32)


def rows_kernel(x_hbm, top_hbm, height_ref, up_ref, down_ref, x_ref, top_ref, sems):
    x_copy = pltpu.make_async_copy(x_hbm, x_ref, sems.at[0])
    top_copy = pltpu.make_async_copy(top_hbm, top_ref, sems.at[1])
    x_copy.start()
    top_copy.start()
    x_copy.wait()
    top_copy.wait()
    lowest = lax.axis_index("pipe") == 0
    code = code_of(height_ref, (16, 3 * WIDE)).astype(BF16)
    spare = jnp.zeros((C, 64), BF16)
    up_ref[C:, :] = code
    down_ref[C:, :] = code
    up_ref[:C, :WIDE] = x_ref[:, 384:512]
    down_ref[:C, :WIDE] = x_ref[:, 0:128]

    @pl.when(lowest)
    def _():
        up_ref[:C, WIDE:] = top_ref[:, 256:512]
        down_ref[:C, WIDE:] = top_ref[:, 0:256]

    @pl.when(jnp.logical_not(lowest))
    def _():
        up_ref[:C, WIDE:] = jnp.concatenate([x_ref[:, 192:384], spare], 1)
        down_ref[:C, WIDE:] = jnp.concatenate([x_ref[:, 128:320], spare], 1)


def x_layer(x_ref, before_ref, after_ref, row):
    if row < 5:
        at = 64 * (row - 3) if row >= 3 else WIDE + 64 * row
        return before_ref[:C, at : at + 64]
    if row < 13:
        return x_ref[:, 64 * (row - 5) : 64 * (row - 5) + 64]
    at = 64 * (row - 13) if row < 15 else WIDE + 64 * (row - 15)
    return after_ref[:C, at : at + 64]


def top_layer(before_ref, after_ref, row):
    if row < 5:
        return before_ref[:C, WIDE + 64 * (row - 1) : WIDE + 64 * row]
    return after_ref[:C, WIDE + 64 * (row - 13) : WIDE + 64 * (row - 12)]


def join(parts):
    return jnp.concatenate(parts, 1)


def cols_kernel(x_ref, top_ref, height_ref, before_ref, after_ref, right_ref, left_ref):
    lowest = lax.axis_index("pipe") == 0
    codes = join(
        [before_ref[C:, :WIDE], code_of(height_ref, (16, WIDE)).astype(BF16), after_ref[C:, :WIDE]]
    )
    for out, start, fifth in ((right_ref, 32, 24), (left_ref, 0, 32)):

        def piece(layer, start=start):
            return layer[:, start : start + 32]

        out[C:, : 3 * WIDE] = codes
        out[C:, 3 * WIDE :] = jnp.zeros((16, 5 * WIDE), BF16)
        for four in range(3):
            rows = range(3 + 4 * four, 7 + 4 * four)
            out[:C, lane(four)] = join(
                [piece(x_layer(x_ref, before_ref, after_ref, row)) for row in rows]
            )

        @pl.when(lowest)
        def _(out=out, piece=piece):
            tops = [piece(top_layer(before_ref, after_ref, row)) for row in OUTER]
            out[:C, lane(3)] = join(tops[:4])
            out[:C, lane(4)] = join(tops[4:])
            out[:C, lane(5, 3)] = jnp.zeros((C, 3 * WIDE), BF16)

        @pl.when(jnp.logical_not(lowest))
        def _(out=out, piece=piece, fifth=fifth):
            outer = [
                piece(x_layer(x_ref, before_ref, after_ref, row)) for row in (0, 1, 2, 15, 16, 17)
            ]
            more = [
                x_layer(x_ref, before_ref, after_ref, row)[:, fifth : fifth + 8]
                for row in range(18)
            ]
            tops = [piece(top_ref[:, 64 * n : 64 * n + 64]) for n in range(8)]
            out[:C, lane(3)] = join(outer[:4])
            out[:C, lane(4)] = join(outer[4:] + more[:8])
            out[:C, lane(5)] = join(more[8:] + [jnp.zeros((C, 48), BF16)])
            out[:C, lane(6)] = join(tops[:4])
            out[:C, lane(7)] = join(tops[4:])


def x_side(side_ref, row):
    if 3 <= row < 15:
        at = 32 * (row - 3)
    else:
        at = 3 * WIDE + 32 * (row if row < 3 else row - 12)
    return side_ref[:C, at : at + 32]


def halo_kernel(before_ref, after_ref, left_ref, right_ref, first_ref, second_ref):
    @pl.when(lax.axis_index("pipe") == 0)
    def _():
        for n, row in enumerate(OUTER):
            at = 3 * WIDE + 32 * n
            middle = top_layer(before_ref, after_ref, row)
            sides = left_ref[:C, at : at + 32], right_ref[:C, at : at + 32]
            halo_ref = first_ref if n < 4 else second_ref
            halo_ref[:, lane(n % 4)] = join([sides[0], middle, sides[1]])


def forward_kernel(
    x_ref, height_ref, before_ref, after_ref, left_ref, right_ref, fwd_ref,
    slope_ref, mask_ref, rows_ref,
    base_ref, cols_ref, code_ref, pre_ref,
):
    where = lax.broadcasted_iota(jnp.int32, (8, WIDE), 1)
    middle = (
        before_ref[C : C + 8, :WIDE].astype(F32),
        code_of(height_ref, (8, WIDE)),
        after_ref[C : C + 8, :WIDE].astype(F32),
    )
    codes = []
    for n in range(3):
        left = left_ref[C : C + 8, lane(n)].astype(F32)
        right = right_ref[C : C + 8, lane(n)].astype(F32)
        codes.append(jnp.where(where < 32, left, jnp.where(where < 96, middle[n], right)))
    for row in range(18):
        code_ref[:, lane(row)] = codes[0 if row < 5 else 1 if row < 13 else 2]
    for row in range(18):
        tile = join(
            [
                x_side(left_ref, row),
                x_layer(x_ref, before_ref, after_ref, row),
                x_side(right_ref, row),
            ]
        )
        if 4 <= row < 14:
            rows_ref[:, lane(row - 4)] = tile
        at = 4 * WIDE + 64 + 8 * row
        low = join([tile[:, :120], left_ref[:C, at : at + 8]])
        high = join([right_ref[:C, at : at + 8], tile[:, 8:]])
        shifted_rows(base_ref, row, tile, low, high)

    level = lax.broadcasted_iota(jnp.int32, (8, WIDE), 1) % 8
    rise_of = {
        -1: jnp.where(level == 0, -1.0, 0.0),
        0: jnp.zeros((8, WIDE), F32),
        1: jnp.where(level == 7, 1.0, 0.0),
    }

    for rows in ((0, 1, 2), (3,), (4,), (5, 6, 7, 8, 9, 10), (11,), (12,), (13, 14, 15)):
        here = code_ref[:, lane(rows[0] + 1)]
        for ox in (-1, 0, 1):
            near = code_ref[:, lane(rows[0] + 1 + ox)]
            for oy in (-1, 0, 1):
                if oy < 0:
                    source = jnp.where(where >= 120, near[:, 0:1], near)
                elif oy > 0:
                    source = jnp.where(where < 8, near[:, 127:128], near)
                else:
                    source = near
                rise = turn(source, -8 * oy) - here
                for oz in (-1, 0, 1):
                    keep = jnp.where(rise == rise_of[oz], 1.0, 0.0)
                    keep = jnp.concatenate([keep, keep], 0).astype(BF16)
                    tap = 9 * (ox + 1) + 3 * (oy + 1) + oz + 1
                    for row in rows:
                        mask_ref[tap, :, lane(row)] = keep

    for pair in range(8):
        make_cols(cols_ref, base_ref, mask_ref, 2 * pair + 1, 2 * pair, 2 * pair)
    pre_ref[...] = product(fwd_ref[...], cols_ref[...])
    for row in range(16):
        pre = pre_ref[:, lane(row)]
        sigma = 1.0 / (1.0 + jnp.exp(-pre))
        slope_ref[:, lane(row)] = sigma * (1.0 + pre * (1.0 - sigma))


def top_row(top_ref, halo_ref, left_ref, right_ref, row):
    if 5 <= row < 13:
        at, side = 64 * (row - 5), 6 * WIDE + 32 * (row - 5)
        tile = join(
            [
                left_ref[:C, side : side + 32],
                top_ref[:, at : at + 64],
                right_ref[:C, side : side + 32],
            ]
        )
    else:
        tile = halo_ref[:, lane((row - 1) % 12)]
    return jnp.where(lax.axis_index("pipe") == SECTIONS - 1, tile, jnp.zeros_like(tile))


def step_rows(incoming_ref, slope_ref, mask_ref, bwd_ref, base_ref, cols_ref, store, count, first):
    for row in range(count):
        grad = (
            incoming_ref[:, lane(row)].astype(F32) * slope_ref[:, lane(row + first - 1)]
        ).astype(BF16)
        shifted_rows(base_ref, row, grad)

    for pair in range((count - 2) // 2):
        make_cols(cols_ref, base_ref, mask_ref, 2 * pair + 1, 2 * pair + first, 2 * pair)
    rows = lane(1, count - 2)
    total = incoming_ref[:, rows].astype(F32) + product(bwd_ref[...], cols_ref[...])
    for pair in range((count - 2) // 2):
        store(pair, total[:, 2 * pair * WIDE : 2 * (pair + 1) * WIDE].astype(BF16))


def spread(packed_ref, width, row):
    spare = jnp.zeros((C, (WIDE - width) // 2), BF16)
    return join([spare, packed_ref[:, width * row : width * row + width], spare])


TOP_PIECES = (2, 8, WIDE), (10, 6, WIDE)
MIDDLE_PIECES = (3, 6, 96), (9, 6, 96)
LATE_PIECES = (4, 4, 80), (8, 6, 80)


def pieces_row(pieces, row):
    for ref, first, count, width in pieces:
        if first <= row < first + count:
            if width == WIDE:
                return ref[:, lane(row - first)]
            return spread(ref, width, row - first)


def step_part(row_of, low, count, width, result_ref, slope_ref, mask_ref, bwd_ref, scratch):
    base_ref, cols_ref, rows_ref, full_ref = scratch
    for n in range(count + 2):
        rows_ref[:, lane(n)] = row_of(low - 1 + n)

    def store(pair, value):
        full_ref[:, lane(2 * pair, 2)] = value

    step_rows(
        rows_ref, slope_ref, mask_ref, bwd_ref, base_ref, cols_ref, store, count + 2, low - 1
    )
    skip = (WIDE - width) // 2
    packed = [full_ref[:, lane(n)][:, skip : skip + width] for n in range(count)]
    spare = result_ref.shape[1] - width * count
    result_ref[...] = join(packed + [jnp.zeros((C, spare), BF16)] if spare else packed)


def top_kernel(
    low, count, top_ref, halo_ref, left_ref, right_ref, slope_ref, mask_ref, bwd_ref,
    result_ref, *scratch,
):
    def row_of(row):
        return top_row(top_ref, halo_ref, left_ref, right_ref, row)

    step_part(row_of, low, count, WIDE, result_ref, slope_ref, mask_ref, bwd_ref, scratch)


def middle_kernel(pieces, low, count, width, *refs):
    given, refs = refs[: len(pieces)], refs[len(pieces) :]
    slope_ref, mask_ref, bwd_ref, result_ref, *scratch = refs

    def row_of(row):
        return pieces_row([(ref,) + piece for ref, piece in zip(given, pieces)], row)

    step_part(row_of, low, count, width, result_ref, slope_ref, mask_ref, bwd_ref, scratch)


def halves(first, second):
    where = lax.broadcasted_iota(jnp.int32, first.shape, 1)
    return jnp.where(where < 64, turn(first, -32), turn(second, 32))


def gather_kernel(
    top_ref, halo_ref, left_ref, right_ref, slope_ref, mask_ref, x_ref, *refs
):
    kinds = TOP_PIECES + MIDDLE_PIECES + LATE_PIECES
    pieces = [(ref,) + piece for ref, piece in zip(refs[:6], kinds)]
    incoming = [(ref,) + piece for ref, piece in zip(refs[6:10], TOP_PIECES + MIDDLE_PIECES)]
    all_ref, grad_ref, out_ref, base_ref = refs[10:]
    for n in range(8):
        row = n + 5
        scale = slope_ref[:, lane(n + 4)]
        tiles = (
            top_row(top_ref, halo_ref, left_ref, right_ref, row),
            pieces_row(incoming[:2], row),
            pieces_row(incoming[2:], row),
        )
        grads = [(tile.astype(F32) * scale).astype(BF16) for tile in tiles]
        grad_ref[:, lane(n)] = grads[0] + grads[1] + grads[2]
        outs = [pieces_row(pieces[at : at + 2], row) for at in (0, 2, 4)]
        out_ref[:, lane(n)] = outs[0] + outs[1] + outs[2]
    for row in range(10):
        shifted_rows(base_ref, row, x_ref[:, lane(row)])

    def one(pair, carry):
        for tap in range(TAPS):
            ox, j = tap // 9 - 1, tap % 9
            tiles = []
            for n in range(2):
                tile = base_ref[j, :, lane(2 * pair + 1 + n + ox)].reshape(C // 16, 16, WIDE)
                kept = tile * mask_ref[tap, :, lane(2 * pair + 4 + n)][None]
                tiles.append(kept.reshape(C, WIDE))
            all_ref[C * tap : C * tap + C, lane(pair)] = halves(*tiles)
        return carry

    lax.fori_loop(0, 4, one, 0)


def terms_kernel(
    first_ref, second_ref, slope_ref, grad_in, all_ref, terms_ref, incoming_ref
):
    for row in range(10):
        incoming_ref[:, lane(row)] = pieces_row(
            ((first_ref,) + LATE_PIECES[0], (second_ref,) + LATE_PIECES[1]), row + 4
        )
    grads = []
    for row in range(8):
        grad = incoming_ref[:, lane(row + 1)].astype(F32) * slope_ref[:, lane(row + 4)]
        grads.append(grad_in[:, lane(row)] + grad.astype(BF16))
    grads = join([halves(grads[2 * pair], grads[2 * pair + 1]) for pair in range(4)])
    for four in range(7):
        parts = []
        for tap in range(4 * four, 4 * four + 4):
            if tap < TAPS:
                part = lax.dot_general(
                    all_ref[C * tap : C * tap + C, :], grads, (((1,), (1,)), ((), ())),
                    preferred_element_type=F32,
                ).astype(BF16)
            else:
                part = jnp.zeros((C, C), BF16)
            parts.append(part)
        first, second, third, fourth = parts
        at = 3 * C * four
        terms_ref[at : at + C, :] = jnp.concatenate([first, second[:, :32]], 1)
        terms_ref[at + C : at + 2 * C, :] = jnp.concatenate([second[:, 32:], third[:, :64]], 1)
        terms_ref[at + 2 * C : at + 3 * C, :] = jnp.concatenate([third[:, 64:], fourth], 1)
    terms_ref[21 * C :, :] = jnp.zeros((NEAR * CHUNK - 21 * C, WIDE), BF16)


def last_kernel(
    incoming_ref, slope_ref, mask_ref, bwd_ref, out_in, out_ref, base_ref, cols_ref
):
    def store(pair, value):
        total = out_in[:, lane(2 * pair, 2)] + value
        out_ref[:, lane(pair)] = halves(total[:, :WIDE], total[:, WIDE:])

    step_rows(incoming_ref, slope_ref, mask_ref, bwd_ref, base_ref, cols_ref, store, 10, 4)


def sum_kernel(parts_ref, out_ref):
    total = parts_ref[0].astype(F32)
    for n in range(1, parts_ref.shape[0]):
        total = total + parts_ref[n].astype(F32)
    total = total.astype(BF16)
    for n in range(out_ref.shape[0]):
        out_ref[n] = total


def scale_kernel(whole_ref, out_ref):
    whole = whole_ref[...].astype(F32)
    scale = lax.rsqrt(jnp.sum(whole * whole) / (DEEP * C) + 1e-06)
    for four in range(7):
        at = 3 * C * four
        first, second, third = (whole_ref[at + n * C : at + n * C + C, :] for n in range(3))
        parts = (
            first[:, :96],
            jnp.concatenate([first[:, 96:], second[:, :64]], 1),
            jnp.concatenate([second[:, 64:], third[:, :32]], 1),
            third[:, 32:],
        )
        for n, tap in enumerate(range(4 * four, min(4 * four + 4, TAPS))):
            out_ref[C * tap : C * tap + C, :] = parts[n].astype(F32) * scale


def groups():
    def device(y, high, low, core):
        return y * 32 + (2 * high + low) * 2 + core

    kinds = [(y, low, core) for y in range(4) for low in range(2) for core in range(2)]
    near = [[device(y, high, low, core) for y, low, core in kinds] for high in range(FAR)]
    far = [[device(y, high, low, core) for high in range(FAR)] for y, low, core in kinds]
    return near, far


def body(section_input, top_grad, conv_weight, brick_height):
    both = ("space", "pipe")

    def between(by_row, by_col, sections):
        pairs = []
        for x in range(ROWS):
            for y in range(COLS):
                if 0 <= x + by_row < ROWS and 0 <= y + by_col < COLS:
                    source = x * COLS + y
                    target = (x + by_row) * COLS + y + by_col
                    for a, b in sections:
                        pairs.append((source * SECTIONS + a, target * SECTIONS + b))
        return pairs

    same = [(s, s) for s in range(SECTIONS)]
    x = section_input.reshape(C, CELLS)
    top = top_grad.reshape(C, CELLS)
    fwd, bwd = call(weight_kernel, [((C, DEEP), BF16)] * 2)(conv_weight[0])
    up, down, x, top = call(
        rows_kernel,
        [((C + 16, 3 * WIDE), BF16)] * 2 + [((C, CELLS), BF16)] * 2,
        [pltpu.SemaphoreType.DMA((2,))],
        bring=False,
    )(x, top, brick_height)
    before = lax.ppermute(up, both, between(1, 0, same))
    after = lax.ppermute(down, both, between(-1, 0, same))
    before, after, fwd, bwd = lax.optimization_barrier((before, after, fwd, bwd))
    to_right, to_left = call(cols_kernel, [((C + 16, 8 * WIDE), BF16)] * 2)(
        x, top, brick_height, before, after
    )
    left = lax.ppermute(to_right, both, between(0, 1, same))
    right = lax.ppermute(to_left, both, between(0, -1, same))
    halos = call(halo_kernel, [((C, 4 * WIDE), BF16)] * 2)(before, after, left, right)
    halos = [lax.ppermute(halo, both, between(0, 0, [(0, SECTIONS - 1)])) for halo in halos]

    core = ((C, 8 * WIDE), BF16)
    slope, mask, x_rows = call(
        forward_kernel,
        [((C, 16 * WIDE), F32), ((TAPS, 16, 16 * WIDE), BF16), ((C, 10 * WIDE), BF16)],
        [((9, C, 18 * WIDE), BF16), ((DEEP, 16 * WIDE), BF16), ((8, 18 * WIDE), F32),
         ((C, 16 * WIDE), F32)],
    )(x, brick_height, before, after, left, right, fwd)
    def scratch(count):
        return [
            ((9, C, (count + 2) * WIDE), BF16), ((DEEP, count * WIDE), BF16),
            ((C, (count + 2) * WIDE), BF16),
            ((C, count * WIDE), BF16),
        ]

    def hand_on(value, source):
        return lax.ppermute(value, both, between(0, 0, [(source, source - 1)]))

    def behind(kernel, count):
        return lambda *refs: kernel(*refs[:count], *refs[count + 1 :])

    def parts_of(kernels, args, pieces, source):
        made = []
        for kernel, given, (low, count, width) in zip(kernels, args, pieces):
            if made:
                kernel, given = behind(kernel, len(given)), given + (made[0][0],)
            lanes = -(-count * width // WIDE) * WIDE
            (result,) = call(kernel, [((C, lanes), BF16)], scratch(count))(*given)
            made.append((result, hand_on(result, source)))
        return [result for result, _ in made], [moved for _, moved in made]

    def middle(given, pieces, low, count, width):
        return functools.partial(middle_kernel, pieces[:given], low, count, width)

    rest = (slope, mask, bwd)
    tops, moved = parts_of(
        [functools.partial(top_kernel, low, count) for low, count, _ in TOP_PIECES],
        [(top, halo, left, right) + rest for halo in halos],
        TOP_PIECES,
        3,
    )
    middles, moved_on = parts_of(
        [middle(n + 1, TOP_PIECES, *MIDDLE_PIECES[n]) for n in range(2)],
        [tuple(moved[: n + 1]) + rest for n in range(2)],
        MIDDLE_PIECES,
        2,
    )
    lates, (first, second) = parts_of(
        [middle(n + 1, MIDDLE_PIECES, *LATE_PIECES[n]) for n in range(2)],
        [tuple(moved_on[: n + 1]) + rest for n in range(2)],
        LATE_PIECES,
        1,
    )
    x_rows, result = lax.optimization_barrier((x_rows, lates[1]))
    x_cols, grad, out = call(
        gather_kernel, [((DEEP, CELLS), BF16), core, core], [((9, C, 10 * WIDE), BF16)]
    )(
        top, halos[0], left, right, slope, mask, x_rows,
        *tops, *middles, lates[0], result, *moved, *moved_on,
    )
    terms, incoming = call(
        terms_kernel, [((NEAR * CHUNK, WIDE), BF16), ((C, 10 * WIDE), BF16)]
    )(first, second, slope, grad, x_cols)

    near, far = groups()
    parts = lax.all_to_all(
        terms.reshape(NEAR, CHUNK, WIDE), "space", 0, 0, axis_index_groups=near
    )
    parts, out = lax.optimization_barrier((parts, out))
    (out,) = call(
        last_kernel,
        [((C, CELLS), BF16)],
        [((9, C, 10 * WIDE), BF16), ((DEEP, 8 * WIDE), BF16)],
        leave=(0,),
    )(incoming, slope, mask, bwd, out)
    (copies,) = call(sum_kernel, [((FAR, CHUNK, WIDE), BF16)])(parts)
    parts = lax.all_to_all(copies, "space", 0, 0, axis_index_groups=far)
    parts, out = lax.optimization_barrier((parts, out))
    (copies,) = call(sum_kernel, [((NEAR, CHUNK, WIDE), BF16)])(parts)
    whole = lax.all_to_all(copies, "space", 0, 0, axis_index_groups=near)
    (weight_grad,) = call(scale_kernel, [((DEEP, C), F32)], leave=(0,))(
        whole.reshape(NEAR * CHUNK, WIDE)
    )
    return (out.reshape(1, 1, C, CELLS), weight_grad.reshape(1, TAPS, C, C))


def solution(mesh):
    return jax.shard_map(
        body,
        mesh=mesh,
        in_specs=(
            P("pipe", "space", None, None),
            P("space", None, None),
            P("pipe", None, None, None),
            P("space"),
        ),
        out_specs=(P("pipe", "space", None, None), P("pipe", None, None, None)),
        check_vma=False,
    )
```

```python
import functools

import jax
import jax.numpy as jnp
from jax import lax
from jax.experimental import pallas as pl
from jax.experimental.pallas import tpu as pltpu
from jax.sharding import PartitionSpec as P

C = 96
CELLS = 512
COLS = 8
ROWS = 16
SECTIONS = 4
TAPS = 27
DEEP = TAPS * C
WIDE = 128
CODE = 8
NEAR = 16
FAR = 8
CHUNK = 128
VMEM_BYTES = 32 * 1024 * 1024
F32 = jnp.float32
BF16 = jnp.bfloat16


def call(kernel, outs, scratch=(), leave=(), bring=True):
    shapes = [
        jax.ShapeDtypeStruct(shape, dtype) if n in leave else pltpu.VMEM(shape, dtype)
        for n, (shape, dtype) in enumerate(outs)
    ]

    def run(*args):
        inner = pl.pallas_call(
            kernel,
            out_shape=shapes,
            in_specs=[
                pl.BlockSpec(
                    memory_space=pltpu.SMEM if arg.dtype == jnp.int32
                    else pltpu.VMEM if bring else pl.ANY
                )
                for arg in args
            ],
            out_specs=[pl.BlockSpec(memory_space=pltpu.VMEM)] * len(shapes),
            scratch_shapes=[
                pltpu.VMEM(*item) if isinstance(item, tuple) else item for item in scratch
            ],
            compiler_params=pltpu.CompilerParams(vmem_limit_bytes=VMEM_BYTES),
        )
        return inner(
            *[
                arg if arg.dtype == jnp.int32
                else pltpu.with_memory_space_constraint(arg, pltpu.VMEM if bring else pltpu.HBM)
                for arg in args
            ]
        )

    return run


def lane(row, count=1):
    start = row * WIDE
    if not isinstance(start, int):
        start = pl.multiple_of(start, WIDE)
    return pl.ds(start, count * WIDE)


def turn(value, by):
    by = by % value.shape[1]
    return pltpu.roll(value, by, 1) if by else value


def shifted_rows(base_ref, row, tile, low=None, high=None):
    level = lax.broadcasted_iota(jnp.int32, (C, WIDE), 1) % 8
    for oy, source in ((-1, low), (0, None), (1, high)):
        source = tile if source is None else source
        for oz in (-1, 0, 1):
            if oz == 0:
                moved = turn(source, -8 * oy)
            elif oz > 0:
                moved = jnp.where(level < 7, turn(source, -8 * oy - 1), turn(source, -8 * oy + 7))
            else:
                moved = jnp.where(level > 0, turn(source, -8 * oy + 1), turn(source, -8 * oy - 7))
            base_ref[3 * (oy + 1) + oz + 1, :, lane(row)] = moved


def make_cols(cols_ref, base_ref, mask_ref, base_row, mask_row, at=0):
    for ox in (-1, 0, 1):
        for j in range(9):
            tap = 9 * (ox + 1) + j
            tile = base_ref[j, :, lane(base_row + ox, 2)].reshape(C // 16, 16, 2 * WIDE)
            kept = tile * mask_ref[tap, :, lane(mask_row, 2)][None]
            cols_ref[C * tap : C * tap + C, lane(at, 2)] = kept.reshape(C, 2 * WIDE)


def product(weight, cols):
    return lax.dot_general(
        weight, cols, (((1,), (0,)), ((), ())), preferred_element_type=F32
    )


def weight_kernel(w_ref, fwd_ref, bwd_ref):
    for q in range(TAPS):
        fwd_ref[:, C * q : C * q + C] = w_ref[q].T
        bwd_ref[:, C * q : C * q + C] = w_ref[TAPS - 1 - q]


OUTER = (1, 2, 3, 4, 13, 14, 15, 16)


def code_of(height_ref, shape):
    return jnp.full(shape, (height_ref[0] + CODE).astype(F32), F32)


def rows_kernel(x_hbm, top_hbm, height_ref, up_ref, down_ref, x_ref, top_ref, sems):
    x_copy = pltpu.make_async_copy(x_hbm, x_ref, sems.at[0])
    top_copy = pltpu.make_async_copy(top_hbm, top_ref, sems.at[1])
    x_copy.start()
    top_copy.start()
    x_copy.wait()
    top_copy.wait()
    lowest = lax.axis_index("pipe") == 0
    code = code_of(height_ref, (16, 3 * WIDE)).astype(BF16)
    spare = jnp.zeros((C, 64), BF16)
    up_ref[C:, :] = code
    down_ref[C:, :] = code
    up_ref[:C, :WIDE] = x_ref[:, 384:512]
    down_ref[:C, :WIDE] = x_ref[:, 0:128]

    @pl.when(lowest)
    def _():
        up_ref[:C, WIDE:] = top_ref[:, 256:512]
        down_ref[:C, WIDE:] = top_ref[:, 0:256]

    @pl.when(jnp.logical_not(lowest))
    def _():
        up_ref[:C, WIDE:] = jnp.concatenate([x_ref[:, 192:384], spare], 1)
        down_ref[:C, WIDE:] = jnp.concatenate([x_ref[:, 128:320], spare], 1)


def x_layer(x_ref, before_ref, after_ref, row):
    if row < 5:
        at = 64 * (row - 3) if row >= 3 else WIDE + 64 * row
        return before_ref[:C, at : at + 64]
    if row < 13:
        return x_ref[:, 64 * (row - 5) : 64 * (row - 5) + 64]
    at = 64 * (row - 13) if row < 15 else WIDE + 64 * (row - 15)
    return after_ref[:C, at : at + 64]


def top_layer(before_ref, after_ref, row):
    if row < 5:
        return before_ref[:C, WIDE + 64 * (row - 1) : WIDE + 64 * row]
    return after_ref[:C, WIDE + 64 * (row - 13) : WIDE + 64 * (row - 12)]


def join(parts):
    return jnp.concatenate(parts, 1)


def cols_kernel(x_ref, top_ref, height_ref, before_ref, after_ref, right_ref, left_ref):
    lowest = lax.axis_index("pipe") == 0
    codes = join(
        [before_ref[C:, :WIDE], code_of(height_ref, (16, WIDE)).astype(BF16), after_ref[C:, :WIDE]]
    )
    for out, start, fifth in ((right_ref, 32, 24), (left_ref, 0, 32)):

        def piece(layer, start=start):
            return layer[:, start : start + 32]

        out[C:, : 3 * WIDE] = codes
        out[C:, 3 * WIDE :] = jnp.zeros((16, 5 * WIDE), BF16)
        for four in range(3):
            rows = range(3 + 4 * four, 7 + 4 * four)
            out[:C, lane(four)] = join(
                [piece(x_layer(x_ref, before_ref, after_ref, row)) for row in rows]
            )

        @pl.when(lowest)
        def _(out=out, piece=piece):
            tops = [piece(top_layer(before_ref, after_ref, row)) for row in OUTER]
            out[:C, lane(3)] = join(tops[:4])
            out[:C, lane(4)] = join(tops[4:])
            out[:C, lane(5, 3)] = jnp.zeros((C, 3 * WIDE), BF16)

        @pl.when(jnp.logical_not(lowest))
        def _(out=out, piece=piece, fifth=fifth):
            outer = [
                piece(x_layer(x_ref, before_ref, after_ref, row)) for row in (0, 1, 2, 15, 16, 17)
            ]
            more = [
                x_layer(x_ref, before_ref, after_ref, row)[:, fifth : fifth + 8]
                for row in range(18)
            ]
            tops = [piece(top_ref[:, 64 * n : 64 * n + 64]) for n in range(8)]
            out[:C, lane(3)] = join(outer[:4])
            out[:C, lane(4)] = join(outer[4:] + more[:8])
            out[:C, lane(5)] = join(more[8:] + [jnp.zeros((C, 48), BF16)])
            out[:C, lane(6)] = join(tops[:4])
            out[:C, lane(7)] = join(tops[4:])


def x_side(side_ref, row):
    if 3 <= row < 15:
        at = 32 * (row - 3)
    else:
        at = 3 * WIDE + 32 * (row if row < 3 else row - 12)
    return side_ref[:C, at : at + 32]


def halo_kernel(before_ref, after_ref, left_ref, right_ref, first_ref, second_ref):
    @pl.when(lax.axis_index("pipe") == 0)
    def _():
        for n, row in enumerate(OUTER):
            at = 3 * WIDE + 32 * n
            middle = top_layer(before_ref, after_ref, row)
            sides = left_ref[:C, at : at + 32], right_ref[:C, at : at + 32]
            halo_ref = first_ref if n < 4 else second_ref
            halo_ref[:, lane(n % 4)] = join([sides[0], middle, sides[1]])


def forward_kernel(
    x_ref, height_ref, before_ref, after_ref, left_ref, right_ref, fwd_ref,
    slope_ref, mask_ref, rows_ref,
    base_ref, cols_ref, code_ref, pre_ref,
):
    where = lax.broadcasted_iota(jnp.int32, (8, WIDE), 1)
    middle = (
        before_ref[C : C + 8, :WIDE].astype(F32),
        code_of(height_ref, (8, WIDE)),
        after_ref[C : C + 8, :WIDE].astype(F32),
    )
    codes = []
    for n in range(3):
        left = left_ref[C : C + 8, lane(n)].astype(F32)
        right = right_ref[C : C + 8, lane(n)].astype(F32)
        codes.append(jnp.where(where < 32, left, jnp.where(where < 96, middle[n], right)))
    for row in range(18):
        code_ref[:, lane(row)] = codes[0 if row < 5 else 1 if row < 13 else 2]
    for row in range(18):
        tile = join(
            [
                x_side(left_ref, row),
                x_layer(x_ref, before_ref, after_ref, row),
                x_side(right_ref, row),
            ]
        )
        if 4 <= row < 14:
            rows_ref[:, lane(row - 4)] = tile
        at = 4 * WIDE + 64 + 8 * row
        low = join([tile[:, :120], left_ref[:C, at : at + 8]])
        high = join([right_ref[:C, at : at + 8], tile[:, 8:]])
        shifted_rows(base_ref, row, tile, low, high)

    level = lax.broadcasted_iota(jnp.int32, (8, WIDE), 1) % 8
    rise_of = {
        -1: jnp.where(level == 0, -1.0, 0.0),
        0: jnp.zeros((8, WIDE), F32),
        1: jnp.where(level == 7, 1.0, 0.0),
    }

    for rows in ((0, 1, 2), (3,), (4,), (5, 6, 7, 8, 9, 10), (11,), (12,), (13, 14, 15)):
        here = code_ref[:, lane(rows[0] + 1)]
        for ox in (-1, 0, 1):
            near = code_ref[:, lane(rows[0] + 1 + ox)]
            for oy in (-1, 0, 1):
                if oy < 0:
                    source = jnp.where(where >= 120, near[:, 0:1], near)
                elif oy > 0:
                    source = jnp.where(where < 8, near[:, 127:128], near)
                else:
                    source = near
                rise = turn(source, -8 * oy) - here
                for oz in (-1, 0, 1):
                    keep = jnp.where(rise == rise_of[oz], 1.0, 0.0)
                    keep = jnp.concatenate([keep, keep], 0).astype(BF16)
                    tap = 9 * (ox + 1) + 3 * (oy + 1) + oz + 1
                    for row in rows:
                        mask_ref[tap, :, lane(row)] = keep

    for pair in range(8):
        make_cols(cols_ref, base_ref, mask_ref, 2 * pair + 1, 2 * pair, 2 * pair)
    pre_ref[...] = product(fwd_ref[...], cols_ref[...])
    for row in range(16):
        pre = pre_ref[:, lane(row)]
        sigma = 1.0 / (1.0 + jnp.exp(-pre))
        slope_ref[:, lane(row)] = sigma * (1.0 + pre * (1.0 - sigma))


def top_row(top_ref, halo_ref, left_ref, right_ref, row):
    if 5 <= row < 13:
        at, side = 64 * (row - 5), 6 * WIDE + 32 * (row - 5)
        tile = join(
            [
                left_ref[:C, side : side + 32],
                top_ref[:, at : at + 64],
                right_ref[:C, side : side + 32],
            ]
        )
    else:
        tile = halo_ref[:, lane((row - 1) % 12)]
    return jnp.where(lax.axis_index("pipe") == SECTIONS - 1, tile, jnp.zeros_like(tile))


def step_rows(incoming_ref, slope_ref, mask_ref, bwd_ref, base_ref, cols_ref, store, count, first):
    for row in range(count):
        grad = (
            incoming_ref[:, lane(row)].astype(F32) * slope_ref[:, lane(row + first - 1)]
        ).astype(BF16)
        shifted_rows(base_ref, row, grad)

    for pair in range((count - 2) // 2):
        make_cols(cols_ref, base_ref, mask_ref, 2 * pair + 1, 2 * pair + first, 2 * pair)
    rows = lane(1, count - 2)
    total = incoming_ref[:, rows].astype(F32) + product(bwd_ref[...], cols_ref[...])
    for pair in range((count - 2) // 2):
        store(pair, total[:, 2 * pair * WIDE : 2 * (pair + 1) * WIDE].astype(BF16))


def spread(packed_ref, width, row):
    spare = jnp.zeros((C, (WIDE - width) // 2), BF16)
    return join([spare, packed_ref[:, width * row : width * row + width], spare])


TOP_PIECES = (2, 8, 112), (10, 6, 112)
MIDDLE_PIECES = (3, 6, 96), (9, 6, 96)
LATE_PIECES = (4, 4, 80), (8, 6, 80)


def pieces_row(pieces, row):
    for ref, first, count, width in pieces:
        if first <= row < first + count:
            if width == WIDE:
                return ref[:, lane(row - first)]
            return spread(ref, width, row - first)


def step_part(row_of, low, count, width, result_ref, slope_ref, mask_ref, bwd_ref, scratch):
    base_ref, cols_ref, rows_ref, full_ref = scratch
    for n in range(count + 2):
        rows_ref[:, lane(n)] = row_of(low - 1 + n)

    def store(pair, value):
        full_ref[:, lane(2 * pair, 2)] = value

    step_rows(
        rows_ref, slope_ref, mask_ref, bwd_ref, base_ref, cols_ref, store, count + 2, low - 1
    )
    skip = (WIDE - width) // 2
    packed = [full_ref[:, lane(n)][:, skip : skip + width] for n in range(count)]
    spare = result_ref.shape[1] - width * count
    result_ref[...] = join(packed + [jnp.zeros((C, spare), BF16)] if spare else packed)


def top_kernel(
    low, count, width, top_ref, halo_ref, left_ref, right_ref, slope_ref, mask_ref, bwd_ref,
    result_ref, *scratch,
):
    def row_of(row):
        return top_row(top_ref, halo_ref, left_ref, right_ref, row)

    step_part(row_of, low, count, width, result_ref, slope_ref, mask_ref, bwd_ref, scratch)


def middle_kernel(pieces, low, count, width, *refs):
    given, refs = refs[: len(pieces)], refs[len(pieces) :]
    slope_ref, mask_ref, bwd_ref, result_ref, *scratch = refs

    def row_of(row):
        return pieces_row([(ref,) + piece for ref, piece in zip(given, pieces)], row)

    step_part(row_of, low, count, width, result_ref, slope_ref, mask_ref, bwd_ref, scratch)


def halves(first, second):
    where = lax.broadcasted_iota(jnp.int32, first.shape, 1)
    return jnp.where(where < 64, turn(first, -32), turn(second, 32))


def gather_kernel(
    top_ref, halo_ref, left_ref, right_ref, slope_ref, mask_ref, x_ref, *refs
):
    kinds = TOP_PIECES + MIDDLE_PIECES + LATE_PIECES
    pieces = [(ref,) + piece for ref, piece in zip(refs[:6], kinds)]
    incoming = [(ref,) + piece for ref, piece in zip(refs[6:10], TOP_PIECES + MIDDLE_PIECES)]
    all_ref, grad_ref, out_ref, base_ref = refs[10:]
    for n in range(8):
        row = n + 5
        scale = slope_ref[:, lane(n + 4)]
        tiles = (
            top_row(top_ref, halo_ref, left_ref, right_ref, row),
            pieces_row(incoming[:2], row),
            pieces_row(incoming[2:], row),
        )
        grads = [(tile.astype(F32) * scale).astype(BF16) for tile in tiles]
        grad_ref[:, lane(n)] = grads[0] + grads[1] + grads[2]
        outs = [pieces_row(pieces[at : at + 2], row) for at in (0, 2, 4)]
        out_ref[:, lane(n)] = outs[0] + outs[1] + outs[2]
    for row in range(10):
        shifted_rows(base_ref, row, x_ref[:, lane(row)])

    def one(pair, carry):
        for tap in range(TAPS):
            ox, j = tap // 9 - 1, tap % 9
            tiles = []
            for n in range(2):
                tile = base_ref[j, :, lane(2 * pair + 1 + n + ox)].reshape(C // 16, 16, WIDE)
                kept = tile * mask_ref[tap, :, lane(2 * pair + 4 + n)][None]
                tiles.append(kept.reshape(C, WIDE))
            all_ref[C * tap : C * tap + C, lane(pair)] = halves(*tiles)
        return carry

    lax.fori_loop(0, 4, one, 0)


def terms_kernel(
    first_ref, second_ref, slope_ref, grad_in, all_ref, terms_ref, incoming_ref
):
    for row in range(10):
        incoming_ref[:, lane(row)] = pieces_row(
            ((first_ref,) + LATE_PIECES[0], (second_ref,) + LATE_PIECES[1]), row + 4
        )
    grads = []
    for row in range(8):
        grad = incoming_ref[:, lane(row + 1)].astype(F32) * slope_ref[:, lane(row + 4)]
        grads.append(grad_in[:, lane(row)] + grad.astype(BF16))
    grads = join([halves(grads[2 * pair], grads[2 * pair + 1]) for pair in range(4)])
    whole = lax.dot_general(
        all_ref[...], grads, (((1,), (1,)), ((), ())), preferred_element_type=F32
    ).astype(BF16)
    for four in range(7):
        parts = []
        for tap in range(4 * four, 4 * four + 4):
            if tap < TAPS:
                part = whole[C * tap : C * tap + C, :]
            else:
                part = jnp.zeros((C, C), BF16)
            parts.append(part)
        first, second, third, fourth = parts
        at = 3 * C * four
        terms_ref[at : at + C, :] = jnp.concatenate([first, second[:, :32]], 1)
        terms_ref[at + C : at + 2 * C, :] = jnp.concatenate([second[:, 32:], third[:, :64]], 1)
        terms_ref[at + 2 * C : at + 3 * C, :] = jnp.concatenate([third[:, 64:], fourth], 1)
    terms_ref[21 * C :, :] = jnp.zeros((NEAR * CHUNK - 21 * C, WIDE), BF16)


def last_kernel(
    incoming_ref, slope_ref, mask_ref, bwd_ref, out_in, out_ref, base_ref, cols_ref
):
    def store(pair, value):
        total = out_in[:, lane(2 * pair, 2)] + value
        out_ref[:, lane(pair)] = halves(total[:, :WIDE], total[:, WIDE:])

    step_rows(incoming_ref, slope_ref, mask_ref, bwd_ref, base_ref, cols_ref, store, 10, 4)


def sum_kernel(parts_ref, out_ref):
    total = parts_ref[0].astype(F32)
    for n in range(1, parts_ref.shape[0]):
        total = total + parts_ref[n].astype(F32)
    total = total.astype(BF16)
    for n in range(out_ref.shape[0]):
        out_ref[n] = total


def scale_kernel(whole_ref, out_ref):
    whole = whole_ref[...].astype(F32)
    scale = lax.rsqrt(jnp.sum(whole * whole) / (DEEP * C) + 1e-06)
    for four in range(7):
        at = 3 * C * four
        first, second, third = (whole_ref[at + n * C : at + n * C + C, :] for n in range(3))
        parts = (
            first[:, :96],
            jnp.concatenate([first[:, 96:], second[:, :64]], 1),
            jnp.concatenate([second[:, 64:], third[:, :32]], 1),
            third[:, 32:],
        )
        for n, tap in enumerate(range(4 * four, min(4 * four + 4, TAPS))):
            out_ref[C * tap : C * tap + C, :] = parts[n].astype(F32) * scale


def groups():
    def device(y, high, low, core):
        return y * 32 + (2 * high + low) * 2 + core

    kinds = [(y, low, core) for y in range(4) for low in range(2) for core in range(2)]
    near = [[device(y, high, low, core) for y, low, core in kinds] for high in range(FAR)]
    far = [[device(y, high, low, core) for high in range(FAR)] for y, low, core in kinds]
    return near, far


def body(section_input, top_grad, conv_weight, brick_height):
    both = ("space", "pipe")

    def between(by_row, by_col, sections):
        pairs = []
        for x in range(ROWS):
            for y in range(COLS):
                if 0 <= x + by_row < ROWS and 0 <= y + by_col < COLS:
                    source = x * COLS + y
                    target = (x + by_row) * COLS + y + by_col
                    for a, b in sections:
                        pairs.append((source * SECTIONS + a, target * SECTIONS + b))
        return pairs

    same = [(s, s) for s in range(SECTIONS)]
    x = section_input.reshape(C, CELLS)
    top = top_grad.reshape(C, CELLS)
    fwd, bwd = call(weight_kernel, [((C, DEEP), BF16)] * 2)(conv_weight[0])
    up, down, x, top = call(
        rows_kernel,
        [((C + 16, 3 * WIDE), BF16)] * 2 + [((C, CELLS), BF16)] * 2,
        [pltpu.SemaphoreType.DMA((2,))],
        bring=False,
    )(x, top, brick_height)
    before = lax.ppermute(up, both, between(1, 0, same))
    after = lax.ppermute(down, both, between(-1, 0, same))
    before, after, fwd, bwd = lax.optimization_barrier((before, after, fwd, bwd))
    to_right, to_left = call(cols_kernel, [((C + 16, 8 * WIDE), BF16)] * 2)(
        x, top, brick_height, before, after
    )
    left = lax.ppermute(to_right, both, between(0, 1, same))
    right = lax.ppermute(to_left, both, between(0, -1, same))
    halos = call(halo_kernel, [((C, 4 * WIDE), BF16)] * 2)(before, after, left, right)
    halos = [lax.ppermute(halo, both, between(0, 0, [(0, SECTIONS - 1)])) for halo in halos]

    core = ((C, 8 * WIDE), BF16)
    slope, mask, x_rows = call(
        forward_kernel,
        [((C, 16 * WIDE), F32), ((TAPS, 16, 16 * WIDE), BF16), ((C, 10 * WIDE), BF16)],
        [((9, C, 18 * WIDE), BF16), ((DEEP, 16 * WIDE), BF16), ((8, 18 * WIDE), F32),
         ((C, 16 * WIDE), F32)],
    )(x, brick_height, before, after, left, right, fwd)
    def scratch(count):
        return [
            ((9, C, (count + 2) * WIDE), BF16), ((DEEP, count * WIDE), BF16),
            ((C, (count + 2) * WIDE), BF16),
            ((C, count * WIDE), BF16),
        ]

    def hand_on(value, source):
        return lax.ppermute(value, both, between(0, 0, [(source, source - 1)]))

    def behind(kernel, count):
        return lambda *refs: kernel(*refs[:count], *refs[count + 1 :])

    def parts_of(kernels, args, pieces, source):
        made = []
        for kernel, given, (low, count, width) in zip(kernels, args, pieces):
            if made:
                kernel, given = behind(kernel, len(given)), given + (made[0][0],)
            lanes = -(-count * width // WIDE) * WIDE
            (result,) = call(kernel, [((C, lanes), BF16)], scratch(count))(*given)
            made.append((result, hand_on(result, source)))
        return [result for result, _ in made], [moved for _, moved in made]

    def middle(given, pieces, low, count, width):
        return functools.partial(middle_kernel, pieces[:given], low, count, width)

    rest = (slope, mask, bwd)
    tops, moved = parts_of(
        [functools.partial(top_kernel, *piece) for piece in TOP_PIECES],
        [(top, halo, left, right) + rest for halo in halos],
        TOP_PIECES,
        3,
    )
    middles, moved_on = parts_of(
        [middle(n + 1, TOP_PIECES, *MIDDLE_PIECES[n]) for n in range(2)],
        [tuple(moved[: n + 1]) + rest for n in range(2)],
        MIDDLE_PIECES,
        2,
    )
    lates, (first, second) = parts_of(
        [middle(n + 1, MIDDLE_PIECES, *LATE_PIECES[n]) for n in range(2)],
        [tuple(moved_on[: n + 1]) + rest for n in range(2)],
        LATE_PIECES,
        1,
    )
    x_rows, result = lax.optimization_barrier((x_rows, lates[1]))
    x_cols, grad, out = call(
        gather_kernel, [((DEEP, CELLS), BF16), core, core], [((9, C, 10 * WIDE), BF16)]
    )(
        top, halos[0], left, right, slope, mask, x_rows,
        *tops, *middles, lates[0], result, *moved, *moved_on,
    )
    terms, incoming = call(
        terms_kernel, [((NEAR * CHUNK, WIDE), BF16), ((C, 10 * WIDE), BF16)]
    )(first, second, slope, grad, x_cols)

    near, far = groups()
    parts = lax.all_to_all(
        terms.reshape(NEAR, CHUNK, WIDE), "space", 0, 0, axis_index_groups=near
    )
    parts, out = lax.optimization_barrier((parts, out))
    (out,) = call(
        last_kernel,
        [((C, CELLS), BF16)],
        [((9, C, 10 * WIDE), BF16), ((DEEP, 8 * WIDE), BF16)],
        leave=(0,),
    )(incoming, slope, mask, bwd, out)
    (copies,) = call(sum_kernel, [((FAR, CHUNK, WIDE), BF16)])(parts)
    parts = lax.all_to_all(copies, "space", 0, 0, axis_index_groups=far)
    parts, out = lax.optimization_barrier((parts, out))
    (copies,) = call(sum_kernel, [((NEAR, CHUNK, WIDE), BF16)])(parts)
    whole = lax.all_to_all(copies, "space", 0, 0, axis_index_groups=near)
    (weight_grad,) = call(scale_kernel, [((DEEP, C), F32)], leave=(0,))(
        whole.reshape(NEAR * CHUNK, WIDE)
    )
    return (out.reshape(1, 1, C, CELLS), weight_grad.reshape(1, TAPS, C, C))


def solution(mesh):
    return jax.shard_map(
        body,
        mesh=mesh,
        in_specs=(
            P("pipe", "space", None, None),
            P("space", None, None),
            P("pipe", None, None, None),
            P("space"),
        ),
        out_specs=(P("pipe", "space", None, None), P("pipe", None, None, None)),
        check_vma=False,
    )
```

```python
import functools

import jax
import jax.numpy as jnp
from jax import lax
from jax.experimental import pallas as pl
from jax.experimental.pallas import tpu as pltpu
from jax.sharding import PartitionSpec as P

C = 96
CELLS = 512
COLS = 8
ROWS = 16
SECTIONS = 4
TAPS = 27
DEEP = TAPS * C
WIDE = 128
CODE = 8
NEAR = 16
FAR = 8
CHUNK = 128
VMEM_BYTES = 32 * 1024 * 1024
F32 = jnp.float32
BF16 = jnp.bfloat16


def call(kernel, outs, scratch=(), leave=(), bring=True):
    shapes = [
        jax.ShapeDtypeStruct(shape, dtype) if n in leave else pltpu.VMEM(shape, dtype)
        for n, (shape, dtype) in enumerate(outs)
    ]

    def run(*args):
        inner = pl.pallas_call(
            kernel,
            out_shape=shapes,
            in_specs=[
                pl.BlockSpec(
                    memory_space=pltpu.SMEM if arg.dtype == jnp.int32
                    else pltpu.VMEM if bring else pl.ANY
                )
                for arg in args
            ],
            out_specs=[pl.BlockSpec(memory_space=pltpu.VMEM)] * len(shapes),
            scratch_shapes=[
                pltpu.VMEM(*item) if isinstance(item, tuple) else item for item in scratch
            ],
            compiler_params=pltpu.CompilerParams(vmem_limit_bytes=VMEM_BYTES),
        )
        return inner(
            *[
                arg if arg.dtype == jnp.int32
                else pltpu.with_memory_space_constraint(arg, pltpu.VMEM if bring else pltpu.HBM)
                for arg in args
            ]
        )

    return run


def lane(row, count=1):
    start = row * WIDE
    if not isinstance(start, int):
        start = pl.multiple_of(start, WIDE)
    return pl.ds(start, count * WIDE)


def turn(value, by):
    by = by % value.shape[1]
    return pltpu.roll(value, by, 1) if by else value


def shifted_rows(base_ref, row, tile, low=None, high=None):
    level = lax.broadcasted_iota(jnp.int32, (C, WIDE), 1) % 8
    for oy, source in ((-1, low), (0, None), (1, high)):
        source = tile if source is None else source
        for oz in (-1, 0, 1):
            if oz == 0:
                moved = turn(source, -8 * oy)
            elif oz > 0:
                moved = jnp.where(level < 7, turn(source, -8 * oy - 1), turn(source, -8 * oy + 7))
            else:
                moved = jnp.where(level > 0, turn(source, -8 * oy + 1), turn(source, -8 * oy - 7))
            base_ref[3 * (oy + 1) + oz + 1, :, lane(row)] = moved


def make_cols(cols_ref, base_ref, mask_ref, base_row, mask_row, at=0):
    for ox in (-1, 0, 1):
        for j in range(9):
            tap = 9 * (ox + 1) + j
            tile = base_ref[j, :, lane(base_row + ox, 2)].reshape(C // 16, 16, 2 * WIDE)
            kept = tile * mask_ref[tap, :, lane(mask_row, 2)][None]
            cols_ref[C * tap : C * tap + C, lane(at, 2)] = kept.reshape(C, 2 * WIDE)


def product(weight, cols):
    return lax.dot_general(
        weight, cols, (((1,), (0,)), ((), ())), preferred_element_type=F32
    )


def weight_kernel(w_ref, fwd_ref, bwd_ref):
    for q in range(TAPS):
        fwd_ref[:, C * q : C * q + C] = w_ref[q].T
        bwd_ref[:, C * q : C * q + C] = w_ref[TAPS - 1 - q]


OUTER = (1, 2, 3, 4, 13, 14, 15, 16)


def code_of(height_ref, shape):
    return jnp.full(shape, (height_ref[0] + CODE).astype(F32), F32)


def rows_kernel(x_hbm, top_hbm, height_ref, up_ref, down_ref, x_ref, top_ref, sems):
    x_copy = pltpu.make_async_copy(x_hbm, x_ref, sems.at[0])
    top_copy = pltpu.make_async_copy(top_hbm, top_ref, sems.at[1])
    x_copy.start()
    top_copy.start()
    x_copy.wait()
    top_copy.wait()
    lowest = lax.axis_index("pipe") == 0
    code = code_of(height_ref, (16, 3 * WIDE)).astype(BF16)
    spare = jnp.zeros((C, 64), BF16)
    up_ref[C:, :] = code
    down_ref[C:, :] = code
    up_ref[:C, :WIDE] = x_ref[:, 384:512]
    down_ref[:C, :WIDE] = x_ref[:, 0:128]

    @pl.when(lowest)
    def _():
        up_ref[:C, WIDE:] = top_ref[:, 256:512]
        down_ref[:C, WIDE:] = top_ref[:, 0:256]

    @pl.when(jnp.logical_not(lowest))
    def _():
        up_ref[:C, WIDE:] = jnp.concatenate([x_ref[:, 192:384], spare], 1)
        down_ref[:C, WIDE:] = jnp.concatenate([x_ref[:, 128:320], spare], 1)


def x_layer(x_ref, before_ref, after_ref, row):
    if row < 5:
        at = 64 * (row - 3) if row >= 3 else WIDE + 64 * row
        return before_ref[:C, at : at + 64]
    if row < 13:
        return x_ref[:, 64 * (row - 5) : 64 * (row - 5) + 64]
    at = 64 * (row - 13) if row < 15 else WIDE + 64 * (row - 15)
    return after_ref[:C, at : at + 64]


def top_layer(before_ref, after_ref, row):
    if row < 5:
        return before_ref[:C, WIDE + 64 * (row - 1) : WIDE + 64 * row]
    return after_ref[:C, WIDE + 64 * (row - 13) : WIDE + 64 * (row - 12)]


def join(parts):
    return jnp.concatenate(parts, 1)


def cols_kernel(x_ref, top_ref, height_ref, before_ref, after_ref, right_ref, left_ref):
    lowest = lax.axis_index("pipe") == 0
    codes = join(
        [before_ref[C:, :WIDE], code_of(height_ref, (16, WIDE)).astype(BF16), after_ref[C:, :WIDE]]
    )
    for out, start, fifth in ((right_ref, 32, 24), (left_ref, 0, 32)):

        def piece(layer, start=start):
            return layer[:, start : start + 32]

        out[C:, : 3 * WIDE] = codes
        out[C:, 3 * WIDE :] = jnp.zeros((16, 5 * WIDE), BF16)
        for four in range(3):
            rows = range(3 + 4 * four, 7 + 4 * four)
            out[:C, lane(four)] = join(
                [piece(x_layer(x_ref, before_ref, after_ref, row)) for row in rows]
            )

        @pl.when(lowest)
        def _(out=out, piece=piece):
            tops = [piece(top_layer(before_ref, after_ref, row)) for row in OUTER]
            out[:C, lane(3)] = join(tops[:4])
            out[:C, lane(4)] = join(tops[4:])
            out[:C, lane(5, 3)] = jnp.zeros((C, 3 * WIDE), BF16)

        @pl.when(jnp.logical_not(lowest))
        def _(out=out, piece=piece, fifth=fifth):
            outer = [
                piece(x_layer(x_ref, before_ref, after_ref, row)) for row in (0, 1, 2, 15, 16, 17)
            ]
            more = [
                x_layer(x_ref, before_ref, after_ref, row)[:, fifth : fifth + 8]
                for row in range(18)
            ]
            tops = [piece(top_ref[:, 64 * n : 64 * n + 64]) for n in range(8)]
            out[:C, lane(3)] = join(outer[:4])
            out[:C, lane(4)] = join(outer[4:] + more[:8])
            out[:C, lane(5)] = join(more[8:] + [jnp.zeros((C, 48), BF16)])
            out[:C, lane(6)] = join(tops[:4])
            out[:C, lane(7)] = join(tops[4:])


def x_side(side_ref, row):
    if 3 <= row < 15:
        at = 32 * (row - 3)
    else:
        at = 3 * WIDE + 32 * (row if row < 3 else row - 12)
    return side_ref[:C, at : at + 32]


def halo_kernel(before_ref, after_ref, left_ref, right_ref, first_ref, second_ref):
    @pl.when(lax.axis_index("pipe") == 0)
    def _():
        for n, row in enumerate(OUTER):
            at = 3 * WIDE + 32 * n
            middle = top_layer(before_ref, after_ref, row)
            sides = left_ref[:C, at : at + 32], right_ref[:C, at : at + 32]
            halo_ref = first_ref if n < 4 else second_ref
            halo_ref[:, lane(n % 4)] = join([sides[0], middle, sides[1]])


def forward_kernel(
    x_ref, height_ref, before_ref, after_ref, left_ref, right_ref, fwd_ref,
    slope_ref, mask_ref, rows_ref,
    base_ref, cols_ref, code_ref, pre_ref,
):
    where = lax.broadcasted_iota(jnp.int32, (8, WIDE), 1)
    middle = (
        before_ref[C : C + 8, :WIDE].astype(F32),
        code_of(height_ref, (8, WIDE)),
        after_ref[C : C + 8, :WIDE].astype(F32),
    )
    codes = []
    for n in range(3):
        left = left_ref[C : C + 8, lane(n)].astype(F32)
        right = right_ref[C : C + 8, lane(n)].astype(F32)
        codes.append(jnp.where(where < 32, left, jnp.where(where < 96, middle[n], right)))
    for row in range(18):
        code_ref[:, lane(row)] = codes[0 if row < 5 else 1 if row < 13 else 2]
    for row in range(18):
        tile = join(
            [
                x_side(left_ref, row),
                x_layer(x_ref, before_ref, after_ref, row),
                x_side(right_ref, row),
            ]
        )
        if 4 <= row < 14:
            rows_ref[:, lane(row - 4)] = tile
        at = 4 * WIDE + 64 + 8 * row
        low = join([tile[:, :120], left_ref[:C, at : at + 8]])
        high = join([right_ref[:C, at : at + 8], tile[:, 8:]])
        shifted_rows(base_ref, row, tile, low, high)

    level = lax.broadcasted_iota(jnp.int32, (8, WIDE), 1) % 8
    rise_of = {
        -1: jnp.where(level == 0, -1.0, 0.0),
        0: jnp.zeros((8, WIDE), F32),
        1: jnp.where(level == 7, 1.0, 0.0),
    }

    for rows in ((0, 1, 2), (3,), (4,), (5, 6, 7, 8, 9, 10), (11,), (12,), (13, 14, 15)):
        here = code_ref[:, lane(rows[0] + 1)]
        for ox in (-1, 0, 1):
            near = code_ref[:, lane(rows[0] + 1 + ox)]
            for oy in (-1, 0, 1):
                if oy < 0:
                    source = jnp.where(where >= 120, near[:, 0:1], near)
                elif oy > 0:
                    source = jnp.where(where < 8, near[:, 127:128], near)
                else:
                    source = near
                rise = turn(source, -8 * oy) - here
                for oz in (-1, 0, 1):
                    keep = jnp.where(rise == rise_of[oz], 1.0, 0.0)
                    keep = jnp.concatenate([keep, keep], 0).astype(BF16)
                    tap = 9 * (ox + 1) + 3 * (oy + 1) + oz + 1
                    for row in rows:
                        mask_ref[tap, :, lane(row)] = keep

    for pair in range(8):
        make_cols(cols_ref, base_ref, mask_ref, 2 * pair + 1, 2 * pair, 2 * pair)
    pre_ref[...] = product(fwd_ref[...], cols_ref[...])
    for row in range(16):
        pre = pre_ref[:, lane(row)]
        sigma = 1.0 / (1.0 + jnp.exp(-pre))
        slope_ref[:, lane(row)] = sigma * (1.0 + pre * (1.0 - sigma))


def top_row(top_ref, halo_ref, left_ref, right_ref, row):
    if 5 <= row < 13:
        at, side = 64 * (row - 5), 6 * WIDE + 32 * (row - 5)
        tile = join(
            [
                left_ref[:C, side : side + 32],
                top_ref[:, at : at + 64],
                right_ref[:C, side : side + 32],
            ]
        )
    else:
        tile = halo_ref[:, lane((row - 1) % 12)]
    return jnp.where(lax.axis_index("pipe") == SECTIONS - 1, tile, jnp.zeros_like(tile))


def step_rows(incoming_ref, slope_ref, mask_ref, bwd_ref, base_ref, cols_ref, store, count, first):
    for row in range(count):
        grad = (
            incoming_ref[:, lane(row)].astype(F32) * slope_ref[:, lane(row + first - 1)]
        ).astype(BF16)
        shifted_rows(base_ref, row, grad)

    for pair in range((count - 2) // 2):
        make_cols(cols_ref, base_ref, mask_ref, 2 * pair + 1, 2 * pair + first, 2 * pair)
    rows = lane(1, count - 2)
    total = incoming_ref[:, rows].astype(F32) + product(bwd_ref[...], cols_ref[...])
    for pair in range((count - 2) // 2):
        store(pair, total[:, 2 * pair * WIDE : 2 * (pair + 1) * WIDE].astype(BF16))


def spread(packed_ref, width, row):
    spare = jnp.zeros((C, (WIDE - width) // 2), BF16)
    return join([spare, packed_ref[:, width * row : width * row + width], spare])


TOP_PIECES = (2, 8, WIDE), (10, 6, WIDE)
MIDDLE_PIECES = (3, 6, 96), (9, 6, 96)
LATE_PIECES = (4, 4, 80), (8, 6, 80)


def pieces_row(pieces, row):
    for ref, first, count, width in pieces:
        if first <= row < first + count:
            if width == WIDE:
                return ref[:, lane(row - first)]
            return spread(ref, width, row - first)


def step_part(row_of, low, count, width, result_ref, slope_ref, mask_ref, bwd_ref, scratch):
    base_ref, cols_ref, rows_ref, full_ref = scratch
    for n in range(count + 2):
        rows_ref[:, lane(n)] = row_of(low - 1 + n)

    def store(pair, value):
        full_ref[:, lane(2 * pair, 2)] = value

    step_rows(
        rows_ref, slope_ref, mask_ref, bwd_ref, base_ref, cols_ref, store, count + 2, low - 1
    )
    skip = (WIDE - width) // 2
    packed = [full_ref[:, lane(n)][:, skip : skip + width] for n in range(count)]
    spare = result_ref.shape[1] - width * count
    result_ref[...] = join(packed + [jnp.zeros((C, spare), BF16)] if spare else packed)


def top_kernel(
    low, count, top_ref, halo_ref, left_ref, right_ref, slope_ref, mask_ref, bwd_ref,
    result_ref, *scratch,
):
    def row_of(row):
        return top_row(top_ref, halo_ref, left_ref, right_ref, row)

    step_part(row_of, low, count, WIDE, result_ref, slope_ref, mask_ref, bwd_ref, scratch)


def middle_kernel(pieces, low, count, width, *refs):
    given, refs = refs[: len(pieces)], refs[len(pieces) :]
    slope_ref, mask_ref, bwd_ref, result_ref, *scratch = refs

    def row_of(row):
        return pieces_row([(ref,) + piece for ref, piece in zip(given, pieces)], row)

    step_part(row_of, low, count, width, result_ref, slope_ref, mask_ref, bwd_ref, scratch)


def halves(first, second):
    where = lax.broadcasted_iota(jnp.int32, first.shape, 1)
    return jnp.where(where < 64, turn(first, -32), turn(second, 32))


def gather_kernel(
    top_ref, halo_ref, left_ref, right_ref, slope_ref, mask_ref, x_ref, *refs
):
    kinds = TOP_PIECES + MIDDLE_PIECES + LATE_PIECES
    pieces = [(ref,) + piece for ref, piece in zip(refs[:6], kinds)]
    incoming = [(ref,) + piece for ref, piece in zip(refs[6:10], TOP_PIECES + MIDDLE_PIECES)]
    all_ref, grad_ref, out_ref, base_ref = refs[10:]
    for n in range(8):
        row = n + 5
        scale = slope_ref[:, lane(n + 4)]
        tiles = (
            top_row(top_ref, halo_ref, left_ref, right_ref, row),
            pieces_row(incoming[:2], row),
            pieces_row(incoming[2:], row),
        )
        grads = [(tile.astype(F32) * scale).astype(BF16) for tile in tiles]
        grad_ref[:, lane(n)] = grads[0] + grads[1] + grads[2]
        outs = [pieces_row(pieces[at : at + 2], row) for at in (0, 2, 4)]
        out_ref[:, lane(n)] = outs[0] + outs[1] + outs[2]
    for row in range(10):
        shifted_rows(base_ref, row, x_ref[:, lane(row)])

    def one(pair, carry):
        for tap in range(TAPS):
            ox, j = tap // 9 - 1, tap % 9
            tiles = []
            for n in range(2):
                tile = base_ref[j, :, lane(2 * pair + 1 + n + ox)].reshape(C // 16, 16, WIDE)
                kept = tile * mask_ref[tap, :, lane(2 * pair + 4 + n)][None]
                tiles.append(kept.reshape(C, WIDE))
            all_ref[C * tap : C * tap + C, lane(pair)] = halves(*tiles)
        return carry

    lax.fori_loop(0, 4, one, 0)


def terms_kernel(
    first_ref, second_ref, slope_ref, grad_in, all_ref, terms_ref, incoming_ref
):
    for row in range(10):
        incoming_ref[:, lane(row)] = pieces_row(
            ((first_ref,) + LATE_PIECES[0], (second_ref,) + LATE_PIECES[1]), row + 4
        )
    grads = []
    for row in range(8):
        grad = incoming_ref[:, lane(row + 1)].astype(F32) * slope_ref[:, lane(row + 4)]
        grads.append(grad_in[:, lane(row)] + grad.astype(BF16))
    grads = join([halves(grads[2 * pair], grads[2 * pair + 1]) for pair in range(4)])
    whole = lax.dot_general(
        all_ref[...], grads, (((1,), (1,)), ((), ())), preferred_element_type=F32
    ).astype(BF16)
    for four in range(7):
        parts = []
        for tap in range(4 * four, 4 * four + 4):
            if tap < TAPS:
                part = whole[C * tap : C * tap + C, :]
            else:
                part = jnp.zeros((C, C), BF16)
            parts.append(part)
        first, second, third, fourth = parts
        at = 3 * C * four
        terms_ref[at : at + C, :] = jnp.concatenate([first, second[:, :32]], 1)
        terms_ref[at + C : at + 2 * C, :] = jnp.concatenate([second[:, 32:], third[:, :64]], 1)
        terms_ref[at + 2 * C : at + 3 * C, :] = jnp.concatenate([third[:, 64:], fourth], 1)
    terms_ref[21 * C :, :] = jnp.zeros((NEAR * CHUNK - 21 * C, WIDE), BF16)


def last_kernel(
    incoming_ref, slope_ref, mask_ref, bwd_ref, out_in, out_ref, base_ref, cols_ref
):
    def store(pair, value):
        total = out_in[:, lane(2 * pair, 2)] + value
        out_ref[:, lane(pair)] = halves(total[:, :WIDE], total[:, WIDE:])

    step_rows(incoming_ref, slope_ref, mask_ref, bwd_ref, base_ref, cols_ref, store, 10, 4)


def sum_kernel(parts_ref, out_ref):
    total = parts_ref[0].astype(F32)
    for n in range(1, parts_ref.shape[0]):
        total = total + parts_ref[n].astype(F32)
    total = total.astype(BF16)
    for n in range(out_ref.shape[0]):
        out_ref[n] = total


def scale_kernel(whole_ref, out_ref):
    whole = whole_ref[...].astype(F32)
    scale = lax.rsqrt(jnp.sum(whole * whole) / (DEEP * C) + 1e-06)
    for four in range(7):
        at = 3 * C * four
        first, second, third = (whole_ref[at + n * C : at + n * C + C, :] for n in range(3))
        parts = (
            first[:, :96],
            jnp.concatenate([first[:, 96:], second[:, :64]], 1),
            jnp.concatenate([second[:, 64:], third[:, :32]], 1),
            third[:, 32:],
        )
        for n, tap in enumerate(range(4 * four, min(4 * four + 4, TAPS))):
            out_ref[C * tap : C * tap + C, :] = parts[n].astype(F32) * scale


def groups():
    def device(y, high, low, core):
        return y * 32 + (2 * high + low) * 2 + core

    kinds = [(y, low, core) for y in range(4) for low in range(2) for core in range(2)]
    near = [[device(y, high, low, core) for y, low, core in kinds] for high in range(FAR)]
    far = [[device(y, high, low, core) for high in range(FAR)] for y, low, core in kinds]
    return near, far


def body(section_input, top_grad, conv_weight, brick_height):
    both = ("space", "pipe")

    def between(by_row, by_col, sections):
        pairs = []
        for x in range(ROWS):
            for y in range(COLS):
                if 0 <= x + by_row < ROWS and 0 <= y + by_col < COLS:
                    source = x * COLS + y
                    target = (x + by_row) * COLS + y + by_col
                    for a, b in sections:
                        pairs.append((source * SECTIONS + a, target * SECTIONS + b))
        return pairs

    same = [(s, s) for s in range(SECTIONS)]
    x = section_input.reshape(C, CELLS)
    top = top_grad.reshape(C, CELLS)
    fwd, bwd = call(weight_kernel, [((C, DEEP), BF16)] * 2)(conv_weight[0])
    up, down, x, top = call(
        rows_kernel,
        [((C + 16, 3 * WIDE), BF16)] * 2 + [((C, CELLS), BF16)] * 2,
        [pltpu.SemaphoreType.DMA((2,))],
        bring=False,
    )(x, top, brick_height)
    before = lax.ppermute(up, both, between(1, 0, same))
    after = lax.ppermute(down, both, between(-1, 0, same))
    before, after, fwd, bwd = lax.optimization_barrier((before, after, fwd, bwd))
    to_right, to_left = call(cols_kernel, [((C + 16, 8 * WIDE), BF16)] * 2)(
        x, top, brick_height, before, after
    )
    left = lax.ppermute(to_right, both, between(0, 1, same))
    right = lax.ppermute(to_left, both, between(0, -1, same))
    halos = call(halo_kernel, [((C, 4 * WIDE), BF16)] * 2)(before, after, left, right)
    halos = [lax.ppermute(halo, both, between(0, 0, [(0, SECTIONS - 1)])) for halo in halos]

    core = ((C, 8 * WIDE), BF16)
    slope, mask, x_rows = call(
        forward_kernel,
        [((C, 16 * WIDE), F32), ((TAPS, 16, 16 * WIDE), BF16), ((C, 10 * WIDE), BF16)],
        [((9, C, 18 * WIDE), BF16), ((DEEP, 16 * WIDE), BF16), ((8, 18 * WIDE), F32),
         ((C, 16 * WIDE), F32)],
    )(x, brick_height, before, after, left, right, fwd)
    def scratch(count):
        return [
            ((9, C, (count + 2) * WIDE), BF16), ((DEEP, count * WIDE), BF16),
            ((C, (count + 2) * WIDE), BF16),
            ((C, count * WIDE), BF16),
        ]

    def hand_on(value, source):
        return lax.ppermute(value, both, between(0, 0, [(source, source - 1)]))

    def behind(kernel, count):
        return lambda *refs: kernel(*refs[:count], *refs[count + 1 :])

    def parts_of(kernels, args, pieces, source):
        made = []
        for kernel, given, (low, count, width) in zip(kernels, args, pieces):
            if made:
                kernel, given = behind(kernel, len(given)), given + (made[0][0],)
            lanes = -(-count * width // WIDE) * WIDE
            (result,) = call(kernel, [((C, lanes), BF16)], scratch(count))(*given)
            made.append((result, hand_on(result, source)))
        return [result for result, _ in made], [moved for _, moved in made]

    def middle(given, pieces, low, count, width):
        return functools.partial(middle_kernel, pieces[:given], low, count, width)

    rest = (slope, mask, bwd)
    tops, moved = parts_of(
        [functools.partial(top_kernel, low, count) for low, count, _ in TOP_PIECES],
        [(top, halo, left, right) + rest for halo in halos],
        TOP_PIECES,
        3,
    )
    middles, moved_on = parts_of(
        [middle(n + 1, TOP_PIECES, *MIDDLE_PIECES[n]) for n in range(2)],
        [tuple(moved[: n + 1]) + rest for n in range(2)],
        MIDDLE_PIECES,
        2,
    )
    lates, (first, second) = parts_of(
        [middle(n + 1, MIDDLE_PIECES, *LATE_PIECES[n]) for n in range(2)],
        [tuple(moved_on[: n + 1]) + rest for n in range(2)],
        LATE_PIECES,
        1,
    )
    x_rows, result = lax.optimization_barrier((x_rows, lates[1]))
    x_cols, grad, out = call(
        gather_kernel, [((DEEP, CELLS), BF16), core, core], [((9, C, 10 * WIDE), BF16)]
    )(
        top, halos[0], left, right, slope, mask, x_rows,
        *tops, *middles, lates[0], result, *moved, *moved_on,
    )
    terms, incoming = call(
        terms_kernel, [((NEAR * CHUNK, WIDE), BF16), ((C, 10 * WIDE), BF16)]
    )(first, second, slope, grad, x_cols)

    near, far = groups()
    parts = lax.all_to_all(
        terms.reshape(NEAR, CHUNK, WIDE), "space", 0, 0, axis_index_groups=near
    )
    parts, out = lax.optimization_barrier((parts, out))
    (out,) = call(
        last_kernel,
        [((C, CELLS), BF16)],
        [((9, C, 10 * WIDE), BF16), ((DEEP, 8 * WIDE), BF16)],
        leave=(0,),
    )(incoming, slope, mask, bwd, out)
    (copies,) = call(sum_kernel, [((FAR, CHUNK, WIDE), BF16)])(parts)
    parts = lax.all_to_all(copies, "space", 0, 0, axis_index_groups=far)
    parts, out = lax.optimization_barrier((parts, out))
    (copies,) = call(sum_kernel, [((NEAR, CHUNK, WIDE), BF16)])(parts)
    whole = lax.all_to_all(copies, "space", 0, 0, axis_index_groups=near)
    (weight_grad,) = call(scale_kernel, [((DEEP, C), F32)], leave=(0,))(
        whole.reshape(NEAR * CHUNK, WIDE)
    )
    return (out.reshape(1, 1, C, CELLS), weight_grad.reshape(1, TAPS, C, C))


def solution(mesh):
    return jax.shard_map(
        body,
        mesh=mesh,
        in_specs=(
            P("pipe", "space", None, None),
            P("space", None, None),
            P("pipe", None, None, None),
            P("space"),
        ),
        out_specs=(P("pipe", "space", None, None), P("pipe", None, None, None)),
        check_vma=False,
    )
```
